128 devices in a mesh: dp: 32 (over y_lo, x, z), tensor: 4 (over y_hi, core).
Axes of the slice: x: 4, y: 4 (y_hi: 2, y_lo: 2; y = y_hi * 2 + y_lo), z: 4, core: 2. Of those that a mesh axis runs over, the one named last changes fastest.
Arguments:
- tokens: bfloat16 [32768, 1024], P(('dp', 'tensor')), may hold values from -6 to 6
- segment_ids: int32 [32768], P('dp'), may hold values from 0 to 510, as said below
- norm_gain: bfloat16 [2, 1024], P(None, ('dp', 'tensor')), may hold values from 0.25 to 1.75
- norm_shift: bfloat16 [2, 1024], P(None, ('dp', 'tensor')), may hold values from -3 to 3
- qkv_weight: bfloat16 [2, 3, 1024, 1024], P(None, None, 'dp', 'tensor'), may hold values from -0.1875 to 0.1875
- proj_weight: bfloat16 [2, 1024, 1024], P(None, ('tensor', 'dp')), may hold values from -1.5 to 1.5
- up_weight: bfloat16 [2, 1024, 4096], P(None, 'dp', 'tensor'), may hold values from -0.1875 to 0.1875
- hidden_bias: bfloat16 [2, 4096], P(None, ('tensor', 'dp')), may hold values from -3 to 3
- down_weight: bfloat16 [2, 4096, 1024], P(None, ('tensor', 'dp')), may hold values from -0.09375 to 0.09375
- final_bias: bfloat16 [2, 1024], P(None, ('dp', 'tensor')), may hold values from -3 to 3
- cotangent: bfloat16 [32768, 1024], P(('dp', 'tensor')), may hold values from -6 to 6
Outputs:
- mixed: bfloat16 [32768, 1024], P(('dp', 'tensor'))
- token_grad: float32 [32768, 1024], P(('dp', 'tensor'))
- gain_grad: float32 [2, 1024], P(None, ('dp', 'tensor'))
- shift_grad: float32 [2, 1024], P(None, ('dp', 'tensor'))
- qkv_grad: float32 [2, 3, 1024, 1024], P(None, None, 'dp', 'tensor')
- proj_grad: float32 [2, 1024, 1024], P(None, ('tensor', 'dp'))
- up_grad: float32 [2, 1024, 4096], P(None, 'dp', 'tensor')
- hidden_grad: float32 [2, 4096], P(None, ('tensor', 'dp'))
- down_grad: float32 [2, 4096, 1024], P(None, ('tensor', 'dp'))
- final_grad: float32 [2, 1024], P(None, ('dp', 'tensor'))
The draws below stay inside these ranges and needn't reach their ends.
Inputs may be any that keep to these rules, and one draw needn't show every extreme that they name: `segment_ids`: within each group of 1024 consecutive tokens the ids start at 0 and never fall; a sequence holds 1 to 1024 tokens; some group reaches the largest id.
All inputs are finite; a program needn't handle non-finite values.
Results may differ from the reference program's by a relative error of at most 0.028.
Values may be sent and summed in bfloat16 or wider, within the bound.
A program may use at most 192 MiB of HBM per device.

```python
import math
import jax
import jax.numpy as jnp
from jax import lax

D = 1024
HEADS = 16
HEAD_DIM = 64
ROT = 32
FF = 4096
LAYERS = 2
TOK_DEV = 256
HH = 1024
GROUP = 1024
TOKENS = 32768
N_DP = 32
N_TENSOR = 4


def draw_segment_ids(key, part):
    key = jax.random.fold_in(key, 7)
    group = TOK_DEV * N_TENSOR
    keys = jax.random.split(key, 5)
    chosen = jax.random.randint(keys[4], (), 0, N_DP)
    rows = jnp.arange(N_DP, dtype=jnp.int32)[:, None]
    picked = rows == chosen
    begin = jax.random.randint(keys[0], (N_DP, 1), 0, TOK_DEV)
    finish = jax.random.randint(keys[1], (N_DP, 1), (N_TENSOR - 1) * TOK_DEV + 1, group + 1)
    begin = jnp.where(picked, TOK_DEV - 1, begin)
    finish = jnp.where(picked, (N_TENSOR - 1) * TOK_DEV + 1, finish)
    level = jax.random.randint(keys[2], (N_DP, 1), 0, 4)
    flips = jax.random.randint(keys[3], (N_DP, group), 0, 256)
    index = jnp.arange(group, dtype=jnp.int32)[None, :]
    inside = (index > begin) & (index < finish)
    cuts = ((flips < level * 16) | picked) & jnp.logical_not(inside)
    cuts = cuts | (index == 0) | (index == begin) | (index == finish)
    ids = jnp.cumsum(cuts.astype(jnp.int32), axis=1) - 1
    return ids.reshape(N_DP * group).astype(jnp.int32)


def shard_levels(key, dims, shards, least, top_value):
    def one(axis_at, blocks):
        draws = jax.random.uniform(jax.random.fold_in(jax.random.fold_in(key, 6), axis_at), (blocks,), jnp.float32, least / len(shards), top_value / len(shards))
        return jnp.repeat(jnp.exp(draws), dims[axis_at] // blocks).reshape((-1,) + (1,) * (len(dims) - axis_at - 1))

    factor_of = one(*shards[0])
    for cut in shards[1:]:
        factor_of = factor_of * one(*cut)
    return factor_of


def centred(rng, shape, spread, reach, shards=(), held_as=jnp.bfloat16):
    values = jax.random.normal(rng, shape, jnp.float32) * spread
    if len(shards) > 0:
        values = shard_levels(rng, shape, shards, -0.22, 0.18) * values
    return jnp.clip(values, min=-reach, max=reach).astype(held_as)


def setup_inputs(seed: int = 0) -> dict:
    arg_keys = jax.random.split(jax.random.key(seed), 12)
    return {
        "tokens": centred(arg_keys[0], (TOKENS, D), 1.0, 6.0, ((0, 128),)),
        "segment_ids": draw_segment_ids(jax.random.fold_in(arg_keys[11], 71), 0),
        "norm_gain": jnp.clip(1.0 + 0.15 * jax.random.normal(arg_keys[2], (LAYERS, D), jnp.float32), 0.25, 1.75).astype(jnp.bfloat16),
        "norm_shift": centred(arg_keys[3], (LAYERS, D), 0.5, 3.0, ((1, 128),)),
        "qkv_weight": centred(arg_keys[4], (LAYERS, 3, D, HH), D ** -0.5, 0.1875, ((2, 32), (3, 4))),
        "proj_weight": centred(arg_keys[5], (LAYERS, HH, D), (HEADS * HEAD_DIM // 64) ** -0.5, 1.5, ((1, 128),)),
        "up_weight": centred(arg_keys[6], (LAYERS, D, FF), D ** -0.5, 0.1875, ((1, 32), (2, 4))),
        "hidden_bias": centred(arg_keys[7], (LAYERS, FF), 0.5, 3.0, ((1, 128),)),
        "down_weight": centred(arg_keys[8], (LAYERS, FF, D), FF ** -0.5, 0.09375, ((1, 128),)),
        "final_bias": centred(arg_keys[9], (LAYERS, D), 0.5, 3.0, ((1, 128),)),
        "cotangent": centred(arg_keys[10], (TOKENS, D), 1.0, 6.0, ((0, 128),)),
    }


@jax.custom_vjp
def low(v):
    return lax.optimization_barrier(v.astype(jnp.bfloat16)).astype(jnp.float32)

@jax.custom_vjp
def low_back(v):
    return v

def low_keep(v):
    return (low(v), None)

def low_pass(kept, grad):
    return (grad,)

def back_keep(v):
    return (v, None)

def back_low(kept, grad):
    return (low(grad),)
low.defvjp(low_keep, low_pass)
low_back.defvjp(back_keep, back_low)
epsilon = 1e-05
highest = lax.Precision.HIGHEST

def product(left, right):
    return jnp.dot(left, right, precision=highest, preferred_element_type=jnp.float32)

def seq_positions(segments):
    count = segments.shape[0]
    index = jnp.arange(count, dtype=jnp.int32)
    first = jnp.concatenate([jnp.ones((1,), dtype=bool), segments[1:] != segments[:-1]])
    begin = lax.cummax(jnp.where(first, index, 0).astype(jnp.int32), axis=0)
    return index - begin

def rotary_tables(positions):
    half = ROT // 2
    freq = jnp.exp(jnp.arange(half, dtype=jnp.float32) * (-2.0 * math.log(10000.0) / ROT))
    angle = positions.astype(jnp.float32)[:, None] * freq[None, :]
    return (jnp.cos(angle)[:, None, :], jnp.sin(angle)[:, None, :])

def rotate(heads, cosine, sine):
    half = ROT // 2
    first = heads[..., :half]
    second = heads[..., half:ROT]
    return jnp.concatenate([first * cosine - second * sine, second * cosine + first * sine, heads[..., ROT:]], axis=-1)

def layer_forward(state, gain, shift, qkv_full, proj_full, up_full, hidden_full, down_full, bias_final, cosine, sine, allowed):
    count = state.shape[0]
    center = state - lax.optimization_barrier(jnp.mean(state, axis=-1, keepdims=True))
    inverse = lax.rsqrt(lax.optimization_barrier(jnp.mean(center * center, axis=-1, keepdims=True)) + epsilon)
    normed = low(center * inverse * gain + shift)
    joined = low_back(jnp.einsum('td,cde->cte', normed, qkv_full, precision=highest))
    joined = joined.reshape(3, count, HEADS, HEAD_DIM)
    query = low(rotate(joined[0], cosine, sine))
    keys = low(rotate(joined[1], cosine, sine))
    values = low(joined[2])
    scores = low_back(jnp.einsum('qhe,khe->hqk', query, keys, precision=highest) * HEAD_DIM ** (-0.5))
    scores = jnp.where(allowed[None], scores, -1e+30)
    probs = low(jax.nn.softmax(scores, axis=-1))
    attended = low(low_back(jnp.einsum('hqk,khe->qhe', probs, values, precision=highest)))
    attended = attended.reshape(count, HEADS * HEAD_DIM)
    up = low_back(product(normed, up_full) + hidden_full)
    active = low(jax.nn.gelu(up, approximate=True))
    branch = low_back(product(attended, proj_full) + product(active, down_full))
    return state + branch + bias_final

def reference(tokens, segment_ids, norm_gain, norm_shift, qkv_weight, proj_weight, up_weight, hidden_bias, down_weight, final_bias, cotangent):
    params = tuple((item.astype(jnp.float32) for item in (norm_gain, norm_shift, qkv_weight, proj_weight, up_weight, hidden_bias, down_weight, final_bias)))
    inputs = tokens.astype(jnp.float32).reshape(N_DP, GROUP, D)
    segments = segment_ids.reshape(N_DP, GROUP)

    def group_forward(weights, block, ids):
        positions = seq_positions(ids)
        cosine, sine = rotary_tables(positions)
        index = jnp.arange(ids.shape[0], dtype=jnp.int32)
        allowed = (ids[:, None] == ids[None, :]) & (index[:, None] >= index[None, :])
        for layer in range(LAYERS):
            block = layer_forward(block, *[item[layer] for item in weights], cosine, sine, allowed)
        return block

    def whole(values_in, weights):

        def step(carry, item):
            return (carry, group_forward(weights, item[0], item[1]))
        _, outputs = lax.scan(jax.checkpoint(step), None, (values_in, segments))
        return outputs
    outputs, pullback = jax.vjp(whole, inputs, params)
    grad_in, grads = pullback(cotangent.astype(jnp.float32).reshape(N_DP, GROUP, D))
    mixed = outputs.reshape(N_DP * GROUP, D).astype(jnp.bfloat16)
    return (mixed, grad_in.reshape(N_DP * GROUP, D), grads[0], grads[1], grads[2], grads[3], grads[4], grads[5], grads[6], grads[7])
```

```python
import functools
import math

import jax
import jax.numpy as jnp
from jax import lax
from jax.experimental import pallas as pl
from jax.experimental.pallas import tpu as pltpu
from jax.sharding import PartitionSpec as P

HEAD_DIM = 64
ROT = 32
MESH = pl.DeviceIdType.MESH
ALL = slice(None)


epsilon = 1e-05
block_rows = 512


class Place:
    def __init__(self):
        dp = lax.axis_index("dp")
        self.t = lax.axis_index("tensor")
        self.dp = dp
        self.at = {"y": dp // 16, "x": lax.rem(dp // 4, 4), "z": lax.rem(dp, 4)}

    def plus(self, axis, step):
        return lax.rem(self.at[axis] + (step % 4), 4)

    def peer(self, axis, step):
        if axis == "core":
            return (self.dp, self.t ^ 1)
        if axis == "far":
            return (self.dp, self.t ^ 2)
        if axis == "both":
            return (self.dp, self.t ^ 3)
        c = dict(self.at)
        c[axis] = 1 - c["y"] if axis == "y" else self.plus(axis, step)
        return ((c["y"] * 4 + c["x"]) * 4 + c["z"], self.t)


def meet(peers):
    barrier = pltpu.get_barrier_semaphore()
    for peer in peers:
        pl.semaphore_signal(barrier, inc=1, device_id=peer, device_id_type=MESH)
    pl.semaphore_wait(barrier, len(peers))


def ring_peers(place):
    return [place.peer(a, s) for a, s in (("x", 1), ("x", -1), ("z", 1), ("z", -1), ("y", 1))]


def tensor_peers(place):
    return [place.peer(a, 0) for a in ("core", "far", "both")]


class Sems:
    def __init__(self, send, recv):
        self.send, self.recv, self.used = send, recv, 0

    def take(self):
        self.used += 1
        return self.send.at[self.used - 1], self.recv.at[self.used - 1]


class Link:
    def __init__(self, sems, peer):
        self.send, self.recv = sems.take()
        self.peer = peer

    def copy(self, src, dst):
        return pltpu.make_async_remote_copy(
            src_ref=src, dst_ref=dst, send_sem=self.send, recv_sem=self.recv,
            device_id=self.peer, device_id_type=MESH,
        )

    def start(self, src, dst):
        self.out = self.copy(src, dst)
        self.out.start()

    def arrived(self, dst):
        self.copy(dst, dst).wait_recv()

    def sent(self):
        self.out.wait_send()


def paths_of(columns, both):
    half = columns // 2
    if both:
        return (("z", "x", pl.ds(0, half)), ("x", "z", pl.ds(half, half)))
    return (("z", "x", pl.ds(0, columns)),)


def region(ref, lead, where, cols):
    return ref.at[(ALL,) * lead + (where["y"], where["x"], where["z"], ALL, cols)]


class Gather:
    links = 17
    stages = 6

    def __init__(self, place, sems, own, full, lead, local_sem):
        self.place, self.own, self.full, self.lead, self.local_sem = place, own, full, lead, local_sem
        self.paths = paths_of(full.shape[-1], full.shape[-1] % 256 == 0)
        self.cross = Link(sems, place.peer("y", 1))
        self.rings = []
        for first, second, cols in self.paths:
            self.rings.append(
                [
                    [Link(sems, place.peer(axis, 1)), Link(sems, place.peer(axis, -1)),
                     Link(sems, place.peer(axis, 1)), Link(sems, place.peer(axis, -1))]
                    for axis in (first, second)
                ]
            )

    def _at(self, cols, **where):
        return region(self.full, self.lead, where, cols)

    def stage(self, number):
        place, everything = self.place, pl.ds(0, self.full.shape[-1])
        here = dict(place.at)
        if number == 0:
            mine = self._at(everything, **here)
            self.local = pltpu.make_async_copy(self.own, mine, self.local_sem)
            self.local.start()
            self.cross.start(self.own, mine)
            return
        if number == 1:
            self.local.wait()
            self.cross.arrived(self._at(everything, **{**here, "y": 1 - here["y"]}))
        for (first, second, cols), rings in zip(self.paths, self.rings):
            axis = first if number <= 2 else second
            other = here[second] if number <= 2 else ALL
            rest = second if number <= 2 else first
            ring = rings[0] if number <= 2 else rings[1]

            def at(y, step):
                index = here[axis] if step == 0 else place.plus(axis, step)
                return self._at(cols, **{"y": y, axis: index, rest: other})

            if number in (1, 3):
                if number == 3:
                    self._close(rings[0], first, second, cols, here[second])
                ring[0].start(at(ALL, 0), at(ALL, 0))
                ring[1].start(at(ALL, 0), at(ALL, 0))
            elif number in (2, 4):
                ring[0].arrived(at(ALL, -1))
                ring[2].start(at(0, -1), at(0, -1))
                ring[1].arrived(at(ALL, 1))
                ring[3].start(at(1, 1), at(1, 1))
            else:
                self._close(ring, axis, rest, cols, ALL)
        if number == 5:
            self.cross.sent()
            for rings in self.rings:
                for ring in rings:
                    for link in ring:
                        link.sent()

    def _close(self, ring, axis, rest, cols, other):
        opposite = self.place.plus(axis, 2)
        ring[2].arrived(self._at(cols, **{"y": 0, axis: opposite, rest: other}))
        ring[3].arrived(self._at(cols, **{"y": 1, axis: opposite, rest: other}))


class Reduce:
    stages = 6

    @staticmethod
    def links(columns):
        return 1 + 12 * len(paths_of(columns, columns % 256 == 0))

    @staticmethod
    def scratch(shape, dtype):
        *lead, _, _, _, rows, columns = shape
        lead = tuple(lead)
        shapes = []
        for _, _, cols in paths_of(columns, columns % 256 == 0):
            w = cols.size
            shapes += [pltpu.VMEM(lead + (2, 4, rows, w), dtype)]
            shapes += [pltpu.VMEM(lead + (2, 2, 4, rows, w), dtype)]
            shapes += [pltpu.VMEM(lead + (2, rows, w), dtype)]
            shapes += [pltpu.VMEM(lead + (2, 2, rows, w), dtype)]
        shapes += [pltpu.VMEM(lead + (2, rows, columns), jnp.float32)]
        shapes += [pltpu.VMEM(lead + (rows, columns), dtype)] * 2
        return shapes

    def __init__(self, place, sems, given, total, lead, scratch):
        self.place, self.given, self.total, self.lead = place, given, total, lead
        columns = given.shape[-1]
        self.dtype = given.dtype
        self.paths = paths_of(columns, columns % 256 == 0)
        self.cross = Link(sems, place.peer("y", 1))
        self.work = []
        for number, (first, second, cols) in enumerate(self.paths):
            ends = []
            for axis in (first, second):
                ends.append([Link(sems, place.peer(axis, s)) for s in (1, -1, 1, -1, 1, -1)])
            self.work.append((ends, scratch[4 * number : 4 * number + 4]))
        self.summed, self.leaving, self.coming = scratch[-3:]

    def _given(self, cols, **where):
        return region(self.given, self.lead, where, cols)

    def _pre(self, *index):
        return (ALL,) * self.lead + index

    def _add(self, into, *terms):
        total = terms[0][...].astype(jnp.float32)
        for term in terms[1:]:
            total = total + term[...].astype(jnp.float32)
        into[...] = total.astype(into.dtype)

    def _send(self, links, near, far, at):
        pre = self._pre
        links[0].start(at(0, 2), near.at[pre(0)])
        links[1].start(at(1, 2), near.at[pre(1)])
        links[2].start(at(1, 1), far.at[pre(0, 1)])
        links[3].start(at(0, -1), far.at[pre(1, 0)])

    def _pass(self, links, near, far, at):
        pre = self._pre
        for way, step in ((0, 1), (1, -1)):
            slot = near.at[pre(way)]
            links[way].arrived(slot)
            self._add(slot, slot, at(way, step))
            links[4 + way].start(slot, far.at[pre(way, way)])

    def _join(self, links, far):
        pre = self._pre
        links[2].arrived(far.at[pre(0, 1)])
        links[3].arrived(far.at[pre(1, 0)])
        links[4].arrived(far.at[pre(0, 0)])
        links[5].arrived(far.at[pre(1, 1)])

    def stage(self, number):
        place, pre = self.place, self._pre
        here = dict(place.at)
        for (first, second, cols), (ends, (near1, far1, near2, far2)) in zip(self.paths, self.work):

            def at1(y, step):
                index = here[first] if step == 0 else place.plus(first, step)
                return self._given(cols, **{"y": y, first: index, second: ALL})

            def at2(y, step):
                index = here[second] if step == 0 else place.plus(second, step)
                return far1.at[pre(0, y, index)]

            if number == 0:
                self._send(ends[0], near1, far1, at1)
            elif number == 1:
                self._pass(ends[0], near1, far1, at1)
            elif number == 2:
                self._join(ends[0], far1)
                for y in (0, 1):
                    slot = far1.at[pre(0, y)]
                    self._add(slot, slot, far1.at[pre(1, y)], at1(y, 0))
                self._send(ends[1], near2, far2, at2)
            elif number == 3:
                self._pass(ends[1], near2, far2, at2)
            elif number == 4:
                self._join(ends[1], far2)
                for y in (0, 1):
                    into = self.summed.at[pre(y, ALL, cols)]
                    self._add(into, at2(y, 0), far2.at[pre(0, y)], far2.at[pre(1, y)])
        if number == 4:
            self._add(self.leaving, self.summed.at[pre(1 - here["y"])])
            self.cross.start(self.leaving, self.coming)
        elif number == 5:
            self.cross.arrived(self.coming)
            self._add(self.total, self.summed.at[pre(here["y"])], self.coming)
            self.cross.sent()
            for ends, _ in self.work:
                for links in ends:
                    for link in links:
                        link.sent()


def skewed(jobs):
    last = max(job.stages for job in jobs)
    for step in range(len(jobs) + last):
        for number in range(len(jobs) - 1, -1, -1):
            stage = step - number
            if 0 <= stage < jobs[number].stages:
                jobs[number].stage(stage)


def gather_kernel(shapes, *refs):
    count = len(shapes)
    small, owned = refs[0], refs[1 : 1 + count]
    table, fulls = refs[1 + count], refs[2 + count : 2 + 2 * count]
    four, tile, sends, recvs, locals_ = refs[2 + 2 * count :]
    place = Place()
    sems = Sems(sends, recvs)
    meet(ring_peers(place) + tensor_peers(place))
    links = [Link(sems, peer) for peer in tensor_peers(place)]
    four[place.t] = small[...]
    for link in links:
        link.start(small, four.at[place.t])
    jobs = [
        Gather(place, sems, own, full, lead, locals_.at[number])
        for number, (own, full, lead) in enumerate(zip(owned, fulls, shapes))
    ]
    for job in jobs:
        job.stage(0)
    for link, flip in zip(links, (1, 2, 3)):
        link.arrived(four.at[place.t ^ flip])
    row = lax.broadcasted_iota(jnp.int32, (8, 128), 0)
    packed = jnp.zeros((8, 128), jnp.float32)
    for t in range(4):
        packed = jnp.where(row == t, four[t], packed)
    tile[...] = packed
    jobs = [Gather(place, sems, tile, table, 0, locals_.at[count])] + jobs
    jobs[0].stage(0)
    for job in jobs:
        job.stages = 5
        job.later = job.stage
        job.stage = functools.partial(lambda stage, number: stage(number + 1), job.later)
    skewed(jobs)
    for link in links:
        link.sent()


def gather_weights(small, pieces):
    outs = [jax.ShapeDtypeStruct((2, 4, 4, 8, 128), jnp.float32)]
    for own, lead in pieces:
        outs.append(jax.ShapeDtypeStruct(own.shape[:lead] + (2, 4, 4) + own.shape[lead:], own.dtype))
    count = len(pieces)
    number = 3 + Gather.links * (count + 1)
    anywhere = pl.BlockSpec(memory_space=pl.ANY)
    return pl.pallas_call(
        functools.partial(gather_kernel, tuple(lead for _, lead in pieces)),
        out_shape=outs,
        in_specs=[pl.BlockSpec(memory_space=pltpu.VMEM)] + [anywhere] * count,
        out_specs=[anywhere] * (count + 1),
        scratch_shapes=[
            pltpu.VMEM((4, 8, 128), jnp.float32),
            pltpu.VMEM((8, 128), jnp.float32),
            pltpu.SemaphoreType.DMA((number,)),
            pltpu.SemaphoreType.DMA((number,)),
            pltpu.SemaphoreType.DMA((count + 1,)),
        ],
        compiler_params=pltpu.CompilerParams(collective_id=0, has_side_effects=True),
        name="gather_weights",
    )(small, *[own for own, _ in pieces])


def scatter_kernel(leads, *refs):
    count = len(leads)
    table, given = refs[0], refs[1 : 1 + count]
    own_table, totals = refs[1 + count], refs[2 + count : 2 + 2 * count]
    rest = list(refs[2 + 2 * count :])
    four, tile, sends, recvs = rest[:4]
    rest = rest[4:]
    place = Place()
    sems = Sems(sends, recvs)
    meet(ring_peers(place) + tensor_peers(place))
    jobs = []
    for part, total, lead in zip((table,) + tuple(given), (tile,) + tuple(totals), (0,) + tuple(leads)):
        need = 4 * len(paths_of(part.shape[-1], part.shape[-1] % 256 == 0)) + 3
        jobs.append(Reduce(place, sems, part, total, lead, rest[:need]))
        rest = rest[need:]
    skewed(jobs)
    links = [Link(sems, peer) for peer in tensor_peers(place)]
    for number, link in enumerate(links):
        link.start(tile, four.at[number])
    whole = tile[...]
    for number, link in enumerate(links):
        link.arrived(four.at[number])
        whole = whole + four[number]
    own_table[...] = whole
    for link in links:
        link.sent()


def scatter_grads(table, pieces):
    outs = [jax.ShapeDtypeStruct((8, 128), jnp.float32)]
    scratch = Reduce.scratch(table.shape, table.dtype)
    number = 3 + Reduce.links(128)
    for part, lead in pieces:
        outs.append(jax.ShapeDtypeStruct(part.shape[:lead] + part.shape[lead + 3 :], jnp.float32))
        scratch += Reduce.scratch(part.shape, part.dtype)
        number += Reduce.links(part.shape[-1])
    count = len(pieces)
    inside = pl.BlockSpec(memory_space=pltpu.VMEM)
    return pl.pallas_call(
        functools.partial(scatter_kernel, tuple(lead for _, lead in pieces)),
        out_shape=outs,
        in_specs=[inside] * (count + 1),
        out_specs=[inside] * (count + 1),
        scratch_shapes=[
            pltpu.VMEM((3, 8, 128), jnp.float32),
            pltpu.VMEM((8, 128), jnp.float32),
            pltpu.SemaphoreType.DMA((number,)),
            pltpu.SemaphoreType.DMA((number,)),
        ]
        + scratch,
        compiler_params=pltpu.CompilerParams(
            collective_id=1, has_side_effects=True, vmem_limit_bytes=56 * 2**20
        ),
        name="scatter_grads",
    )(table, *[part for part, _ in pieces])


CHUNKS = 4


def rows_kernel(own, full, local_sem, sends, recvs):
    place = Place()
    sems = Sems(sends, recvs)
    t = place.t
    meet([place.peer("core", 0), place.peer("far", 0)])
    rows = own.shape[0] // CHUNKS
    local = pltpu.make_async_copy(own, full.at[t], local_sem)
    local.start()
    far = [Link(sems, place.peer("far", 0)) for _ in range(CHUNKS)]
    onward = [Link(sems, place.peer("core", 0)) for _ in range(CHUNKS)]
    near = Link(sems, place.peer("core", 0))
    part = [pl.ds(k * rows, rows) for k in range(CHUNKS)]
    for k in range(CHUNKS):
        far[k].start(own.at[part[k]], full.at[t, part[k]])
    near.start(own, full.at[t])
    for k in range(CHUNKS):
        got = full.at[t ^ 2, part[k]]
        far[k].arrived(got)
        onward[k].start(got, got)
    near.arrived(full.at[t ^ 1])
    for k in range(CHUNKS):
        onward[k].arrived(full.at[t ^ 3, part[k]])
    for link in far + onward + [near]:
        link.sent()
    local.wait()


def gather_rows(own):
    count, width = own.shape
    number = 2 * CHUNKS + 1
    anywhere = pl.BlockSpec(memory_space=pl.ANY)
    full = pl.pallas_call(
        rows_kernel,
        out_shape=jax.ShapeDtypeStruct((4, count, width), own.dtype),
        in_specs=[anywhere],
        out_specs=anywhere,
        scratch_shapes=[
            pltpu.SemaphoreType.DMA,
            pltpu.SemaphoreType.DMA((number,)),
            pltpu.SemaphoreType.DMA((number,)),
        ],
        compiler_params=pltpu.CompilerParams(collective_id=2, has_side_effects=True),
        name="gather_rows",
    )(own)
    return full.reshape(4 * count, width)


def sum_rows_kernel(given, total, pair, across, sends, recvs):
    place = Place()
    sems = Sems(sends, recvs)
    t = place.t
    meet([place.peer("core", 0), place.peer("far", 0)])
    rows = given.shape[1] // CHUNKS
    part = [pl.ds(k * rows, rows) for k in range(CHUNKS)]
    to_core = [Link(sems, place.peer("core", 0)) for _ in range(CHUNKS)]
    far = [Link(sems, place.peer("far", 0)) for _ in range(CHUNKS)]
    near = Link(sems, place.peer("core", 0))
    for k in range(CHUNKS):
        to_core[k].start(given.at[t ^ 3, part[k]], pair.at[0, part[k]])
    near.start(given.at[t ^ 1], pair.at[1])
    for k in range(CHUNKS):
        slot = pair.at[0, part[k]]
        to_core[k].arrived(slot)
        slot[...] = (
            slot[...].astype(jnp.float32) + given[t ^ 2, part[k]].astype(jnp.float32)
        ).astype(slot.dtype)
        far[k].start(slot, across.at[part[k]])
    near.arrived(pair.at[1])
    for k in range(CHUNKS):
        far[k].arrived(across.at[part[k]])
        total[part[k]] = (
            given[t, part[k]].astype(jnp.float32)
            + pair[1, part[k]].astype(jnp.float32)
            + across[part[k]].astype(jnp.float32)
        )
    for link in to_core + far + [near]:
        link.sent()


def sum_rows(partial):
    count, width = partial.shape
    number = 2 * CHUNKS + 1
    inside = pl.BlockSpec(memory_space=pltpu.VMEM)
    own = count // 4
    return pl.pallas_call(
        sum_rows_kernel,
        out_shape=jax.ShapeDtypeStruct((own, width), jnp.float32),
        in_specs=[inside],
        out_specs=inside,
        scratch_shapes=[
            pltpu.VMEM((2, own, width), partial.dtype),
            pltpu.VMEM((own, width), partial.dtype),
            pltpu.SemaphoreType.DMA((number,)),
            pltpu.SemaphoreType.DMA((number,)),
        ],
        compiler_params=pltpu.CompilerParams(
            collective_id=3, has_side_effects=True, vmem_limit_bytes=32 * 2**20
        ),
        name="sum_rows",
    )(partial.reshape(4, own, width))


def seq_positions(segments):
    count = segments.shape[0]
    index = jnp.arange(count, dtype=jnp.int32)
    first = jnp.concatenate([jnp.ones((1,), dtype=bool), segments[1:] != segments[:-1]])
    begin = lax.cummax(jnp.where(first, index, 0), axis=0)
    return index - begin


def rotary_tables(positions):
    half = ROT // 2
    freq = jnp.exp(jnp.arange(half, dtype=jnp.float32) * (-2.0 * math.log(10000.0) / ROT))
    angle = positions.astype(jnp.float32)[:, None] * freq[None, :]
    return (jnp.cos(angle)[:, None, :], jnp.sin(angle)[:, None, :])


def rotate(heads, cosine, sine):
    half = ROT // 2
    first = heads[..., :half]
    second = heads[..., half:ROT]
    return jnp.concatenate(
        [first * cosine - second * sine, second * cosine + first * sine, heads[..., ROT:]], axis=-1
    )


def contract_rows(left, right):
    return lax.dot_general(
        left, right, (((0,), (0,)), ((), ())), preferred_element_type=jnp.float32
    )


def contract_cols(left, right):
    return lax.dot_general(
        left, right, (((1,), (1,)), ((), ())), preferred_element_type=jnp.float32
    )


def masked_scores(query, keys, segments, start, size, stop):
    index = jnp.arange(segments.shape[0], dtype=jnp.int32)
    own_ids = segments[start : start + size]
    allowed = (own_ids[:, None] == segments[None, :stop]) & (
        index[start : start + size, None] >= index[None, :stop]
    )
    scale = query.shape[-1] ** (-0.5)
    scores = (
        jnp.einsum(
            "qhe,khe->hqk",
            query[start : start + size],
            keys[:stop],
            preferred_element_type=jnp.float32,
        )
        * scale
    )
    return jnp.where(allowed[None], scores, -1e30)


def attend_forward(query, keys, values, segments):
    count = query.shape[0]
    size = min(block_rows, count)
    outputs = []
    totals = []
    for block in range(count // size):
        start = block * size
        stop = start + size
        scores = masked_scores(query, keys, segments, start, size, stop)
        peak = jnp.max(scores, axis=-1, keepdims=True)
        weights = jnp.exp(scores - peak)
        total = jnp.sum(weights, axis=-1, keepdims=True)
        probs = (weights / total).astype(jnp.bfloat16)
        outputs.append(
            jnp.einsum("hqk,khe->qhe", probs, values[:stop], preferred_element_type=jnp.float32)
        )
        totals.append(peak + jnp.log(total))
    return (jnp.concatenate(outputs, axis=0), jnp.concatenate(totals, axis=1))


def attend_backward(query, keys, values, segments, logsum, grad_out):
    count = query.shape[0]
    size = min(block_rows, count)
    scale = query.shape[-1] ** (-0.5)
    grad_keys = jnp.zeros(keys.shape, jnp.float32)
    grad_values = jnp.zeros(values.shape, jnp.float32)
    grad_rows = []
    for block in range(count // size):
        start = block * size
        stop = start + size
        scores = masked_scores(query, keys, segments, start, size, stop)
        probs = jnp.exp(scores - logsum[:, start:stop])
        probs_low = probs.astype(jnp.bfloat16)
        grad_block = grad_out[start:stop]
        grad_values = grad_values.at[:stop].add(
            jnp.einsum("hqk,qhe->khe", probs_low, grad_block, preferred_element_type=jnp.float32)
        )
        grad_probs = jnp.einsum(
            "qhe,khe->hqk", grad_block, values[:stop], preferred_element_type=jnp.float32
        )
        delta = jnp.sum(probs * grad_probs, axis=-1, keepdims=True)
        grad_scores = (probs * (grad_probs - delta)).astype(jnp.bfloat16)
        grad_rows.append(
            jnp.einsum("hqk,khe->qhe", grad_scores, keys[:stop], preferred_element_type=jnp.float32)
            * scale
        )
        grad_keys = grad_keys.at[:stop].add(
            jnp.einsum(
                "hqk,qhe->khe", grad_scores, query[start:stop], preferred_element_type=jnp.float32
            )
            * scale
        )
    return (jnp.concatenate(grad_rows, axis=0), grad_keys, grad_values)


def layer_forward(state, gain, shift, weights, bias_final, segments, cosine, sine):
    qkv_full, proj_full, up_full, hidden_full, down_full = weights
    center = state - jnp.mean(state, axis=-1, keepdims=True)
    inverse = lax.rsqrt(jnp.mean(center * center, axis=-1, keepdims=True) + epsilon)
    unit = center * inverse
    normed_own = (unit * gain + shift).astype(jnp.bfloat16)
    normed = gather_rows(normed_own)
    count = normed.shape[0]
    joined = jnp.einsum("td,cde->cte", normed, qkv_full, preferred_element_type=jnp.float32)
    joined = joined.reshape(3, count, -1, HEAD_DIM)
    query = rotate(joined[0], cosine, sine).astype(jnp.bfloat16)
    keys = rotate(joined[1], cosine, sine).astype(jnp.bfloat16)
    values = joined[2].astype(jnp.bfloat16)
    attended, logsum = attend_forward(query, keys, values, segments)
    attended = attended.astype(jnp.bfloat16).reshape(count, -1)
    up = jnp.dot(normed, up_full, preferred_element_type=jnp.float32) + hidden_full
    active = jax.nn.gelu(up, approximate=True).astype(jnp.bfloat16)
    local_sum = jnp.dot(attended, proj_full, preferred_element_type=jnp.float32) + jnp.dot(
        active, down_full, preferred_element_type=jnp.float32
    )
    branch = sum_rows(local_sum.astype(jnp.bfloat16))
    result = state + branch + bias_final
    kept = (unit, inverse, normed, query, keys, values, logsum, attended, up, active)
    return (result, kept)


def layer_backward(grad, gain, weights, kept, segments, cosine, sine):
    qkv_full, proj_full, up_full, hidden_full, down_full = weights
    unit, inverse, normed, query, keys, values, logsum, attended, up, active = kept
    count = normed.shape[0]
    grad_final = jnp.sum(grad, axis=0)
    grad_rows = gather_rows(grad.astype(jnp.bfloat16))
    grad_down = contract_rows(active, grad_rows)
    grad_active = contract_cols(grad_rows, down_full)
    _, gelu_back = jax.vjp(lambda value: jax.nn.gelu(value, approximate=True), up)
    grad_up = gelu_back(grad_active)[0].astype(jnp.bfloat16)
    grad_hidden = jnp.sum(grad_up, axis=0, dtype=jnp.float32)
    grad_upw = contract_rows(normed, grad_up)
    grad_normed = contract_cols(grad_up, up_full)
    grad_proj = contract_rows(attended, grad_rows)
    grad_attended = contract_cols(grad_rows, proj_full).astype(jnp.bfloat16).reshape(query.shape)
    grad_query, grad_keys, grad_values = attend_backward(
        query, keys, values, segments, logsum, grad_attended
    )
    grad_query = rotate(grad_query, cosine, -sine)
    grad_keys = rotate(grad_keys, cosine, -sine)
    grad_joined = (
        jnp.stack([grad_query, grad_keys, grad_values]).reshape(3, count, -1).astype(jnp.bfloat16)
    )
    grad_qkv = jnp.einsum("td,cte->cde", normed, grad_joined, preferred_element_type=jnp.float32)
    grad_normed = grad_normed + jnp.einsum(
        "cte,cde->td", grad_joined, qkv_full, preferred_element_type=jnp.float32
    )
    grad_own = sum_rows(grad_normed.astype(jnp.bfloat16))
    grad_gain = jnp.sum(grad_own * unit, axis=0)
    grad_shift = jnp.sum(grad_own, axis=0)
    scaled = grad_own * gain
    grad_state = grad + inverse * (
        scaled
        - jnp.mean(scaled, axis=-1, keepdims=True)
        - unit * jnp.mean(scaled * unit, axis=-1, keepdims=True)
    )
    return (
        grad_state,
        (grad_qkv, grad_proj, grad_upw, grad_hidden, grad_down),
        (grad_gain, grad_shift, grad_final),
    )


def fold(rows):
    return jnp.concatenate([rows[..., :512], rows[..., 512:]], axis=-2)


def unfold(rows):
    return jnp.concatenate([rows[..., :8, :], rows[..., 8:, :]], axis=-1)


def local(
    tokens,
    segment_ids,
    norm_gain,
    norm_shift,
    qkv_weight,
    proj_weight,
    up_weight,
    hidden_bias,
    down_weight,
    final_bias,
    cotangent,
):
    layers = qkv_weight.shape[0]
    f32 = jnp.float32
    row = jnp.concatenate(
        [norm_gain.reshape(16), norm_shift.reshape(16), final_bias.reshape(16), hidden_bias.reshape(64)]
    ).astype(f32)
    small = jnp.broadcast_to(jnp.pad(row, (0, 16))[None], (8, 128))
    pieces = []
    proj_own = fold(proj_weight)
    for layer in range(layers):
        pieces += [
            (qkv_weight[layer], 1), (up_weight[layer], 0), (down_weight[layer], 0), (proj_own[layer], 0)
        ]
    table, *wholes = gather_weights(small, pieces)
    table = table.reshape(32, 8, 128)[:, :4]

    def features(start):
        return table[:, :, start : start + 16].reshape(128, 2, 8).transpose(1, 0, 2).reshape(2, 1024)

    gains, shifts, finals = features(0), features(16), features(32)
    t = lax.axis_index("tensor")
    mine = lax.dynamic_index_in_dim(table, t, axis=1, keepdims=False)
    hidden = mine[:, 48:112].reshape(32, 2, 32).transpose(1, 0, 2).reshape(2, 1024)
    weights = []
    for layer in range(layers):
        qkv, up, down, proj = wholes[4 * layer : 4 * layer + 4]
        weights.append(
            (
                qkv.reshape(3, 1024, 256),
                unfold(proj.reshape(32, 16, 512)).reshape(256, 1024),
                up.reshape(1024, 1024),
                hidden[layer],
                down.reshape(1024, 1024),
            )
        )
    positions = seq_positions(segment_ids)
    cosine, sine = rotary_tables(positions)
    state = tokens.astype(jnp.float32)
    saved = []
    for layer in range(layers):
        state, kept = layer_forward(
            state, gains[layer], shifts[layer], weights[layer], finals[layer], segment_ids, cosine, sine
        )
        saved.append(kept)
    mixed = state.astype(jnp.bfloat16)
    grad = cotangent.astype(jnp.float32)
    weight_terms = [None] * layers
    norm_terms = [None] * layers
    for layer in reversed(range(layers)):
        grad, weight_terms[layer], norm_terms[layer] = layer_backward(
            grad, gains[layer], weights[layer], saved[layer], segment_ids, cosine, sine
        )
    low = jnp.bfloat16
    parts = []
    for layer in reversed(range(layers)):
        qkv, proj, up, _, down = weight_terms[layer]
        parts += [
            (down.astype(low).reshape(2, 4, 4, 32, 1024), 0),
            (up.astype(low).reshape(2, 4, 4, 32, 1024), 0),
            (fold(proj.reshape(32, 8, 1024)).astype(low).reshape(2, 4, 4, 16, 512), 0),
            (qkv.astype(low).reshape(3, 2, 4, 4, 32, 256), 1),
        ]

    def spread(member):
        both = jnp.stack([norm_terms[layer][member] for layer in range(layers)])
        return both.reshape(2, 32, 4, 8).transpose(1, 2, 0, 3).reshape(32, 4, 16)

    hid = jnp.stack([weight_terms[layer][3] for layer in range(layers)])
    hid = hid.reshape(2, 32, 32).transpose(1, 0, 2).reshape(32, 1, 64)
    hid = jnp.where(jnp.arange(4)[None, :, None] == t, hid, 0.0)
    sums = jnp.concatenate([spread(0), spread(1), spread(2), hid], axis=-1)
    sums = jnp.pad(sums, ((0, 0), (0, 4), (0, 16))).reshape(2, 4, 4, 8, 128)
    own_sums, *owned = scatter_grads(sums, parts)
    line = lax.dynamic_index_in_dim(own_sums, t, axis=0, keepdims=False)
    down, up, proj, qkv = [jnp.stack([owned[4 + k], owned[k]]) for k in range(4)]
    return (
        mixed,
        grad,
        line[0:16].reshape(2, 8),
        line[16:32].reshape(2, 8),
        qkv,
        unfold(proj),
        up,
        line[48:112].reshape(2, 32),
        down,
        line[32:48].reshape(2, 8),
    )


def solution(mesh):
    placed = (
        P(("dp", "tensor"), None),
        P("dp"),
        P(None, ("dp", "tensor")),
        P(None, ("dp", "tensor")),
        P(None, None, "dp", "tensor"),
        P(None, ("tensor", "dp"), None),
        P(None, "dp", "tensor"),
        P(None, ("tensor", "dp")),
        P(None, ("tensor", "dp"), None),
        P(None, ("dp", "tensor")),
        P(("dp", "tensor"), None),
    )
    return jax.shard_map(
        local,
        mesh=mesh,
        in_specs=placed,
        out_specs=(
            P(("dp", "tensor"), None),
            P(("dp", "tensor"), None),
            P(None, ("dp", "tensor")),
            P(None, ("dp", "tensor")),
            P(None, None, "dp", "tensor"),
            P(None, ("tensor", "dp"), None),
            P(None, "dp", "tensor"),
            P(None, ("tensor", "dp")),
            P(None, ("tensor", "dp"), None),
            P(None, ("dp", "tensor")),
        ),
        check_vma=False,
    )
```

```python
import functools
import math

import jax
import jax.numpy as jnp
from jax import lax
from jax.experimental import pallas as pl
from jax.experimental.pallas import tpu as pltpu
from jax.sharding import PartitionSpec as P

HEAD_DIM = 64
ROT = 32
MESH = pl.DeviceIdType.MESH
ALL = slice(None)


epsilon = 1e-05


class Place:
    def __init__(self):
        dp = lax.axis_index("dp")
        self.t = lax.axis_index("tensor")
        self.dp = dp
        self.at = {"y": dp // 16, "x": lax.rem(dp // 4, 4), "z": lax.rem(dp, 4)}

    def plus(self, axis, step):
        return lax.rem(self.at[axis] + (step % 4), 4)

    def peer(self, axis, step):
        if axis == "core":
            return (self.dp, self.t ^ 1)
        if axis == "far":
            return (self.dp, self.t ^ 2)
        if axis == "both":
            return (self.dp, self.t ^ 3)
        c = dict(self.at)
        c[axis] = 1 - c["y"] if axis == "y" else self.plus(axis, step)
        return ((c["y"] * 4 + c["x"]) * 4 + c["z"], self.t)


def meet(peers):
    barrier = pltpu.get_barrier_semaphore()
    for peer in peers:
        pl.semaphore_signal(barrier, inc=1, device_id=peer, device_id_type=MESH)
    pl.semaphore_wait(barrier, len(peers))


def ring_peers(place):
    return [place.peer(a, s) for a, s in (("x", 1), ("x", -1), ("z", 1), ("z", -1), ("y", 1))]


def tensor_peers(place):
    return [place.peer(a, 0) for a in ("core", "far", "both")]


class Sems:
    def __init__(self, send, recv):
        self.send, self.recv, self.used = send, recv, 0

    def take(self):
        self.used += 1
        return self.send.at[self.used - 1], self.recv.at[self.used - 1]


class Link:
    def __init__(self, sems, peer):
        self.send, self.recv = sems.take()
        self.peer = peer

    def copy(self, src, dst):
        return pltpu.make_async_remote_copy(
            src_ref=src, dst_ref=dst, send_sem=self.send, recv_sem=self.recv,
            device_id=self.peer, device_id_type=MESH,
        )

    def start(self, src, dst):
        self.out = self.copy(src, dst)
        self.out.start()

    def arrived(self, dst):
        self.copy(dst, dst).wait_recv()

    def sent(self):
        self.out.wait_send()


def paths_of(columns, both):
    half = columns // 2
    if both:
        return (("z", "x", pl.ds(0, half)), ("x", "z", pl.ds(half, half)))
    return (("z", "x", pl.ds(0, columns)),)


def region(ref, lead, where, cols):
    return ref.at[(ALL,) * lead + (where["y"], where["x"], where["z"], ALL, cols)]


class Gather:
    links = 17
    stages = 6

    def __init__(self, place, sems, own, full, lead, local_sem):
        self.place, self.own, self.full, self.lead, self.local_sem = place, own, full, lead, local_sem
        self.paths = paths_of(full.shape[-1], full.shape[-1] % 256 == 0)
        self.cross = Link(sems, place.peer("y", 1))
        self.rings = []
        for first, second, cols in self.paths:
            self.rings.append(
                [
                    [Link(sems, place.peer(axis, 1)), Link(sems, place.peer(axis, -1)),
                     Link(sems, place.peer(axis, 1)), Link(sems, place.peer(axis, -1))]
                    for axis in (first, second)
                ]
            )

    def _at(self, cols, **where):
        return region(self.full, self.lead, where, cols)

    def stage(self, number):
        place, everything = self.place, pl.ds(0, self.full.shape[-1])
        here = dict(place.at)
        if number == 0:
            mine = self._at(everything, **here)
            self.local = pltpu.make_async_copy(self.own, mine, self.local_sem)
            self.local.start()
            self.cross.start(self.own, mine)
            return
        if number == 1:
            self.local.wait()
            self.cross.arrived(self._at(everything, **{**here, "y": 1 - here["y"]}))
        for (first, second, cols), rings in zip(self.paths, self.rings):
            axis = first if number <= 2 else second
            other = here[second] if number <= 2 else ALL
            rest = second if number <= 2 else first
            ring = rings[0] if number <= 2 else rings[1]

            def at(y, step):
                index = here[axis] if step == 0 else place.plus(axis, step)
                return self._at(cols, **{"y": y, axis: index, rest: other})

            if number in (1, 3):
                if number == 3:
                    self._close(rings[0], first, second, cols, here[second])
                ring[0].start(at(ALL, 0), at(ALL, 0))
                ring[1].start(at(ALL, 0), at(ALL, 0))
            elif number in (2, 4):
                ring[0].arrived(at(ALL, -1))
                ring[2].start(at(0, -1), at(0, -1))
                ring[1].arrived(at(ALL, 1))
                ring[3].start(at(1, 1), at(1, 1))
            else:
                self._close(ring, axis, rest, cols, ALL)
        if number == 5:
            self.cross.sent()
            for rings in self.rings:
                for ring in rings:
                    for link in ring:
                        link.sent()

    def _close(self, ring, axis, rest, cols, other):
        opposite = self.place.plus(axis, 2)
        ring[2].arrived(self._at(cols, **{"y": 0, axis: opposite, rest: other}))
        ring[3].arrived(self._at(cols, **{"y": 1, axis: opposite, rest: other}))


class Reduce:
    stages = 6

    @staticmethod
    def links(columns):
        return 1 + 12 * len(paths_of(columns, columns % 256 == 0))

    @staticmethod
    def scratch(shape, dtype):
        *lead, _, _, _, rows, columns = shape
        lead = tuple(lead)
        shapes = []
        for _, _, cols in paths_of(columns, columns % 256 == 0):
            w = cols.size
            shapes += [pltpu.VMEM(lead + (2, 4, rows, w), dtype)]
            shapes += [pltpu.VMEM(lead + (2, 2, 4, rows, w), dtype)]
            shapes += [pltpu.VMEM(lead + (2, rows, w), dtype)]
            shapes += [pltpu.VMEM(lead + (2, 2, rows, w), dtype)]
        shapes += [pltpu.VMEM(lead + (2, rows, columns), jnp.float32)]
        shapes += [pltpu.VMEM(lead + (rows, columns), dtype)] * 2
        return shapes

    def __init__(self, place, sems, given, total, lead, scratch):
        self.place, self.given, self.total, self.lead = place, given, total, lead
        columns = given.shape[-1]
        self.dtype = given.dtype
        self.paths = paths_of(columns, columns % 256 == 0)
        self.cross = Link(sems, place.peer("y", 1))
        self.work = []
        for number, (first, second, cols) in enumerate(self.paths):
            ends = []
            for axis in (first, second):
                ends.append([Link(sems, place.peer(axis, s)) for s in (1, -1, 1, -1, 1, -1)])
            self.work.append((ends, scratch[4 * number : 4 * number + 4]))
        self.summed, self.leaving, self.coming = scratch[-3:]

    def _given(self, cols, **where):
        return region(self.given, self.lead, where, cols)

    def _pre(self, *index):
        return (ALL,) * self.lead + index

    def _add(self, into, *terms):
        total = terms[0][...].astype(jnp.float32)
        for term in terms[1:]:
            total = total + term[...].astype(jnp.float32)
        into[...] = total.astype(into.dtype)

    def _send(self, links, near, far, at):
        pre = self._pre
        links[0].start(at(0, 2), near.at[pre(0)])
        links[1].start(at(1, 2), near.at[pre(1)])
        links[2].start(at(1, 1), far.at[pre(0, 1)])
        links[3].start(at(0, -1), far.at[pre(1, 0)])

    def _pass(self, links, near, far, at):
        pre = self._pre
        for way, step in ((0, 1), (1, -1)):
            slot = near.at[pre(way)]
            links[way].arrived(slot)
            self._add(slot, slot, at(way, step))
            links[4 + way].start(slot, far.at[pre(way, way)])

    def _join(self, links, far):
        pre = self._pre
        links[2].arrived(far.at[pre(0, 1)])
        links[3].arrived(far.at[pre(1, 0)])
        links[4].arrived(far.at[pre(0, 0)])
        links[5].arrived(far.at[pre(1, 1)])

    def stage(self, number):
        place, pre = self.place, self._pre
        here = dict(place.at)
        for (first, second, cols), (ends, (near1, far1, near2, far2)) in zip(self.paths, self.work):

            def at1(y, step):
                index = here[first] if step == 0 else place.plus(first, step)
                return self._given(cols, **{"y": y, first: index, second: ALL})

            def at2(y, step):
                index = here[second] if step == 0 else place.plus(second, step)
                return far1.at[pre(0, y, index)]

            if number == 0:
                self._send(ends[0], near1, far1, at1)
            elif number == 1:
                self._pass(ends[0], near1, far1, at1)
            elif number == 2:
                self._join(ends[0], far1)
                for y in (0, 1):
                    slot = far1.at[pre(0, y)]
                    self._add(slot, slot, far1.at[pre(1, y)], at1(y, 0))
                self._send(ends[1], near2, far2, at2)
            elif number == 3:
                self._pass(ends[1], near2, far2, at2)
            elif number == 4:
                self._join(ends[1], far2)
                for y in (0, 1):
                    into = self.summed.at[pre(y, ALL, cols)]
                    self._add(into, at2(y, 0), far2.at[pre(0, y)], far2.at[pre(1, y)])
        if number == 4:
            self._add(self.leaving, self.summed.at[pre(1 - here["y"])])
            self.cross.start(self.leaving, self.coming)
        elif number == 5:
            self.cross.arrived(self.coming)
            self._add(self.total, self.summed.at[pre(here["y"])], self.coming)
            self.cross.sent()
            for ends, _ in self.work:
                for links in ends:
                    for link in links:
                        link.sent()


def skewed(jobs):
    last = max(job.stages for job in jobs)
    for step in range(len(jobs) + last):
        for number in range(len(jobs) - 1, -1, -1):
            stage = step - number
            if 0 <= stage < jobs[number].stages:
                jobs[number].stage(stage)


def gather_kernel(shapes, *refs):
    count = len(shapes)
    small, owned = refs[0], refs[1 : 1 + count]
    table, fulls = refs[1 + count], refs[2 + count : 2 + 2 * count]
    four, tile, sends, recvs, locals_ = refs[2 + 2 * count :]
    place = Place()
    sems = Sems(sends, recvs)
    meet(ring_peers(place) + tensor_peers(place))
    links = [Link(sems, peer) for peer in tensor_peers(place)]
    four[place.t] = small[...]
    for link in links:
        link.start(small, four.at[place.t])
    jobs = [
        Gather(place, sems, own, full, lead, locals_.at[number])
        for number, (own, full, lead) in enumerate(zip(owned, fulls, shapes))
    ]
    for job in jobs:
        job.stage(0)
    for link, flip in zip(links, (1, 2, 3)):
        link.arrived(four.at[place.t ^ flip])
    row = lax.broadcasted_iota(jnp.int32, (8, 128), 0)
    packed = jnp.zeros((8, 128), jnp.float32)
    for t in range(4):
        packed = jnp.where(row == t, four[t], packed)
    tile[...] = packed
    jobs = [Gather(place, sems, tile, table, 0, locals_.at[count])] + jobs
    jobs[0].stage(0)
    for job in jobs:
        job.stages = 5
        job.later = job.stage
        job.stage = functools.partial(lambda stage, number: stage(number + 1), job.later)
    skewed(jobs)
    for link in links:
        link.sent()


def gather_weights(small, pieces):
    outs = [jax.ShapeDtypeStruct((2, 4, 4, 8, 128), jnp.float32)]
    for own, lead in pieces:
        outs.append(jax.ShapeDtypeStruct(own.shape[:lead] + (2, 4, 4) + own.shape[lead:], own.dtype))
    count = len(pieces)
    number = 3 + Gather.links * (count + 1)
    anywhere = pl.BlockSpec(memory_space=pl.ANY)
    return pl.pallas_call(
        functools.partial(gather_kernel, tuple(lead for _, lead in pieces)),
        out_shape=outs,
        in_specs=[pl.BlockSpec(memory_space=pltpu.VMEM)] + [anywhere] * count,
        out_specs=[anywhere] * (count + 1),
        scratch_shapes=[
            pltpu.VMEM((4, 8, 128), jnp.float32),
            pltpu.VMEM((8, 128), jnp.float32),
            pltpu.SemaphoreType.DMA((number,)),
            pltpu.SemaphoreType.DMA((number,)),
            pltpu.SemaphoreType.DMA((count + 1,)),
        ],
        compiler_params=pltpu.CompilerParams(collective_id=0, has_side_effects=True),
        name="gather_weights",
    )(small, *[own for own, _ in pieces])


def scatter_kernel(leads, *refs):
    count = len(leads)
    table, given = refs[0], refs[1 : 1 + count]
    own_table, totals = refs[1 + count], refs[2 + count : 2 + 2 * count]
    rest = list(refs[2 + 2 * count :])
    four, tile, sends, recvs = rest[:4]
    rest = rest[4:]
    place = Place()
    sems = Sems(sends, recvs)
    meet(ring_peers(place) + tensor_peers(place))
    jobs = []
    for part, total, lead in zip((table,) + tuple(given), (tile,) + tuple(totals), (0,) + tuple(leads)):
        need = 4 * len(paths_of(part.shape[-1], part.shape[-1] % 256 == 0)) + 3
        jobs.append(Reduce(place, sems, part, total, lead, rest[:need]))
        rest = rest[need:]
    skewed(jobs)
    links = [Link(sems, peer) for peer in tensor_peers(place)]
    for number, link in enumerate(links):
        link.start(tile, four.at[number])
    whole = tile[...]
    for number, link in enumerate(links):
        link.arrived(four.at[number])
        whole = whole + four[number]
    own_table[...] = whole
    for link in links:
        link.sent()


def scatter_grads(table, pieces):
    outs = [jax.ShapeDtypeStruct((8, 128), jnp.float32)]
    scratch = Reduce.scratch(table.shape, table.dtype)
    number = 3 + Reduce.links(128)
    for part, lead in pieces:
        outs.append(jax.ShapeDtypeStruct(part.shape[:lead] + part.shape[lead + 3 :], jnp.float32))
        scratch += Reduce.scratch(part.shape, part.dtype)
        number += Reduce.links(part.shape[-1])
    count = len(pieces)
    inside = pl.BlockSpec(memory_space=pltpu.VMEM)
    return pl.pallas_call(
        functools.partial(scatter_kernel, tuple(lead for _, lead in pieces)),
        out_shape=outs,
        in_specs=[inside] * (count + 1),
        out_specs=[inside] * (count + 1),
        scratch_shapes=[
            pltpu.VMEM((3, 8, 128), jnp.float32),
            pltpu.VMEM((8, 128), jnp.float32),
            pltpu.SemaphoreType.DMA((number,)),
            pltpu.SemaphoreType.DMA((number,)),
        ]
        + scratch,
        compiler_params=pltpu.CompilerParams(
            collective_id=1, has_side_effects=True, vmem_limit_bytes=56 * 2**20
        ),
        name="scatter_grads",
    )(table, *[part for part, _ in pieces])


CHUNKS = 4


TOK = 256
BF = jnp.bfloat16
F32 = jnp.float32


def dot(left, right):
    return jnp.dot(left, right, preferred_element_type=F32)


def dot_cols(left, right):
    return lax.dot_general(left, right, (((1,), (1,)), ((), ())), preferred_element_type=F32)


def dot_rows(left, right):
    return lax.dot_general(left, right, (((0,), (0,)), ((), ())), preferred_element_type=F32)


def rows_of(block):
    return pl.ds(pl.multiple_of(block * TOK, TOK), TOK)


def turned(z, table, rows, sign):
    ahead, behind = pltpu.roll(z, 112, 1), pltpu.roll(z, 16, 1)
    if sign > 0:
        return z * table[0, rows] + ahead * table[1, rows] + behind * table[2, rows]
    return z * table[0, rows] - ahead * table[1, rows] - behind * table[2, rows]


def gelu_and_slope(u):
    c, a = math.sqrt(2.0 / math.pi), 0.044715
    square = u * u
    t = jnp.tanh(c * u * (1.0 + a * square))
    half = 0.5 * (1.0 + t)
    return u * half, half + (0.5 * c) * u * (1.0 - t * t) * (1.0 + (3.0 * a) * square)


def normalize(x):
    center = x - jnp.mean(x, axis=-1, keepdims=True)
    inverse = lax.rsqrt(jnp.mean(center * center, axis=-1, keepdims=True) + epsilon)
    return center * inverse, inverse


class Loads:
    def __init__(self, sems):
        self.sems, self.used, self.open = sems, 0, []

    def start(self, src, dst):
        copy = pltpu.make_async_copy(src, dst, self.sems.at[self.used])
        self.used += 1
        copy.start()
        self.open.append(copy)
        return copy

    def finish(self):
        for copy in self.open:
            copy.wait()
        self.open = []


def attend(r, query, keys, values, begin, attended, marks, lse):
    width = (r + 1) * TOK
    rows = pl.ds(r * TOK, TOK)
    row = lax.broadcasted_iota(jnp.int32, (TOK, width), 0) + r * TOK
    column = lax.broadcasted_iota(jnp.int32, (TOK, width), 1)
    allowed = (column >= begin[rows]) & (column <= row)
    lane = lax.broadcasted_iota(jnp.int32, (TOK, 128), 1)

    def pair(g, _):
        lanes = pl.ds(pl.multiple_of(g * 128, 128), 128)
        q, k, v = query[rows, lanes], keys[:width, lanes], values[:width, lanes]
        outs = []
        for half in range(2):
            mine = jnp.where((lane // 64) == half, q, jnp.zeros_like(q))
            scores = jnp.where(allowed, dot_cols(mine, k), -1e30)
            peak = jnp.max(scores, axis=-1, keepdims=True)
            weights = jnp.exp(scores - peak)
            total = jnp.sum(weights, axis=-1, keepdims=True)
            outs.append(dot(weights.astype(BF), v) * (1.0 / total))
            marks[...] = jnp.where(lane == 2 * g + half, peak + jnp.log(total), marks[...])
        attended[rows, lanes] = jnp.where(lane < 64, outs[0], outs[1]).astype(BF)
        return 0

    lax.fori_loop(0, 2, pair, 0)
    lse[:, rows] = marks[...].T[:8]


def forward_kernel(
    state, norms, table, begin, qkv_h, up_h, down_h, proj_h,
    result, lse, normed_h, joined_h, attended_h, active_h, slope_h,
    wq, wu, wd, wp, normed, joined, attended, active, slope, partial, pair, across, marks,
    loads, sends, recvs,
):
    place = Place()
    sems = Sems(sends, recvs)
    t = place.t
    yh = t // 2
    core, far = place.peer("core", 0), place.peer("far", 0)
    copies = Loads(loads)
    weights = [copies.start(a, b) for a, b in ((qkv_h, wq), (up_h, wu), (down_h, wd), (proj_h, wp))]
    meet([core, far])

    unit, _ = normalize(state[...])
    normed[t] = (unit * norms[0:1] + norms[1:2]).astype(BF)
    n = TOK // CHUNKS
    part = [pl.ds(k * n, n) for k in range(CHUNKS)]
    across_in = [Link(sems, far) for _ in range(CHUNKS)]
    onward = [Link(sems, core) for _ in range(CHUNKS)]
    near = Link(sems, core)
    for k in range(CHUNKS):
        across_in[k].start(normed.at[t, part[k]], normed.at[t, part[k]])
    near.start(normed.at[t], normed.at[t])

    def project(i, _):
        j = t ^ i
        x, rows = normed[j], rows_of(j)
        for c in range(3):
            y = dot(x, wq[c])
            for h in range(2):
                z = y[:, h * 128 : (h + 1) * 128]
                if c < 2:
                    z = turned(z, table, rows, 1)
                if c == 0:
                    z = z * (HEAD_DIM ** -0.5)
                joined[c, rows, pl.ds(h * 128, 128)] = z.astype(BF)
        for m in range(4):
            cols = pl.ds(m * 256, 256)
            u = dot(x, wu[:, cols]) + norms[3:4, cols]
            a, s = gelu_and_slope(u)
            active[j, :, cols] = a.astype(BF)
            slope[j, :, cols] = s.astype(BF)
        return 0

    weights[0].wait()
    weights[1].wait()
    lax.fori_loop(0, 1, project, 0)
    near.arrived(normed.at[t ^ 1])
    lax.fori_loop(1, 2, project, 0)
    for k in range(CHUNKS):
        got = normed.at[t ^ 2, part[k]]
        across_in[k].arrived(got)
        onward[k].start(got, got)
    lax.fori_loop(2, 3, project, 0)
    for k in range(CHUNKS):
        onward[k].arrived(normed.at[t ^ 3, part[k]])
    lax.fori_loop(3, 4, project, 0)
    weights[2].wait()
    weights[3].wait()
    copies.open = []
    outward = [
        copies.start(a, b)
        for a, b in ((normed, normed_h), (joined, joined_h), (active, active_h), (slope, slope_h))
    ]

    query, keys, values = joined.at[0], joined.at[1], joined.at[2]

    def output(j):
        x, y = attended[rows_of(j)], active[j]
        for m in range(2):
            cols = pl.ds(m * 512, 512)
            partial[j, :, cols] = (dot(x, wp[:, cols]) + dot(y, wd[:, cols])).astype(BF)

    marks[...] = jnp.zeros_like(marks)
    for r in range(4):
        pl.when(yh != r // 2)(
            functools.partial(attend, r, query, keys, values, begin, attended, marks, lse)
        )
    to_core, to_far, back = Link(sems, core), Link(sems, far), Link(sems, core)
    output(t ^ 3)
    to_core.start(partial.at[t ^ 3], pair.at[0])
    output(t ^ 2)
    to_core.arrived(pair.at[0])
    pair[0] = (pair[0].astype(F32) + partial[t ^ 2].astype(F32)).astype(BF)
    to_far.start(pair.at[0], across)
    for r in range(4):
        pl.when(yh == r // 2)(
            functools.partial(attend, r, query, keys, values, begin, attended, marks, lse)
        )
    outward.append(copies.start(attended, attended_h))
    output(t ^ 1)
    back.start(partial.at[t ^ 1], pair.at[1])
    output(t)
    result[...] = state[...] + norms[2:3] + partial[t].astype(F32)
    back.arrived(pair.at[1])
    result[...] += pair[1].astype(F32)
    to_far.arrived(across)
    result[...] += across[...].astype(F32)
    for link in across_in + onward + [near, to_core, to_far, back]:
        link.sent()
    copies.finish()


def forward_layer(state, norms, table, begin, qkv, up, down, proj):
    vm, anywhere = pl.BlockSpec(memory_space=pltpu.VMEM), pl.BlockSpec(memory_space=pl.ANY)
    number = 2 * CHUNKS + 4
    wide = (4, TOK, 1024)
    S = jax.ShapeDtypeStruct
    return pl.pallas_call(
        forward_kernel,
        out_shape=[
            S((TOK, 1024), F32), S((8, 1024), F32), S(wide, BF), S((3, 1024, 256), BF),
            S((1024, 256), BF), S(wide, BF), S(wide, BF),
        ],
        in_specs=[vm] * 4 + [anywhere] * 4,
        out_specs=[vm] * 2 + [anywhere] * 5,
        scratch_shapes=[
            pltpu.VMEM((3, 1024, 256), BF), pltpu.VMEM((1024, 1024), BF),
            pltpu.VMEM((1024, 1024), BF), pltpu.VMEM((256, 1024), BF),
            pltpu.VMEM(wide, BF), pltpu.VMEM((3, 1024, 256), BF), pltpu.VMEM((1024, 256), BF),
            pltpu.VMEM(wide, BF), pltpu.VMEM(wide, BF), pltpu.VMEM(wide, BF),
            pltpu.VMEM((2, TOK, 1024), BF), pltpu.VMEM((TOK, 1024), BF),
            pltpu.VMEM((TOK, 128), F32),
            pltpu.SemaphoreType.DMA((9,)),
            pltpu.SemaphoreType.DMA((number,)), pltpu.SemaphoreType.DMA((number,)),
        ],
        compiler_params=pltpu.CompilerParams(
            collective_id=4, has_side_effects=True, vmem_limit_bytes=56 * 2**20
        ),
        name="forward_layer",
    )(state, norms, table, begin, qkv, up, down, proj)


def spread_rows(sems, place, whole, core, far):
    t = place.t
    n = TOK // CHUNKS
    part = [pl.ds(k * n, n) for k in range(CHUNKS)]
    across = [Link(sems, far) for _ in range(CHUNKS)]
    onward = [Link(sems, core) for _ in range(CHUNKS)]
    near = Link(sems, core)
    for k in range(CHUNKS):
        across[k].start(whole.at[t, part[k]], whole.at[t, part[k]])
    near.start(whole.at[t], whole.at[t])

    def near_here():
        near.arrived(whole.at[t ^ 1])

    def far_here():
        for k in range(CHUNKS):
            got = whole.at[t ^ 2, part[k]]
            across[k].arrived(got)
            onward[k].start(got, got)

    def both_here():
        for k in range(CHUNKS):
            onward[k].arrived(whole.at[t ^ 3, part[k]])

    def sent():
        for link in across + onward + [near]:
            link.sent()

    return near_here, far_here, both_here, sent


def attend_back(query, keys, values, grad_out, begin, lse, delta, grad_query, grad_joined, table):
    def pair(g, _):
        lanes = pl.ds(pl.multiple_of(g * 128, 128), 128)
        for block in range(4):
            start, size = block * TOK, 1024 - block * TOK
            here, on = pl.ds(start, TOK), pl.ds(start, size)
            k, v = keys[here, lanes], values[here, lanes]
            q, d = query[on, lanes], grad_out[on, lanes]
            row = lax.broadcasted_iota(jnp.int32, (TOK, size), 0) + start
            column = lax.broadcasted_iota(jnp.int32, (TOK, size), 1) + start
            allowed = (row >= begin[:, on]) & (row <= column)
            lane = lax.broadcasted_iota(jnp.int32, (TOK, 128), 1)
            by_value, by_key, by_query = [], [], None
            for half in range(2):
                head = pl.ds(2 * g + half, 1)
                mine = (lane // 64) == half
                kh, vh = [jnp.where(mine, part, jnp.zeros_like(part)) for part in (k, v)]
                scores = jnp.where(allowed, dot_cols(kh, q), -1e30)
                probs = jnp.exp(scores - lse[head, on])
                grad_scores = (probs * (dot_cols(vh, d) - delta[head, on])).astype(BF)
                by_value.append(dot(probs.astype(BF), d))
                by_key.append(dot(grad_scores, q))
                back = dot_rows(grad_scores, kh)
                by_query = back if by_query is None else by_query + back
            if block == 0:
                grad_query[on, lanes] = by_query
            else:
                grad_query[on, lanes] += by_query
            both = jnp.where(lane < 64, by_key[0], by_key[1])
            grad_joined[1, here, lanes] = turned(both, table, here, -1).astype(BF)
            grad_joined[2, here, lanes] = jnp.where(lane < 64, by_value[0], by_value[1]).astype(BF)
        return 0

    lax.fori_loop(0, 2, pair, 0)


def backward_kernel(
    grad, state, norms, table, begin, lse,
    qkv_h, up_h, down_h, proj_h, normed_h, joined_h, attended_h, active_h, slope_h,
    grad_state, sums, dqkv_h, dup_h, ddown_h, dproj_h,
    wq, wu, wd, wp, normed, joined, attended, active, slope,
    whole, grad_up, grad_att, delta, grad_query, grad_joined, dqkv, dup, ddown, dproj,
    partial, pair, across, total,
    loads, sends, recvs,
):
    place = Place()
    sems = Sems(sends, recvs)
    t = place.t
    core, far = place.peer("core", 0), place.peer("far", 0)
    copies = Loads(loads)
    ready = [
        copies.start(a, b)
        for a, b in (
            (down_h, wd), (slope_h, slope), (proj_h, wp), (attended_h, attended), (joined_h, joined),
            (up_h, wu), (qkv_h, wq), (active_h, active), (normed_h, normed),
        )
    ]
    meet([core, far])
    whole[t] = grad[...].astype(BF)
    near_here, far_here, both_here, sent = spread_rows(sems, place, whole, core, far)
    sums[...] = jnp.zeros_like(sums)
    sums[2:3] = jnp.sum(grad[...], axis=0, keepdims=True)
    for copy in ready[:4]:
        copy.wait()
    head = lax.broadcasted_iota(jnp.int32, (8, 256), 0)
    member = jnp.where(lax.broadcasted_iota(jnp.int32, (8, 256), 1) // 64 == head, 1.0, 0.0).astype(BF)

    def enter(i, _):
        j = t ^ i
        g, rows = whole[j], rows_of(j)
        for m in range(4):
            cols = pl.ds(m * 256, 256)
            back = dot_cols(g, wd[cols]) * slope[rows, cols].astype(F32)
            low = back.astype(BF)
            grad_up[rows, cols] = low
            sums[3:4, cols] += jnp.sum(low.astype(F32), axis=0, keepdims=True)
        d = dot_cols(g, wp[...]).astype(BF)
        grad_att[rows] = d
        both = d.astype(F32) * attended[rows].astype(F32)
        high = both.astype(BF)
        rest = (both - high.astype(F32)).astype(BF)
        delta[:, rows] = dot_cols(member, high) + dot_cols(member, rest)
        return 0

    lax.fori_loop(0, 1, enter, 0)
    near_here()
    lax.fori_loop(1, 2, enter, 0)
    far_here()
    lax.fori_loop(2, 3, enter, 0)
    both_here()
    lax.fori_loop(3, 4, enter, 0)
    ready[4].wait()
    attend_back(
        joined.at[0], joined.at[1], joined.at[2], grad_att, begin, lse, delta,
        grad_query, grad_joined, table,
    )
    for copy in ready[5:]:
        copy.wait()
    copies.open = []

    def leave(j):
        rows = rows_of(j)
        for h in range(2):
            lanes = pl.ds(h * 128, 128)
            z = grad_query[rows, lanes] * (HEAD_DIM ** -0.5)
            grad_joined[0, rows, lanes] = turned(z, table, rows, -1).astype(BF)
        for m in range(4):
            cols = pl.ds(m * 256, 256)
            out = dot_cols(grad_up[rows], wu[cols])
            for c in range(3):
                out = out + dot_cols(grad_joined[c, rows], wq[c, cols])
            partial[j, :, cols] = out.astype(BF)

    to_core, to_far, back = Link(sems, core), Link(sems, far), Link(sems, core)
    leave(t ^ 3)
    to_core.start(partial.at[t ^ 3], pair.at[0])
    leave(t ^ 2)
    to_core.arrived(pair.at[0])
    pair[0] = (pair[0].astype(F32) + partial[t ^ 2].astype(F32)).astype(BF)
    to_far.start(pair.at[0], across)
    leave(t ^ 1)
    back.start(partial.at[t ^ 1], pair.at[1])
    leave(t)

    def weights_of(b, _):
        cols = pl.ds(pl.multiple_of(b * 256, 256), 256)
        left = active[:, cols].T
        for m in range(2):
            right = pl.ds(m * 512, 512)
            out = dot(left[:, :TOK], whole[0, :, right])
            for j in range(1, 4):
                out = out + dot(left[:, j * TOK : (j + 1) * TOK], whole[j, :, right])
            ddown[cols, right] = out.astype(BF)
        left = normed[:, cols].T
        for m in range(2):
            right = pl.ds(m * 512, 512)
            dup[cols, right] = dot(left, grad_up[:, right]).astype(BF)
        for c in range(3):
            dqkv[c, cols] = dot(left, grad_joined[c]).astype(BF)
        return 0

    lax.fori_loop(0, 4, weights_of, 0)
    left = attended[...].T
    halves = []
    for m in range(2):
        right = pl.ds(m * 512, 512)
        out = dot(left[:, :TOK], whole[0, :, right])
        for j in range(1, 4):
            out = out + dot(left[:, j * TOK : (j + 1) * TOK], whole[j, :, right])
        halves.append(out.reshape(32, 8, 512))
    dproj[...] = jnp.concatenate(halves, axis=1).astype(BF)
    for a, b in ((ddown, ddown_h), (dup, dup_h), (dqkv, dqkv_h), (dproj, dproj_h)):
        copies.start(a, b)

    back.arrived(pair.at[1])
    total[...] = partial[t].astype(F32) + pair[1].astype(F32)
    to_far.arrived(across)
    own = total[...] + across[...].astype(F32)
    unit, inverse = normalize(state[...])
    sums[0:1] = jnp.sum(own * unit, axis=0, keepdims=True)
    sums[1:2] = jnp.sum(own, axis=0, keepdims=True)
    scaled = own * norms[0:1]
    grad_state[...] = grad[...] + inverse * (
        scaled
        - jnp.mean(scaled, axis=-1, keepdims=True)
        - unit * jnp.mean(scaled * unit, axis=-1, keepdims=True)
    )
    sent()
    for link in (to_core, to_far, back):
        link.sent()
    copies.finish()


def backward_layer(grad, state, norms, table, begin, lse, weights, saved):
    vm, anywhere = pl.BlockSpec(memory_space=pltpu.VMEM), pl.BlockSpec(memory_space=pl.ANY)
    number = 2 * CHUNKS + 4
    S = jax.ShapeDtypeStruct
    wide, slim, three = (1024, 1024), (1024, 256), (3, 1024, 256)
    V = pltpu.VMEM
    return pl.pallas_call(
        backward_kernel,
        out_shape=[
            S((TOK, 1024), F32), S((8, 1024), F32), S(three, BF), S(wide, BF), S(wide, BF), S((32, 16, 512), BF),
        ],
        in_specs=[vm] * 6 + [anywhere] * 9,
        out_specs=[vm] * 2 + [anywhere] * 4,
        scratch_shapes=[
            V(three, BF), V(wide, BF), V(wide, BF), V((256, 1024), BF),
            V(wide, BF), V(three, BF), V(slim, BF), V(wide, BF), V(wide, BF),
            V((4, TOK, 1024), BF), V(wide, BF), V(slim, BF), V((8, 1024), F32), V(slim, F32), V(three, BF),
            V(three, BF), V(wide, BF), V(wide, BF), V((32, 16, 512), BF),
            V((4, TOK, 1024), BF), V((2, TOK, 1024), BF), V((TOK, 1024), BF), V((TOK, 1024), F32),
            pltpu.SemaphoreType.DMA((13,)),
            pltpu.SemaphoreType.DMA((number,)), pltpu.SemaphoreType.DMA((number,)),
        ],
        compiler_params=pltpu.CompilerParams(
            collective_id=5, has_side_effects=True, vmem_limit_bytes=60 * 2**20
        ),
        name="backward_layer",
    )(grad, state, norms, table, begin, lse, *weights, *saved)


def seq_positions(segments):
    count = segments.shape[0]
    index = jnp.arange(count, dtype=jnp.int32)
    first = jnp.concatenate([jnp.ones((1,), dtype=bool), segments[1:] != segments[:-1]])
    begin = lax.cummax(jnp.where(first, index, 0), axis=0)
    return index - begin


def rotary_tables(positions):
    half = ROT // 2
    freq = jnp.exp(jnp.arange(half, dtype=jnp.float32) * (-2.0 * math.log(10000.0) / ROT))
    angle = positions.astype(jnp.float32)[:, None] * freq[None, :]
    return jnp.cos(angle), jnp.sin(angle)


def rotation_table(cosine, sine):
    none = jnp.zeros_like(sine)
    one = jnp.ones((cosine.shape[0], 32), F32)
    zero = jnp.zeros_like(one)
    keep = jnp.concatenate([cosine, cosine, one], axis=1)
    ahead = jnp.concatenate([-sine, none, zero], axis=1)
    behind = jnp.concatenate([none, sine, zero], axis=1)
    return jnp.stack([jnp.concatenate([part, part], axis=1) for part in (keep, ahead, behind)])


def fold(rows):
    return jnp.concatenate([rows[..., :512], rows[..., 512:]], axis=-2)


def unfold(rows):
    return jnp.concatenate([rows[..., :8, :], rows[..., 8:, :]], axis=-1)


def local(
    tokens,
    segment_ids,
    norm_gain,
    norm_shift,
    qkv_weight,
    proj_weight,
    up_weight,
    hidden_bias,
    down_weight,
    final_bias,
    cotangent,
):
    layers = qkv_weight.shape[0]
    f32 = jnp.float32
    row = jnp.concatenate(
        [norm_gain.reshape(16), norm_shift.reshape(16), final_bias.reshape(16), hidden_bias.reshape(64)]
    ).astype(f32)
    small = jnp.broadcast_to(jnp.pad(row, (0, 16))[None], (8, 128))
    pieces = []
    proj_own = fold(proj_weight)
    for layer in range(layers):
        pieces += [
            (qkv_weight[layer], 1), (up_weight[layer], 0), (down_weight[layer], 0), (proj_own[layer], 0)
        ]
    table, *wholes = gather_weights(small, pieces)
    table = table.reshape(32, 8, 128)[:, :4]

    def features(start):
        return table[:, :, start : start + 16].reshape(128, 2, 8).transpose(1, 0, 2).reshape(2, 1024)

    gains, shifts, finals = features(0), features(16), features(32)
    t = lax.axis_index("tensor")
    mine = lax.dynamic_index_in_dim(table, t, axis=1, keepdims=False)
    hidden = mine[:, 48:112].reshape(32, 2, 32).transpose(1, 0, 2).reshape(2, 1024)
    weights = []
    for layer in range(layers):
        qkv, up, down, proj = wholes[4 * layer : 4 * layer + 4]
        weights.append(
            (
                qkv.reshape(3, 1024, 256),
                unfold(proj.reshape(32, 16, 512)).reshape(256, 1024),
                up.reshape(1024, 1024),
                hidden[layer],
                down.reshape(1024, 1024),
            )
        )
    positions = seq_positions(segment_ids)
    begin = jnp.arange(1024, dtype=jnp.int32) - positions
    table = rotation_table(*rotary_tables(positions))
    state = tokens.astype(F32)
    saved = []
    for layer in range(layers):
        qkv, proj, up, hid, down = weights[layer]
        norms = jnp.concatenate(
            [jnp.stack([gains[layer], shifts[layer], finals[layer], hid]), jnp.zeros((4, 1024), F32)]
        )
        outs = forward_layer(state, norms, table, begin[:, None], qkv, up, down, proj)
        saved.append((state, norms, outs[1], outs[2:], (qkv, up, down, proj)))
        state = outs[0]
    mixed = state.astype(BF)
    grad = cotangent.astype(F32)
    terms = [None] * layers
    for layer in reversed(range(layers)):
        before, norms, lse, kept, full = saved[layer]
        kept = [part.reshape(1024, 1024) if part.shape == (4, TOK, 1024) else part for part in kept]
        grad, *terms[layer] = backward_layer(grad, before, norms, table, begin[None], lse, full, kept)
    parts = []
    for layer in reversed(range(layers)):
        _, dqkv, dup, ddown, dproj = terms[layer]
        parts += [
            (ddown.reshape(2, 4, 4, 32, 1024), 0),
            (dup.reshape(2, 4, 4, 32, 1024), 0),
            (dproj.reshape(2, 4, 4, 16, 512), 0),
            (dqkv.reshape(3, 2, 4, 4, 32, 256), 1),
        ]

    def spread(member):
        both = jnp.stack([terms[layer][0][member] for layer in range(layers)])
        return both.reshape(2, 32, 4, 8).transpose(1, 2, 0, 3).reshape(32, 4, 16)

    hid = jnp.stack([terms[layer][0][3] for layer in range(layers)])
    hid = hid.reshape(2, 32, 32).transpose(1, 0, 2).reshape(32, 1, 64)
    hid = jnp.where(jnp.arange(4)[None, :, None] == t, hid, 0.0)
    sums = jnp.concatenate([spread(0), spread(1), spread(2), hid], axis=-1)
    sums = jnp.pad(sums, ((0, 0), (0, 4), (0, 16))).reshape(2, 4, 4, 8, 128)
    own_sums, *owned = scatter_grads(sums, parts)
    line = lax.dynamic_index_in_dim(own_sums, t, axis=0, keepdims=False)
    down, up, proj, qkv = [jnp.stack([owned[4 + k], owned[k]]) for k in range(4)]
    return (
        mixed,
        grad,
        line[0:16].reshape(2, 8),
        line[16:32].reshape(2, 8),
        qkv,
        unfold(proj),
        up,
        line[48:112].reshape(2, 32),
        down,
        line[32:48].reshape(2, 8),
    )


def solution(mesh):
    placed = (
        P(("dp", "tensor"), None),
        P("dp"),
        P(None, ("dp", "tensor")),
        P(None, ("dp", "tensor")),
        P(None, None, "dp", "tensor"),
        P(None, ("tensor", "dp"), None),
        P(None, "dp", "tensor"),
        P(None, ("tensor", "dp")),
        P(None, ("tensor", "dp"), None),
        P(None, ("dp", "tensor")),
        P(("dp", "tensor"), None),
    )
    return jax.shard_map(
        local,
        mesh=mesh,
        in_specs=placed,
        out_specs=(
            P(("dp", "tensor"), None),
            P(("dp", "tensor"), None),
            P(None, ("dp", "tensor")),
            P(None, ("dp", "tensor")),
            P(None, None, "dp", "tensor"),
            P(None, ("tensor", "dp"), None),
            P(None, "dp", "tensor"),
            P(None, ("tensor", "dp")),
            P(None, ("tensor", "dp"), None),
            P(None, ("dp", "tensor")),
        ),
        check_vma=False,
    )
```

```python
import functools
import math

import jax
import jax.numpy as jnp
from jax import lax
from jax.experimental import pallas as pl
from jax.experimental.pallas import tpu as pltpu
from jax.sharding import PartitionSpec as P

HEAD_DIM = 64
ROT = 32
MESH = pl.DeviceIdType.MESH
ALL = slice(None)


epsilon = 1e-05


class Place:
    def __init__(self):
        dp = lax.axis_index("dp")
        self.t = lax.axis_index("tensor")
        self.dp = dp
        self.at = {"y": dp // 16, "x": lax.rem(dp // 4, 4), "z": lax.rem(dp, 4)}

    def plus(self, axis, step):
        return lax.rem(self.at[axis] + (step % 4), 4)

    def peer(self, axis, step):
        if axis == "core":
            return (self.dp, self.t ^ 1)
        if axis == "far":
            return (self.dp, self.t ^ 2)
        if axis == "both":
            return (self.dp, self.t ^ 3)
        c = dict(self.at)
        c[axis] = 1 - c["y"] if axis == "y" else self.plus(axis, step)
        return ((c["y"] * 4 + c["x"]) * 4 + c["z"], self.t)


def meet(peers):
    barrier = pltpu.get_barrier_semaphore()
    for peer in peers:
        pl.semaphore_signal(barrier, inc=1, device_id=peer, device_id_type=MESH)
    pl.semaphore_wait(barrier, len(peers))


def ring_peers(place):
    return [place.peer(a, s) for a, s in (("x", 1), ("x", -1), ("z", 1), ("z", -1), ("y", 1))]


def second_peers(place):
    return [place.peer("x", 2), place.peer("z", 2)]


def tensor_peers(place):
    return [place.peer(a, 0) for a in ("core", "far", "both")]


class Sems:
    def __init__(self, send, recv):
        self.send, self.recv, self.used = send, recv, 0

    def take(self):
        self.used += 1
        return self.send.at[self.used - 1], self.recv.at[self.used - 1]


class Link:
    def __init__(self, sems, peer):
        self.send, self.recv = sems.take()
        self.peer = peer

    def copy(self, src, dst):
        return pltpu.make_async_remote_copy(
            src_ref=src, dst_ref=dst, send_sem=self.send, recv_sem=self.recv,
            device_id=self.peer, device_id_type=MESH,
        )

    def start(self, src, dst):
        self.out = self.copy(src, dst)
        self.out.start()

    def arrived(self, dst):
        self.copy(dst, dst).wait_recv()

    def sent(self):
        self.out.wait_send()


def paths_of(columns, both):
    half = columns // 2
    if both:
        return (("z", "x", pl.ds(0, half)), ("x", "z", pl.ds(half, half)))
    return (("z", "x", pl.ds(0, columns)),)


def region(ref, lead, where, cols):
    return ref.at[(ALL,) * lead + (where["y"], where["x"], where["z"], ALL, cols)]


class Gather:
    links = 17
    stages = 6

    def __init__(self, place, sems, own, full, lead, local_sem):
        self.place, self.own, self.full, self.lead, self.local_sem = place, own, full, lead, local_sem
        self.paths = paths_of(full.shape[-1], full.shape[-1] % 256 == 0)
        self.cross = Link(sems, place.peer("y", 1))
        self.rings = []
        for first, second, cols in self.paths:
            self.rings.append(
                [
                    [Link(sems, place.peer(axis, 1)), Link(sems, place.peer(axis, -1)),
                     Link(sems, place.peer(axis, 1)), Link(sems, place.peer(axis, -1))]
                    for axis in (first, second)
                ]
            )

    def _at(self, cols, **where):
        return region(self.full, self.lead, where, cols)

    def stage(self, number):
        place, everything = self.place, pl.ds(0, self.full.shape[-1])
        here = dict(place.at)
        if number == 0:
            mine = self._at(everything, **here)
            self.local = pltpu.make_async_copy(self.own, mine, self.local_sem)
            self.local.start()
            self.cross.start(self.own, mine)
            return
        if number == 1:
            self.local.wait()
            self.cross.arrived(self._at(everything, **{**here, "y": 1 - here["y"]}))
        for (first, second, cols), rings in zip(self.paths, self.rings):
            axis = first if number <= 2 else second
            other = here[second] if number <= 2 else ALL
            rest = second if number <= 2 else first
            ring = rings[0] if number <= 2 else rings[1]

            def at(y, step):
                index = here[axis] if step == 0 else place.plus(axis, step)
                return self._at(cols, **{"y": y, axis: index, rest: other})

            if number in (1, 3):
                if number == 3:
                    self._close(rings[0], first, second, cols, here[second])
                ring[0].start(at(ALL, 0), at(ALL, 0))
                ring[1].start(at(ALL, 0), at(ALL, 0))
            elif number in (2, 4):
                ring[0].arrived(at(ALL, -1))
                ring[2].start(at(0, -1), at(0, -1))
                ring[1].arrived(at(ALL, 1))
                ring[3].start(at(1, 1), at(1, 1))
            else:
                self._close(ring, axis, rest, cols, ALL)
        if number == 5:
            self.cross.sent()
            for rings in self.rings:
                for ring in rings:
                    for link in ring:
                        link.sent()

    def _close(self, ring, axis, rest, cols, other):
        opposite = self.place.plus(axis, 2)
        ring[2].arrived(self._at(cols, **{"y": 0, axis: opposite, rest: other}))
        ring[3].arrived(self._at(cols, **{"y": 1, axis: opposite, rest: other}))


class Reduce:
    stages = 6

    @staticmethod
    def links(columns):
        return 1 + 12 * len(paths_of(columns, columns % 256 == 0))

    @staticmethod
    def scratch(shape, dtype):
        *lead, _, _, _, rows, columns = shape
        lead = tuple(lead)
        shapes = []
        for _, _, cols in paths_of(columns, columns % 256 == 0):
            w = cols.size
            shapes += [pltpu.VMEM(lead + (2, 4, rows, w), dtype)]
            shapes += [pltpu.VMEM(lead + (2, 2, 4, rows, w), dtype)]
            shapes += [pltpu.VMEM(lead + (2, rows, w), dtype)]
            shapes += [pltpu.VMEM(lead + (2, 2, rows, w), dtype)]
        shapes += [pltpu.VMEM(lead + (2, rows, columns), jnp.float32)]
        shapes += [pltpu.VMEM(lead + (rows, columns), dtype)] * 2
        return shapes

    def __init__(self, place, sems, given, total, lead, scratch):
        self.place, self.given, self.total, self.lead = place, given, total, lead
        columns = given.shape[-1]
        self.dtype = given.dtype
        self.paths = paths_of(columns, columns % 256 == 0)
        self.cross = Link(sems, place.peer("y", 1))
        self.work = []
        for number, (first, second, cols) in enumerate(self.paths):
            ends = []
            for axis in (first, second):
                ends.append([Link(sems, place.peer(axis, s)) for s in (1, -1, 1, -1, 1, -1)])
            self.work.append((ends, scratch[4 * number : 4 * number + 4]))
        self.summed, self.leaving, self.coming = scratch[-3:]

    def _given(self, cols, **where):
        return region(self.given, self.lead, where, cols)

    def _pre(self, *index):
        return (ALL,) * self.lead + index

    def _add(self, into, *terms):
        total = terms[0][...].astype(jnp.float32)
        for term in terms[1:]:
            total = total + term[...].astype(jnp.float32)
        into[...] = total.astype(into.dtype)

    def _send(self, links, near, far, at):
        pre = self._pre
        links[0].start(at(0, 2), near.at[pre(0)])
        links[1].start(at(1, 2), near.at[pre(1)])
        links[2].start(at(1, 1), far.at[pre(0, 1)])
        links[3].start(at(0, -1), far.at[pre(1, 0)])

    def _pass(self, links, near, far, at):
        pre = self._pre
        for way, step in ((0, 1), (1, -1)):
            slot = near.at[pre(way)]
            links[way].arrived(slot)
            self._add(slot, slot, at(way, step))
            links[4 + way].start(slot, far.at[pre(way, way)])

    def _join(self, links, far):
        pre = self._pre
        links[2].arrived(far.at[pre(0, 1)])
        links[3].arrived(far.at[pre(1, 0)])
        links[4].arrived(far.at[pre(0, 0)])
        links[5].arrived(far.at[pre(1, 1)])

    def stage(self, number):
        place, pre = self.place, self._pre
        here = dict(place.at)
        for (first, second, cols), (ends, (near1, far1, near2, far2)) in zip(self.paths, self.work):

            def at1(y, step):
                index = here[first] if step == 0 else place.plus(first, step)
                return self._given(cols, **{"y": y, first: index, second: ALL})

            def at2(y, step):
                index = here[second] if step == 0 else place.plus(second, step)
                return far1.at[pre(0, y, index)]

            if number == 0:
                self._send(ends[0], near1, far1, at1)
            elif number == 1:
                self._pass(ends[0], near1, far1, at1)
            elif number == 2:
                self._join(ends[0], far1)
                for y in (0, 1):
                    slot = far1.at[pre(0, y)]
                    self._add(slot, slot, far1.at[pre(1, y)], at1(y, 0))
                self._send(ends[1], near2, far2, at2)
            elif number == 3:
                self._pass(ends[1], near2, far2, at2)
            elif number == 4:
                self._join(ends[1], far2)
                for y in (0, 1):
                    into = self.summed.at[pre(y, ALL, cols)]
                    self._add(into, at2(y, 0), far2.at[pre(0, y)], far2.at[pre(1, y)])
        if number == 4:
            self._add(self.leaving, self.summed.at[pre(1 - here["y"])])
            self.cross.start(self.leaving, self.coming)
        elif number == 5:
            self.cross.arrived(self.coming)
            self._add(self.total, self.summed.at[pre(here["y"])], self.coming)
            self.cross.sent()
            for ends, _ in self.work:
                for links in ends:
                    for link in links:
                        link.sent()


TOK = 256
CHUNKS = 4
BF = jnp.bfloat16
F32 = jnp.float32


def dot(left, right):
    return jnp.dot(left, right, preferred_element_type=F32)


def dot_cols(left, right):
    return lax.dot_general(left, right, (((1,), (1,)), ((), ())), preferred_element_type=F32)


def dot_rows(left, right):
    return lax.dot_general(left, right, (((0,), (0,)), ((), ())), preferred_element_type=F32)


def rows_of(block):
    return pl.ds(pl.multiple_of(block * TOK, TOK), TOK)


def iota(shape, dim):
    return lax.broadcasted_iota(jnp.int32, shape, dim)


def turned(z, table, rows, sign):
    ahead, behind = pltpu.roll(z, 112, 1), pltpu.roll(z, 16, 1)
    if sign > 0:
        return z * table[0, rows] + ahead * table[1, rows] + behind * table[2, rows]
    return z * table[0, rows] - ahead * table[1, rows] - behind * table[2, rows]


def gelu_and_slope(u):
    c, a = math.sqrt(2.0 / math.pi), 0.044715
    square = u * u
    t = jnp.tanh(c * u * (1.0 + a * square))
    half = 0.5 * (1.0 + t)
    return u * half, half + (0.5 * c) * u * (1.0 - t * t) * (1.0 + (3.0 * a) * square)


def normalize(x):
    center = x - jnp.mean(x, axis=-1, keepdims=True)
    inverse = lax.rsqrt(jnp.mean(center * center, axis=-1, keepdims=True) + epsilon)
    return center * inverse, inverse


class Loads:
    def __init__(self, sems):
        self.sems, self.used = sems, 0

    def start(self, src, dst):
        copy = pltpu.make_async_copy(src, dst, self.sems.at[self.used])
        self.used += 1
        copy.start()
        return copy


class Pump:
    def __init__(self):
        self.steps = []

    def add(self, jobs, first):
        for step in range(first, len(jobs) + max(job.stages for job in jobs)):
            row = [(job, step - number) for number, job in enumerate(jobs)]
            row = [(job, stage) for job, stage in reversed(row) if first <= stage < job.stages]
            if row:
                self.steps.append(row)

    def run(self, count):
        for _ in range(min(count, len(self.steps))):
            advance(self.steps.pop(0))

    def finish(self):
        self.run(len(self.steps))


def advance(row):
    for job, stage in row:
        job.stage(stage)


class QuickGather:
    links = 7

    def __init__(self, place, sems, full):
        self.place, self.full = place, full
        self.ends = {"y": [Link(sems, place.peer("y", 1))]}
        for axis in ("x", "z"):
            self.ends[axis] = [Link(sems, place.peer(axis, step)) for step in (1, 2, 3)]

    def _at(self, axis, step):
        here = self.place.at
        if axis == "y":
            return self.full.at[here["y"] if step == 0 else 1 - here["y"], here["x"], here["z"]]
        if axis == "x":
            return self.full.at[:, self.place.plus("x", step), here["z"]]
        return self.full.at[:, :, self.place.plus("z", step)]

    def begin(self, axis):
        for link in self.ends[axis]:
            link.start(self._at(axis, 0), self._at(axis, 0))

    def end(self, axis):
        for number, link in enumerate(self.ends[axis]):
            link.arrived(self._at(axis, -1 - number))

    def sent(self):
        for links in self.ends.values():
            for link in links:
                link.sent()


class QuickReduce:
    links = 7

    def __init__(self, place, sems, given, first, second, third, total):
        self.place, self.given, self.total = place, given, total
        self.first, self.second, self.third = first, second, third
        self.ends = {"y": [Link(sems, place.peer("y", 1))]}
        for axis in ("x", "z"):
            self.ends[axis] = [Link(sems, place.peer(axis, step)) for step in (1, 2, 3)]

    def begin(self, axis):
        place = self.place
        if axis == "y":
            self.ends["y"][0].start(self.second.at[3, 1 - place.at["y"]], self.third)
            return
        for number, link in enumerate(self.ends[axis]):
            if axis == "z":
                link.start(self.given.at[:, :, place.plus("z", number + 1)], self.first.at[number])
            else:
                link.start(self.first.at[3, :, place.plus("x", number + 1)], self.second.at[number])

    def end(self, axis):
        place = self.place
        if axis == "y":
            self.ends["y"][0].arrived(self.third)
            self.total[...] = self.second[3, place.at["y"]] + self.third[...]
            return
        into = self.first if axis == "z" else self.second
        total = self.given[:, :, place.at["z"]] if axis == "z" else self.first[3, :, place.at["x"]]
        for number, link in enumerate(self.ends[axis]):
            link.arrived(into.at[number])
            total = total + into[number]
        into[3] = total

    def sent(self):
        for links in self.ends.values():
            for link in links:
                link.sent()


class Spread:
    links = 2 * CHUNKS + 1

    def __init__(self, place, sems, own, whole):
        self.t, self.own, self.whole = place.t, own, whole
        core, far = place.peer("core", 0), place.peer("far", 0)
        self.across = [Link(sems, far) for _ in range(CHUNKS)]
        self.onward = [Link(sems, core) for _ in range(CHUNKS)]
        self.near = Link(sems, core)
        n = TOK // CHUNKS
        self.part = [pl.ds(k * n, n) for k in range(CHUNKS)]

    def start(self):
        for k, part in enumerate(self.part):
            self.across[k].start(self.own.at[part], self.whole.at[self.t, part])
        self.near.start(self.own, self.whole.at[self.t])

    def near_here(self):
        self.near.arrived(self.whole.at[self.t ^ 1])

    def far_here(self):
        for k, part in enumerate(self.part):
            got = self.whole.at[self.t ^ 2, part]
            self.across[k].arrived(got)
            self.onward[k].start(got, got)

    def both_here(self):
        for k, part in enumerate(self.part):
            self.onward[k].arrived(self.whole.at[self.t ^ 3, part])

    def sent(self):
        for link in self.across + self.onward + [self.near]:
            link.sent()


class Collect:
    links = 3

    def __init__(self, place, sems, partial, pair, across):
        self.t, self.partial, self.pair, self.across = place.t, partial, pair, across
        self.to_core, self.back = Link(sems, place.peer("core", 0)), Link(sems, place.peer("core", 0))
        self.to_far = Link(sems, place.peer("far", 0))

    def first(self):
        self.to_core.start(self.partial.at[self.t ^ 3], self.pair.at[0])

    def second(self):
        self.to_core.arrived(self.pair.at[0])
        self.pair[0] = (self.pair[0].astype(F32) + self.partial[self.t ^ 2].astype(F32)).astype(BF)
        self.to_far.start(self.pair.at[0], self.across)

    def third(self):
        self.back.start(self.partial.at[self.t ^ 1], self.pair.at[1])

    def chip_sum(self):
        self.back.arrived(self.pair.at[1])
        return self.partial[self.t].astype(F32) + self.pair[1].astype(F32)

    def far_sum(self):
        self.to_far.arrived(self.across)
        return self.across[...].astype(F32)

    def sent(self):
        for link in (self.to_core, self.to_far, self.back):
            link.sent()


def feature_owner(shape):
    row, column = iota(shape, 0), iota(shape, 1)
    return ((column >> 3) == (row >> 3) * 4 + (row & 7)) & ((row & 7) < 4)


def hidden_owner(shape, t):
    row, column = iota(shape, 0), iota(shape, 1)
    return ((column >> 5) == (row >> 3)) & ((row & 7) == t)


def lane_of(layer, member, column):
    if member < 3:
        return member * 16 + layer * 8 + (column & 7)
    return 48 + layer * 32 + (column & 31)


def unpack_small(small_table, norms, layer, t):
    packed = small_table[...].reshape(256, 128).astype(BF)
    lane, column = iota((128, 1024), 0), iota((128, 1024), 1)
    shape = (256, 1024)
    for member in range(4):
        mine = feature_owner(shape) if member < 3 else hidden_owner(shape, t)
        pick = jnp.where(lane == lane_of(layer, member, column), 1.0, 0.0).astype(BF)
        row = jnp.sum(jnp.where(mine, dot(packed, pick), 0.0), axis=0, keepdims=True)
        norms[layer, member : member + 1] = row


def pack_small(sums, small_table, layers, t, fresh):
    lane, column = iota((1024, 128), 1), iota((1024, 128), 0)
    shape = (256, 1024)
    total = jnp.zeros((256, 128), F32)
    for layer in layers:
        for member in range(4):
            mine = feature_owner(shape) if member < 3 else hidden_owner(shape, t)
            pick = jnp.where(lane == lane_of(layer, member, column), 1.0, 0.0).astype(BF)
            rest = jnp.where(mine, sums[layer, member : member + 1], 0.0)
            for _ in range(3):
                part = rest.astype(BF)
                total = total + dot(part, pick)
                rest = rest - part.astype(F32)
    total = total.reshape(2, 4, 4, 8, 128)
    small_table[...] = total if fresh else small_table[...] + total


def attend(r, query, keys, values, begin, attended, marks, lse):
    width = (r + 1) * TOK
    rows = pl.ds(r * TOK, TOK)
    row = iota((TOK, width), 0) + r * TOK
    column = iota((TOK, width), 1)
    allowed = (column >= begin[rows]) & (column <= row)
    lane = iota((TOK, 128), 1)

    def pair(g, _):
        lanes = pl.ds(pl.multiple_of(g * 128, 128), 128)
        q, k, v = query[rows, lanes], keys[:width, lanes], values[:width, lanes]
        outs = []
        for half in range(2):
            mine = jnp.where((lane // 64) == half, q, jnp.zeros_like(q))
            scores = jnp.where(allowed, dot_cols(mine, k), -1e30)
            peak = jnp.max(scores, axis=-1, keepdims=True)
            weights = jnp.exp(scores - peak)
            total = jnp.sum(weights, axis=-1, keepdims=True)
            outs.append(dot(weights.astype(BF), v) * (1.0 / total))
            marks[...] = jnp.where(lane == 2 * g + half, peak + jnp.log(total), marks[...])
        attended[rows, lanes] = jnp.where(lane < 64, outs[0], outs[1]).astype(BF)
        return 0

    lax.fori_loop(0, 2, pair, 0)
    lse[:, rows] = marks[...].T[:8]


def forward_kernel(
    tokens, cotangent, small, begin, table, proj_own, qkv_own, up_own, down_own,
    mixed, middle, norms, lse, cot_h, normed_h, joined_h, attended_h, active_h, slope_h, wq_h, wu_h, wd_h, wp_h,
    four, small_table, folded, wq, wu, wd, wf, wp,
    normed, joined, attended, active, slope, partial, pair, across, marks, last,
    loads, sends, recvs,
):
    place = Place()
    sems = Sems(sends, recvs)
    t = place.t
    yh = t // 2
    copies = Loads(loads)
    both = proj_own[...].astype(F32)
    folded[...] = jnp.concatenate([both[..., :512], both[..., 512:]], axis=1).astype(BF)
    meet(ring_peers(place) + second_peers(place) + tensor_peers(place))

    links = [Link(sems, peer) for peer in tensor_peers(place)]
    four[t] = small[...]
    for link in links:
        link.start(small, four.at[t])
    jobs = {}
    for layer in range(2):
        for name, own, full, lead in (
            ("qkv", qkv_own, wq, 1), ("up", up_own, wu, 0), ("down", down_own, wd, 0), ("proj", folded, wf, 0)
        ):
            number = 4 * layer + len(jobs) % 4
            jobs[name, layer] = Gather(place, sems, own.at[layer], full.at[layer], lead, loads.at[number])
    copies.used = 9
    early = [jobs[name, 0] for name in ("qkv", "up", "down", "proj")]
    for job in early:
        job.stage(0)
    for link, flip in zip(links, (1, 2, 3)):
        link.arrived(four.at[t ^ flip])
    row = iota((8, 128), 0)
    packed = jnp.zeros((8, 128), F32)
    for other in range(4):
        packed = jnp.where(row == other, four[other], packed)
    small_table[place.at["y"], place.at["x"], place.at["z"]] = packed
    shared = QuickGather(place, sems, small_table)
    late = [jobs[name, 1] for name in ("qkv", "up", "down", "proj")]
    pump = Pump()
    pump.add(early, 1)
    pump.steps.append([(job, 0) for job in late])
    pump.add(late, 1)
    shared.begin("y")
    pump.run(1)
    shared.end("y")
    shared.begin("x")
    pump.run(1)
    shared.end("x")
    shared.begin("z")
    pump.run(1)
    shared.end("z")
    unpack_small(small_table, norms, 0, t)
    turn_cot = Spread(place, sems, cotangent, cot_h)
    open_copies = [copies.start(cotangent, cot_h.at[t])]
    spreads, collects = [], []

    for layer in range(2):
        state = tokens[...].astype(F32) if layer == 0 else middle[...]
        result = middle if layer == 0 else last
        norm = norms.at[layer]
        here, act, slp = normed.at[layer], active.at[layer], slope.at[layer]
        query, keys, values = [joined.at[layer, c] for c in range(3)]
        att = attended.at[layer]
        unit, _ = normalize(state)
        here[t] = (unit * norm[0:1] + norm[1:2]).astype(BF)
        spread = Spread(place, sems, here.at[t], here)
        spread.start()
        spreads.append(spread)
        if layer == 0:
            pump.run(1)
            unpack_small(small_table, norms, 1, t)
            pump.run(1)

        def project(i, _, layer=layer, here=here):
            j = t ^ i
            x, rows = here[j], rows_of(j)
            for c in range(3):
                y = dot(x, wq[layer, c].reshape(1024, 256))
                for h in range(2):
                    z = y[:, h * 128 : (h + 1) * 128]
                    if c < 2:
                        z = turned(z, table, rows, 1)
                    if c == 0:
                        z = z * (HEAD_DIM ** -0.5)
                    joined[layer, c, rows, pl.ds(h * 128, 128)] = z.astype(BF)
            return 0

        def expand(i, _, layer=layer, here=here, act=act, slp=slp, norm=norm):
            j = t ^ i
            x, rows = here[j], rows_of(j)
            for m in range(4):
                cols = pl.ds(m * 256, 256)
                u = dot(x, wu[layer, :, :, :, :, cols].reshape(1024, 256)) + norm[3:4, cols]
                a, s = gelu_and_slope(u)
                act[rows, cols] = a.astype(BF)
                slp[rows, cols] = s.astype(BF)
            return 0

        def attention(far, layer=layer, att=att, query=query, keys=keys, values=values):
            for r in range(4):
                wanted = (yh != r // 2) if far else (yh == r // 2)
                pl.when(wanted)(
                    functools.partial(attend, r, query, keys, values, begin, att, marks, lse.at[layer])
                )

        def keep(*pairs, layer=layer):
            for a, b in pairs:
                open_copies.append(copies.start(a, b.at[layer]))

        marks[...] = jnp.zeros_like(marks)
        lax.fori_loop(0, 1, project, 0)
        if layer == 1:
            lax.fori_loop(0, 1, expand, 0)
        spread.near_here()
        lax.fori_loop(1, 2, project, 0)
        if layer == 1:
            lax.fori_loop(1, 2, expand, 0)
        pump.run(1)
        spread.far_here()
        if layer == 0:
            turn_cot.start()
        lax.fori_loop(2, 3, project, 0)
        if layer == 1:
            lax.fori_loop(2, 3, expand, 0)
        spread.both_here()
        lax.fori_loop(3, 4, project, 0)
        if layer == 1:
            lax.fori_loop(3, 4, expand, 0)
        keep((here, normed_h), (joined.at[layer], joined_h), (wq.at[layer], wq_h))
        pump.run(1)
        attention(True)
        if layer == 0:
            pump.run(2)
            attention(False)
            pump.run(1)
            lax.fori_loop(0, 2, expand, 0)
            turn_cot.near_here()
            turn_cot.far_here()
            pump.run(1)
            lax.fori_loop(2, 4, expand, 0)
            pump.run(1)
        else:
            pump.finish()
        keep((act, active_h), (slp, slope_h), (wu.at[layer], wu_h))
        full = wf[layer].reshape(32, 16, 512).astype(F32)
        wp[layer] = jnp.concatenate([full[:, :8], full[:, 8:]], axis=2).reshape(256, 1024).astype(BF)
        collect = Collect(place, sems, partial.at[layer], pair.at[layer], across.at[layer])
        collects.append(collect)

        def output(j, layer=layer, att=att, act=act):
            x, y = att[rows_of(j)], act[rows_of(j)]
            for m in range(2):
                cols = pl.ds(m * 512, 512)
                out = dot(x, wp[layer, :, cols]) + dot(y, wd[layer, :, :, :, :, cols].reshape(1024, 512))
                partial[layer, j, :, cols] = out.astype(BF)

        output(t ^ 3)
        collect.first()
        output(t ^ 2)
        collect.second()
        pump.run(1)
        if layer == 1:
            attention(False)
        keep((att, attended_h), (wd.at[layer], wd_h), (wp.at[layer], wp_h))
        output(t ^ 1)
        collect.third()
        output(t)
        pump.run(1)
        result[...] = state + norm[2:3] + collect.chip_sum()
        pump.run(1)
        result[...] += collect.far_sum()
    mixed[...] = last[...].astype(BF)
    turn_cot.both_here()
    shared.sent()
    for link in links:
        link.sent()
    for part in spreads + collects + [turn_cot]:
        part.sent()
    for copy in open_copies:
        copy.wait()


def forward(tokens, cotangent, small, begin, table, proj, qkv, up, down):
    vm, anywhere = pl.BlockSpec(memory_space=pltpu.VMEM), pl.BlockSpec(memory_space=pl.ANY)
    number = 3 + QuickGather.links + 8 * Gather.links + 3 * Spread.links + 2 * Collect.links
    S, V = jax.ShapeDtypeStruct, pltpu.VMEM
    ring = (2, 4, 4)
    q, w, p = (2, 3) + ring + (32, 256), (2,) + ring + (32, 1024), (2,) + ring + (16, 512)
    group, square, slim = (2, 4, TOK, 1024), (2, 1024, 1024), (2, 1024, 256)
    joined = (2, 3, 1024, 256)
    return pl.pallas_call(
        forward_kernel,
        out_shape=[
            S((TOK, 1024), BF), S((TOK, 1024), F32), S((2, 8, 1024), F32), S((2, 8, 1024), F32),
            S((4, TOK, 1024), BF), S(group, BF), S(joined, BF), S(slim, BF), S(square, BF), S(square, BF),
            S(q, BF), S(w, BF), S(w, BF), S((2, 256, 1024), BF),
        ],
        in_specs=[vm] * 6 + [anywhere] * 3,
        out_specs=[vm] * 4 + [anywhere] * 10,
        scratch_shapes=[
            V((4, 8, 128), F32), V(ring + (8, 128), F32), V((2, 16, 512), BF),
            V(q, BF), V(w, BF), V(w, BF), V(p, BF), V((2, 256, 1024), BF),
            V(group, BF), V(joined, BF), V(slim, BF), V(square, BF), V(square, BF),
            V(group, BF), V((2, 2, TOK, 1024), BF), V((2, TOK, 1024), BF), V((TOK, 128), F32), V((TOK, 1024), F32),
            pltpu.SemaphoreType.DMA((28,)),
            pltpu.SemaphoreType.DMA((number,)), pltpu.SemaphoreType.DMA((number,)),
        ],
        compiler_params=pltpu.CompilerParams(
            collective_id=0, has_side_effects=True, vmem_limit_bytes=62 * 2**20
        ),
        name="forward_layers",
    )(tokens, cotangent, small, begin, table, proj, qkv, up, down)


def attend_back(g, query, keys, values, grad_out, begin, lse, delta, grad_query, grad_joined, table):
    lanes = pl.ds(g * 128, 128)
    for block in range(4):
        start, size = block * TOK, 1024 - block * TOK
        here, on = pl.ds(start, TOK), pl.ds(start, size)
        k, v = keys[here, lanes], values[here, lanes]
        q, d = query[on, lanes], grad_out[on, lanes]
        row = iota((TOK, size), 0) + start
        column = iota((TOK, size), 1) + start
        allowed = (row >= begin[:, on]) & (row <= column)
        lane = iota((TOK, 128), 1)
        by_value, by_key, by_query = [], [], None
        for half in range(2):
            head = pl.ds(2 * g + half, 1)
            mine = (lane // 64) == half
            kh, vh = [jnp.where(mine, part, jnp.zeros_like(part)) for part in (k, v)]
            scores = jnp.where(allowed, dot_cols(kh, q), -1e30)
            probs = jnp.exp(scores - lse[head, on])
            grad_scores = (probs * (dot_cols(vh, d) - delta[head, on])).astype(BF)
            by_value.append(dot(probs.astype(BF), d))
            by_key.append(dot(grad_scores, q))
            back = dot_rows(grad_scores, kh)
            by_query = back if by_query is None else by_query + back
        if block == 0:
            grad_query[on, lanes] = by_query
        else:
            grad_query[on, lanes] += by_query
        both = jnp.where(lane < 64, by_key[0], by_key[1])
        grad_joined[1, here, lanes] = turned(both, table, here, -1).astype(BF)
        grad_joined[2, here, lanes] = jnp.where(lane < 64, by_value[0], by_value[1]).astype(BF)


def grouped(b, *rest):
    return (b // 2, pl.ds(2 * (b % 2), 2)) + rest


def backward_kernel(
    tokens, middle, cotangent, norms, table, begin, lse,
    cot_h, normed_h, joined_h, attended_h, active_h, slope_h, wq_h, wu_h, wd_h, wp_h,
    token_grad, own_sums, total_q, total_p, total_u, total_d,
    wq, wu, wd, wp, normed, joined, attended, active, slope,
    whole, grad_up, grad_att, delta, grad_query, grad_joined, dqkv, dup, ddown, dproj,
    partial, pair, across, sums, small_table, tile, four, first, second, third,
    loads, clear, sends, recvs, *scratch,
):
    place = Place()
    sems = Sems(sends, recvs)
    t = place.t
    copies = Loads(loads)
    sources = {
        "whole": (cot_h, whole.at[1]), "wd": (wd_h, wd), "slope": (slope_h, slope), "wp": (wp_h, wp),
        "attended": (attended_h, attended), "active": (active_h, active), "normed": (normed_h, normed),
        "joined": (joined_h, joined), "wu": (wu_h, wu), "wq": (wq_h, wq),
    }
    fetched = {}

    def fetch(layer, *names):
        for name in names:
            src, dst = sources[name]
            fetched[layer, name] = copies.start(src if name == "whole" else src.at[layer], dst)

    def need(layer, *names):
        for name in names:
            fetched[layer, name].wait()

    fetch(1, *sources)
    meet(ring_peers(place) + second_peers(place) + tensor_peers(place))
    head = iota((8, 256), 0)
    member = jnp.where(iota((8, 256), 1) // 64 == head, 1.0, 0.0).astype(BF)
    closing = []
    holders = [scratch[11 * number : 11 * number + 11] for number in range(4)]

    def reduce_job(number, given, total, lead):
        return Reduce(place, sems, given, total, lead, holders[number])

    def wide_jobs(layer):
        return [reduce_job(0, ddown, total_d.at[layer], 0), reduce_job(1, dup, total_u.at[layer], 0)]

    def slim_jobs(layer):
        return [reduce_job(3, dqkv, total_q.at[layer], 1), reduce_job(2, dproj, total_p.at[layer], 0)]

    def run(jobs, stage):
        for job in jobs:
            job.stage(stage)

    ring = ring_peers(place)

    def hand_over(number):
        for peer in ring:
            pl.semaphore_signal(clear.at[number], inc=1, device_id=peer, device_id_type=MESH)

    def take_over(number):
        pl.semaphore_wait(clear.at[number], len(ring))

    for layer in (1, 0):
        grad = cotangent[...].astype(F32) if layer == 1 else token_grad[...]
        state = middle[...] if layer == 1 else tokens[...].astype(F32)
        rows_in = whole.at[layer]
        small = sums.at[layer]
        small[...] = jnp.zeros((8, 1024), F32)
        small[2:3] = jnp.sum(grad, axis=0, keepdims=True)
        if layer == 0:
            rows_in[t] = grad.astype(BF)
            spread = Spread(place, sems, rows_in.at[t], rows_in)
            spread.start()
            closing.append(spread)
        else:
            need(1, "whole")
        need(layer, "wd", "slope", "wp", "attended")

        def enter(i, _, rows_in=rows_in, small=small):
            j = t ^ i
            g, rows = rows_in[j], rows_of(j)
            for m in range(4):
                cols = pl.ds(m * 256, 256)
                low = (dot_cols(g, wd[cols]) * slope[rows, cols].astype(F32)).astype(BF)
                grad_up[rows, cols] = low
                small[3:4, cols] += jnp.sum(low.astype(F32), axis=0, keepdims=True)
            d = dot_cols(g, wp[...]).astype(BF)
            grad_att[rows] = d
            both = d.astype(F32) * attended[rows].astype(F32)
            high = both.astype(BF)
            rest = (both - high.astype(F32)).astype(BF)
            delta[:, rows] = dot_cols(member, high) + dot_cols(member, rest)
            return 0

        if layer == 1:
            lax.fori_loop(0, 4, enter, 0)
        else:
            lax.fori_loop(0, 1, enter, 0)
            spread.near_here()
            lax.fori_loop(1, 2, enter, 0)
            spread.far_here()
            run(wide, 4)
            lax.fori_loop(2, 3, enter, 0)
            spread.both_here()
            run(slim, 2)
            lax.fori_loop(3, 4, enter, 0)
            run(wide, 5)
            hand_over(0)
        need(layer, "active", "normed")

        def wide_grads(b, _, rows_in=rows_in):
            cols = pl.ds(pl.multiple_of(b * 256, 256), 256)
            left = active[:, cols].T
            for m in range(2):
                right = pl.ds(m * 512, 512)
                out = dot(left[:, :TOK], rows_in[0, :, right])
                for j in range(1, 4):
                    out = out + dot(left[:, j * TOK : (j + 1) * TOK], rows_in[j, :, right])
                ddown[grouped(b, slice(None), slice(None), right)] = out.astype(BF).reshape(2, 4, 32, 512)
            left = normed[:, cols].T
            for m in range(2):
                right = pl.ds(m * 512, 512)
                out = dot(left, grad_up[:, right]).astype(BF)
                dup[grouped(b, slice(None), slice(None), right)] = out.reshape(2, 4, 32, 512)
            return 0

        lax.fori_loop(0, 4, wide_grads, 0)
        if layer == 0:
            run(slim, 3)
            take_over(0)
        wide = wide_jobs(layer)
        run(wide, 0)
        need(layer, "joined")
        for g in range(2):
            attend_back(
                g, joined.at[0], joined.at[1], joined.at[2], grad_att, begin, lse.at[layer], delta,
                grad_query, grad_joined, table,
            )
            if layer == 0:
                run(slim, 4 + g)
        if layer == 0:
            hand_over(1)
        run(wide, 1)
        need(layer, "wu", "wq")
        if layer == 1:
            fetch(0, "wd", "slope", "wp", "active", "joined")

        def turn_back(j, _):
            rows = rows_of(j)
            for h in range(2):
                lanes = pl.ds(h * 128, 128)
                z = grad_query[rows, lanes] * (HEAD_DIM ** -0.5)
                grad_joined[0, rows, lanes] = turned(z, table, rows, -1).astype(BF)
            return 0

        lax.fori_loop(0, 4, turn_back, 0)

        def leave(j):
            rows = rows_of(j)
            for m in range(4):
                cols = pl.ds(m * 256, 256)
                out = dot_cols(grad_up[rows], wu[cols])
                for c in range(3):
                    out = out + dot_cols(grad_joined[c, rows], wq[c, cols])
                partial[j, :, cols] = out.astype(BF)

        def slim_grads(b, _):
            left = normed[:, pl.ds(pl.multiple_of(b * 256, 256), 256)].T
            for c in range(3):
                dqkv[(c,) + grouped(b)] = dot(left, grad_joined[c]).astype(BF).reshape(2, 4, 32, 256)
            return 0

        def slim_all():
            lax.fori_loop(0, 4, slim_grads, 0)
            left = attended[...].T
            halves = []
            for m in range(2):
                right = pl.ds(m * 512, 512)
                out = dot(left[:, :TOK], rows_in[0, :, right])
                for j in range(1, 4):
                    out = out + dot(left[:, j * TOK : (j + 1) * TOK], rows_in[j, :, right])
                halves.append(out.reshape(32, 8, 512))
            dproj[...] = jnp.concatenate(halves, axis=1).astype(BF).reshape(2, 4, 4, 16, 512)
        if layer == 0:
            slim_all()
            slim = slim_jobs(layer)
            take_over(1)
            run(slim, 0)
        collect = Collect(place, sems, partial, pair.at[layer], across.at[layer])
        leave(t ^ 3)
        collect.first()
        leave(t ^ 2)
        collect.second()
        leave(t ^ 1)
        collect.third()
        leave(t)

        if layer == 1:
            slim_all()
            fetch(0, "attended", "normed", "wu", "wq")
            slim = slim_jobs(layer)
            run(slim, 0)
        run(wide, 2)
        if layer == 0:
            pack_small(sums, small_table, (1,), t, True)

        own = collect.chip_sum()
        if layer == 0:
            run(wide, 3)
            run(slim, 1)
        own = own + collect.far_sum()
        collect.sent()
        unit, inverse = normalize(state)
        small[0:1] = jnp.sum(own * unit, axis=0, keepdims=True)
        small[1:2] = jnp.sum(own, axis=0, keepdims=True)
        scaled = own * norms[layer, 0:1]
        after = grad + inverse * (
            scaled
            - jnp.mean(scaled, axis=-1, keepdims=True)
            - unit * jnp.mean(scaled * unit, axis=-1, keepdims=True)
        )
        token_grad[...] = after
        if layer == 1:
            run(wide, 3)
            run(slim, 1)

    pack_small(sums, small_table, (0,), t, False)
    quick = QuickReduce(place, sems, small_table, first, second, third, tile)
    quick.begin("z")
    run(wide, 4)
    quick.end("z")
    quick.begin("x")
    run(slim, 2)
    quick.end("x")
    quick.begin("y")
    run(wide, 5)
    quick.end("y")
    links = [Link(sems, peer) for peer in tensor_peers(place)]
    for number, link in enumerate(links):
        link.start(tile, four.at[number])
    whole_tile = tile[...]
    for number, link in enumerate(links):
        link.arrived(four.at[number])
        whole_tile = whole_tile + four[number]
    own_sums[...] = whole_tile
    run(slim, 3)
    run(slim, 4)
    run(slim, 5)
    quick.sent()
    for part in closing:
        part.sent()
    for link in links:
        link.sent()


def backward(tokens, middle, cotangent, norms, table, begin, lse, saved):
    vm, anywhere = pl.BlockSpec(memory_space=pltpu.VMEM), pl.BlockSpec(memory_space=pl.ANY)
    S, V = jax.ShapeDtypeStruct, pltpu.VMEM
    ring = (2, 4, 4)
    square, slim, three = (1024, 1024), (1024, 256), (3, 1024, 256)
    group = (4, TOK, 1024)
    big, q, p = ring + (32, 1024), (3,) + ring + (32, 256), ring + (16, 512)
    number = 3 + QuickReduce.links + Spread.links + 2 * Collect.links
    number += 2 * (2 * Reduce.links(1024) + Reduce.links(256) + Reduce.links(512))
    reduce_scratch = []
    for shape in (big, big, p, q):
        reduce_scratch += Reduce.scratch(shape, BF)
    return pl.pallas_call(
        backward_kernel,
        out_shape=[
            S((TOK, 1024), F32), S((8, 128), F32), S((2, 3, 32, 256), F32), S((2, 16, 512), F32),
            S((2, 32, 1024), F32), S((2, 32, 1024), F32),
        ],
        in_specs=[vm] * 7 + [anywhere] * 10,
        out_specs=[vm] * 6,
        scratch_shapes=[
            V(three, BF), V(square, BF), V(square, BF), V((256, 1024), BF),
            V(square, BF), V(three, BF), V(slim, BF), V(square, BF), V(square, BF),
            V((2,) + group, BF), V(square, BF), V(slim, BF), V((8, 1024), F32), V(slim, F32), V(three, BF),
            V(q, BF), V(big, BF), V(big, BF), V(p, BF),
            V(group, BF), V((2, 2, TOK, 1024), BF), V((2, TOK, 1024), BF), V((2, 8, 1024), F32),
            V(ring + (8, 128), F32), V((8, 128), F32), V((3, 8, 128), F32),
            V((4, 2, 4, 8, 128), F32), V((4, 2, 8, 128), F32), V((8, 128), F32),
            pltpu.SemaphoreType.DMA((20,)), pltpu.SemaphoreType.REGULAR((2,)),
            pltpu.SemaphoreType.DMA((number,)), pltpu.SemaphoreType.DMA((number,)),
        ]
        + reduce_scratch,
        compiler_params=pltpu.CompilerParams(
            collective_id=1, has_side_effects=True, vmem_limit_bytes=62 * 2**20
        ),
        name="backward_layers",
    )(tokens, middle, cotangent, norms, table, begin, lse, *saved)


def seq_positions(segments):
    count = segments.shape[0]
    index = jnp.arange(count, dtype=jnp.int32)
    first = jnp.concatenate([jnp.ones((1,), dtype=bool), segments[1:] != segments[:-1]])
    begin = lax.cummax(jnp.where(first, index, 0), axis=0)
    return index - begin


def rotary_tables(positions):
    half = ROT // 2
    freq = jnp.exp(jnp.arange(half, dtype=jnp.float32) * (-2.0 * math.log(10000.0) / ROT))
    angle = positions.astype(jnp.float32)[:, None] * freq[None, :]
    return jnp.cos(angle), jnp.sin(angle)


def rotation_table(cosine, sine):
    none = jnp.zeros_like(sine)
    one = jnp.ones((cosine.shape[0], 32), F32)
    zero = jnp.zeros_like(one)
    keep = jnp.concatenate([cosine, cosine, one], axis=1)
    ahead = jnp.concatenate([-sine, none, zero], axis=1)
    behind = jnp.concatenate([none, sine, zero], axis=1)
    return jnp.stack([jnp.concatenate([part, part], axis=1) for part in (keep, ahead, behind)])


def local(
    tokens,
    segment_ids,
    norm_gain,
    norm_shift,
    qkv_weight,
    proj_weight,
    up_weight,
    hidden_bias,
    down_weight,
    final_bias,
    cotangent,
):
    row = jnp.concatenate(
        [norm_gain.reshape(16), norm_shift.reshape(16), final_bias.reshape(16), hidden_bias.reshape(64)]
    ).astype(F32)
    small = jnp.broadcast_to(jnp.pad(row, (0, 16))[None], (8, 128))
    positions = seq_positions(segment_ids)
    begin = jnp.arange(1024, dtype=jnp.int32) - positions
    table = rotation_table(*rotary_tables(positions))
    mixed, middle, norms, lse, cot, *saved = forward(
        tokens, cotangent, small, begin[:, None], table, proj_weight, qkv_weight, up_weight, down_weight
    )
    saved[5] = saved[5].reshape(2, 3, 1024, 256)
    saved[6] = saved[6].reshape(2, 1024, 1024)
    saved[7] = saved[7].reshape(2, 1024, 1024)
    saved[0] = saved[0].reshape(2, 1024, 1024)
    token_grad, sums, qkv, proj, up, down = backward(
        tokens, middle, cotangent, norms, table, begin[None], lse, [cot] + saved
    )
    line = lax.dynamic_index_in_dim(sums, lax.axis_index("tensor"), axis=0, keepdims=False)
    return (
        mixed,
        token_grad,
        line[0:16].reshape(2, 8),
        line[16:32].reshape(2, 8),
        qkv,
        jnp.concatenate([proj[:, :8], proj[:, 8:]], axis=2),
        up,
        line[48:112].reshape(2, 32),
        down,
        line[32:48].reshape(2, 8),
    )


def solution(mesh):
    placed = (
        P(("dp", "tensor"), None),
        P("dp"),
        P(None, ("dp", "tensor")),
        P(None, ("dp", "tensor")),
        P(None, None, "dp", "tensor"),
        P(None, ("tensor", "dp"), None),
        P(None, "dp", "tensor"),
        P(None, ("tensor", "dp")),
        P(None, ("tensor", "dp"), None),
        P(None, ("dp", "tensor")),
        P(("dp", "tensor"), None),
    )
    return jax.shard_map(
        local,
        mesh=mesh,
        in_specs=placed,
        out_specs=(
            P(("dp", "tensor"), None),
            P(("dp", "tensor"), None),
            P(None, ("dp", "tensor")),
            P(None, ("dp", "tensor")),
            P(None, None, "dp", "tensor"),
            P(None, ("tensor", "dp"), None),
            P(None, "dp", "tensor"),
            P(None, ("tensor", "dp")),
            P(None, ("tensor", "dp"), None),
            P(None, ("dp", "tensor")),
        ),
        check_vma=False,
    )
```

```python
import functools
import math

import jax
import jax.numpy as jnp
import numpy as np
from jax import lax
from jax.experimental import pallas as pl
from jax.experimental.pallas import tpu as pltpu
from jax.sharding import PartitionSpec as P

HEAD_DIM = 64
ROT = 32
MESH = pl.DeviceIdType.MESH
ALL = slice(None)


epsilon = 1e-05


class Place:
    def __init__(self):
        dp = lax.axis_index("dp")
        self.t = lax.axis_index("tensor")
        self.dp = dp
        self.at = {"y": dp // 16, "x": lax.rem(dp // 4, 4), "z": lax.rem(dp, 4)}

    def plus(self, axis, step):
        return lax.rem(self.at[axis] + (step % 4), 4)

    def peer(self, axis, step):
        if axis == "core":
            return (self.dp, self.t ^ 1)
        if axis == "far":
            return (self.dp, self.t ^ 2)
        if axis == "both":
            return (self.dp, self.t ^ 3)
        c = dict(self.at)
        c[axis] = 1 - c["y"] if axis == "y" else self.plus(axis, step)
        return ((c["y"] * 4 + c["x"]) * 4 + c["z"], self.t)


def meet(peers):
    barrier = pltpu.get_barrier_semaphore()
    for peer in peers:
        pl.semaphore_signal(barrier, inc=1, device_id=peer, device_id_type=MESH)
    pl.semaphore_wait(barrier, len(peers))


def ring_peers(place):
    return [place.peer(a, s) for a, s in (("x", 1), ("x", -1), ("z", 1), ("z", -1), ("y", 1))]


def second_peers(place):
    return [place.peer("x", 2), place.peer("z", 2)]


def tensor_peers(place):
    return [place.peer(a, 0) for a in ("core", "far", "both")]


class Sems:
    def __init__(self, send, recv):
        self.send, self.recv, self.used = send, recv, 0

    def take(self):
        self.used += 1
        return self.send.at[self.used - 1], self.recv.at[self.used - 1]


class Link:
    def __init__(self, sems, peer):
        self.send, self.recv = sems.take()
        self.peer = peer

    def copy(self, src, dst):
        return pltpu.make_async_remote_copy(
            src_ref=src, dst_ref=dst, send_sem=self.send, recv_sem=self.recv,
            device_id=self.peer, device_id_type=MESH,
        )

    def start(self, src, dst):
        self.out = self.copy(src, dst)
        self.out.start()

    def arrived(self, dst):
        self.copy(dst, dst).wait_recv()

    def sent(self):
        self.out.wait_send()


def paths_of(columns, both):
    half = columns // 2
    if both:
        return (("z", "x", pl.ds(0, half)), ("x", "z", pl.ds(half, half)))
    return (("z", "x", pl.ds(0, columns)),)


def region(ref, lead, where, cols):
    return ref.at[(ALL,) * lead + (where["y"], where["x"], where["z"], ALL, cols)]


class Gather:
    links = 17
    stages = 6

    def __init__(self, place, sems, own, full, lead, local_sem):
        self.place, self.own, self.full, self.lead, self.local_sem = place, own, full, lead, local_sem
        self.paths = paths_of(full.shape[-1], full.shape[-1] % 256 == 0)
        self.cross = Link(sems, place.peer("y", 1))
        self.rings = []
        for first, second, cols in self.paths:
            self.rings.append(
                [
                    [Link(sems, place.peer(axis, 1)), Link(sems, place.peer(axis, -1)),
                     Link(sems, place.peer(axis, 1)), Link(sems, place.peer(axis, -1))]
                    for axis in (first, second)
                ]
            )

    def _at(self, cols, **where):
        return region(self.full, self.lead, where, cols)

    def stage(self, number):
        place, everything = self.place, pl.ds(0, self.full.shape[-1])
        here = dict(place.at)
        if number == 0:
            mine = self._at(everything, **here)
            self.local = pltpu.make_async_copy(self.own, mine, self.local_sem)
            self.local.start()
            self.cross.start(self.own, mine)
            return
        if number == 1:
            self.local.wait()
            self.cross.arrived(self._at(everything, **{**here, "y": 1 - here["y"]}))
        for (first, second, cols), rings in zip(self.paths, self.rings):
            axis = first if number <= 2 else second
            other = here[second] if number <= 2 else ALL
            rest = second if number <= 2 else first
            ring = rings[0] if number <= 2 else rings[1]

            def at(y, step):
                index = here[axis] if step == 0 else place.plus(axis, step)
                return self._at(cols, **{"y": y, axis: index, rest: other})

            if number in (1, 3):
                if number == 3:
                    self._close(rings[0], first, second, cols, here[second])
                ring[0].start(at(ALL, 0), at(ALL, 0))
                ring[1].start(at(ALL, 0), at(ALL, 0))
            elif number in (2, 4):
                ring[0].arrived(at(ALL, -1))
                ring[2].start(at(0, -1), at(0, -1))
                ring[1].arrived(at(ALL, 1))
                ring[3].start(at(1, 1), at(1, 1))
            else:
                self._close(ring, axis, rest, cols, ALL)
        if number == 5:
            self.cross.sent()
            for rings in self.rings:
                for ring in rings:
                    for link in ring:
                        link.sent()

    def _close(self, ring, axis, rest, cols, other):
        opposite = self.place.plus(axis, 2)
        ring[2].arrived(self._at(cols, **{"y": 0, axis: opposite, rest: other}))
        ring[3].arrived(self._at(cols, **{"y": 1, axis: opposite, rest: other}))


class Reduce:
    stages = 6

    @staticmethod
    def links(columns):
        return 1 + 12 * len(paths_of(columns, columns % 256 == 0))

    @staticmethod
    def scratch(shape, dtype):
        *lead, _, _, _, rows, columns = shape
        lead = tuple(lead)
        shapes = []
        for _, _, cols in paths_of(columns, columns % 256 == 0):
            w = cols.size
            shapes += [pltpu.VMEM(lead + (2, 4, rows, w), dtype)]
            shapes += [pltpu.VMEM(lead + (2, 2, 4, rows, w), dtype)]
            shapes += [pltpu.VMEM(lead + (2, rows, w), dtype)]
            shapes += [pltpu.VMEM(lead + (2, 2, rows, w), dtype)]
        shapes += [pltpu.VMEM(lead + (2, rows, columns), jnp.float32)]
        shapes += [pltpu.VMEM(lead + (rows, columns), dtype)] * 2
        return shapes

    def __init__(self, place, sems, given, total, lead, scratch):
        self.place, self.given, self.total, self.lead = place, given, total, lead
        columns = given.shape[-1]
        self.dtype = given.dtype
        self.paths = paths_of(columns, columns % 256 == 0)
        self.cross = Link(sems, place.peer("y", 1))
        self.work = []
        for number, (first, second, cols) in enumerate(self.paths):
            ends = []
            for axis in (first, second):
                ends.append([Link(sems, place.peer(axis, s)) for s in (1, -1, 1, -1, 1, -1)])
            self.work.append((ends, scratch[4 * number : 4 * number + 4]))
        self.summed, self.leaving, self.coming = scratch[-3:]

    def _given(self, cols, **where):
        return region(self.given, self.lead, where, cols)

    def _pre(self, *index):
        return (ALL,) * self.lead + index

    def _add(self, into, *terms):
        total = terms[0][...].astype(jnp.float32)
        for term in terms[1:]:
            total = total + term[...].astype(jnp.float32)
        into[...] = total.astype(into.dtype)

    def _send(self, links, near, far, at):
        pre = self._pre
        links[0].start(at(0, 2), near.at[pre(0)])
        links[1].start(at(1, 2), near.at[pre(1)])
        links[2].start(at(1, 1), far.at[pre(0, 1)])
        links[3].start(at(0, -1), far.at[pre(1, 0)])

    def _pass(self, links, near, far, at):
        pre = self._pre
        for way, step in ((0, 1), (1, -1)):
            slot = near.at[pre(way)]
            links[way].arrived(slot)
            self._add(slot, slot, at(way, step))
            links[4 + way].start(slot, far.at[pre(way, way)])

    def _join(self, links, far):
        pre = self._pre
        links[2].arrived(far.at[pre(0, 1)])
        links[3].arrived(far.at[pre(1, 0)])
        links[4].arrived(far.at[pre(0, 0)])
        links[5].arrived(far.at[pre(1, 1)])

    def stage(self, number):
        place, pre = self.place, self._pre
        here = dict(place.at)
        for (first, second, cols), (ends, (near1, far1, near2, far2)) in zip(self.paths, self.work):

            def at1(y, step):
                index = here[first] if step == 0 else place.plus(first, step)
                return self._given(cols, **{"y": y, first: index, second: ALL})

            def at2(y, step):
                index = here[second] if step == 0 else place.plus(second, step)
                return far1.at[pre(0, y, index)]

            if number == 0:
                self._send(ends[0], near1, far1, at1)
            elif number == 1:
                self._pass(ends[0], near1, far1, at1)
            elif number == 2:
                self._join(ends[0], far1)
                for y in (0, 1):
                    slot = far1.at[pre(0, y)]
                    self._add(slot, slot, far1.at[pre(1, y)], at1(y, 0))
                self._send(ends[1], near2, far2, at2)
            elif number == 3:
                self._pass(ends[1], near2, far2, at2)
            elif number == 4:
                self._join(ends[1], far2)
                for y in (0, 1):
                    into = self.summed.at[pre(y, ALL, cols)]
                    self._add(into, at2(y, 0), far2.at[pre(0, y)], far2.at[pre(1, y)])
        if number == 4:
            self._add(self.leaving, self.summed.at[pre(1 - here["y"])])
            self.cross.start(self.leaving, self.coming)
        elif number == 5:
            self.cross.arrived(self.coming)
            self._add(self.total, self.summed.at[pre(here["y"])], self.coming)
            self.cross.sent()
            for ends, _ in self.work:
                for links in ends:
                    for link in links:
                        link.sent()


TOK = 256
CHUNKS = 4
BF = jnp.bfloat16
F32 = jnp.float32


def dot(left, right):
    return jnp.dot(left, right, preferred_element_type=F32)


def dot_cols(left, right):
    return lax.dot_general(left, right, (((1,), (1,)), ((), ())), preferred_element_type=F32)


def dot_rows(left, right):
    return lax.dot_general(left, right, (((0,), (0,)), ((), ())), preferred_element_type=F32)


def rows_of(block):
    return pl.ds(pl.multiple_of(block * TOK, TOK), TOK)


def iota(shape, dim):
    return lax.broadcasted_iota(jnp.int32, shape, dim)


def turned(z, table, rows, sign):
    ahead, behind = pltpu.roll(z, 112, 1), pltpu.roll(z, 16, 1)
    if sign > 0:
        return z * table[0, rows] + ahead * table[1, rows] + behind * table[2, rows]
    return z * table[0, rows] - ahead * table[1, rows] - behind * table[2, rows]


def gelu_and_slope(u):
    c, a = math.sqrt(2.0 / math.pi), 0.044715
    square = u * u
    t = jnp.tanh(c * u * (1.0 + a * square))
    half = 0.5 * (1.0 + t)
    return u * half, half + (0.5 * c) * u * (1.0 - t * t) * (1.0 + (3.0 * a) * square)


def normalize(x):
    center = x - jnp.mean(x, axis=-1, keepdims=True)
    inverse = lax.rsqrt(jnp.mean(center * center, axis=-1, keepdims=True) + epsilon)
    return center * inverse, inverse


class Loads:
    def __init__(self, sems):
        self.sems, self.used = sems, 0

    def start(self, src, dst):
        copy = pltpu.make_async_copy(src, dst, self.sems.at[self.used])
        self.used += 1
        copy.start()
        return copy


class QuickGather:
    links = 7

    def __init__(self, place, sems, full):
        self.place, self.full = place, full
        self.ends = {"y": [Link(sems, place.peer("y", 1))]}
        for axis in ("x", "z"):
            self.ends[axis] = [Link(sems, place.peer(axis, step)) for step in (1, 2, 3)]

    def _at(self, axis, step):
        here = self.place.at
        if axis == "y":
            return self.full.at[here["y"] if step == 0 else 1 - here["y"], here["x"], here["z"]]
        if axis == "x":
            return self.full.at[:, self.place.plus("x", step), here["z"]]
        return self.full.at[:, :, self.place.plus("z", step)]

    def begin(self, axis):
        for link in self.ends[axis]:
            link.start(self._at(axis, 0), self._at(axis, 0))

    def end(self, axis):
        for number, link in enumerate(self.ends[axis]):
            link.arrived(self._at(axis, -1 - number))

    def sent(self):
        for links in self.ends.values():
            for link in links:
                link.sent()


class QuickReduce:
    links = 7

    def __init__(self, place, sems, given, first, second, third, total):
        self.place, self.given, self.total = place, given, total
        self.first, self.second, self.third = first, second, third
        self.ends = {"y": [Link(sems, place.peer("y", 1))]}
        for axis in ("x", "z"):
            self.ends[axis] = [Link(sems, place.peer(axis, step)) for step in (1, 2, 3)]

    def begin(self, axis):
        place = self.place
        if axis == "y":
            self.ends["y"][0].start(self.second.at[3, 1 - place.at["y"]], self.third)
            return
        for number, link in enumerate(self.ends[axis]):
            if axis == "z":
                link.start(self.given.at[:, :, place.plus("z", number + 1)], self.first.at[number])
            else:
                link.start(self.first.at[3, :, place.plus("x", number + 1)], self.second.at[number])

    def end(self, axis):
        place = self.place
        if axis == "y":
            self.ends["y"][0].arrived(self.third)
            self.total[...] = self.second[3, place.at["y"]] + self.third[...]
            return
        into = self.first if axis == "z" else self.second
        total = self.given[:, :, place.at["z"]] if axis == "z" else self.first[3, :, place.at["x"]]
        for number, link in enumerate(self.ends[axis]):
            link.arrived(into.at[number])
            total = total + into[number]
        into[3] = total

    def sent(self):
        for links in self.ends.values():
            for link in links:
                link.sent()


class Spread:
    links = 2 * CHUNKS + 1

    def __init__(self, place, sems, own, whole):
        self.t, self.own, self.whole = place.t, own, whole
        core, far = place.peer("core", 0), place.peer("far", 0)
        self.across = [Link(sems, far) for _ in range(CHUNKS)]
        self.onward = [Link(sems, core) for _ in range(CHUNKS)]
        self.near = Link(sems, core)
        n = TOK // CHUNKS
        self.part = [pl.ds(k * n, n) for k in range(CHUNKS)]

    def start(self):
        for k, part in enumerate(self.part):
            self.across[k].start(self.own.at[part], self.whole.at[self.t, part])
        self.near.start(self.own, self.whole.at[self.t])

    def near_here(self):
        self.near.arrived(self.whole.at[self.t ^ 1])

    def far_here(self):
        for k, part in enumerate(self.part):
            got = self.whole.at[self.t ^ 2, part]
            self.across[k].arrived(got)
            self.onward[k].start(got, got)

    def both_here(self):
        for k, part in enumerate(self.part):
            self.onward[k].arrived(self.whole.at[self.t ^ 3, part])

    def sent(self):
        for link in self.across + self.onward + [self.near]:
            link.sent()


class Collect:
    links = 3

    def __init__(self, place, sems, partial, pair, across):
        self.t, self.partial, self.pair, self.across = place.t, partial, pair, across
        self.to_core, self.back = Link(sems, place.peer("core", 0)), Link(sems, place.peer("core", 0))
        self.to_far = Link(sems, place.peer("far", 0))

    def first(self):
        self.to_core.start(self.partial.at[self.t ^ 3], self.pair.at[0])

    def second(self):
        self.to_core.arrived(self.pair.at[0])
        self.pair[0] = (self.pair[0].astype(F32) + self.partial[self.t ^ 2].astype(F32)).astype(BF)
        self.to_far.start(self.pair.at[0], self.across)

    def third(self):
        self.back.start(self.partial.at[self.t ^ 1], self.pair.at[1])

    def chip_sum(self):
        self.back.arrived(self.pair.at[1])
        return self.partial[self.t].astype(F32) + self.pair[1].astype(F32)

    def far_sum(self):
        self.to_far.arrived(self.across)
        return self.across[...].astype(F32)

    def sent(self):
        for link in (self.to_core, self.to_far, self.back):
            link.sent()


def feature_owner(shape):
    row, column = iota(shape, 0), iota(shape, 1)
    return ((column >> 3) == (row >> 3) * 4 + (row & 7)) & ((row & 7) < 4)


def hidden_owner(shape, t):
    row, column = iota(shape, 0), iota(shape, 1)
    return ((column >> 5) == (row >> 3)) & ((row & 7) == t)


def lane_of(layer, member, column):
    if member < 3:
        return member * 16 + layer * 8 + (column & 7)
    return 48 + layer * 32 + (column & 31)


def unpack_small(small_table, norms, layer, t, members=range(4)):
    packed = small_table[...].reshape(256, 128).astype(BF)
    lane, column = iota((128, 1024), 0), iota((128, 1024), 1)
    shape = (256, 1024)
    for member in members:
        mine = feature_owner(shape) if member < 3 else hidden_owner(shape, t)
        pick = jnp.where(lane == lane_of(layer, member, column), 1.0, 0.0).astype(BF)
        row = jnp.sum(jnp.where(mine, dot(packed, pick), 0.0), axis=0, keepdims=True)
        norms[layer, member : member + 1] = row


def pack_small(sums, small_table, rows, t, fresh):
    lane, column = iota((1024, 128), 1), iota((1024, 128), 0)
    shape = (256, 1024)
    total = jnp.zeros((256, 128), F32)
    for layer, member in rows:
        mine = feature_owner(shape) if member < 3 else hidden_owner(shape, t)
        pick = jnp.where(lane == lane_of(layer, member, column), 1.0, 0.0).astype(BF)
        rest = jnp.where(mine, sums[layer, member : member + 1], 0.0)
        for _ in range(3):
            part = rest.astype(BF)
            total = total + dot(part, pick)
            rest = rest - part.astype(F32)
    total = total.reshape(2, 4, 4, 8, 128)
    small_table[...] = total if fresh else small_table[...] + total


def places(segments, beginning, begin_row, frequency, table):
    ids = segments[...].astype(F32)
    down = jnp.broadcast_to(ids, (128, 1024)).T
    row_total = jnp.zeros((1, 1024), F32)
    lane = iota((TOK, 128), 1) & 63
    for block in range(4):
        rows = pl.ds(block * TOK, TOK)
        column = down[block * TOK : (block + 1) * TOK, :1]
        row_total = row_total + jnp.sum(jnp.where(column < ids, 1.0, 0.0), axis=0, keepdims=True)
        first = jnp.sum(jnp.where(ids < column, 1.0, 0.0), axis=1, keepdims=True)
        beginning[rows] = first.astype(jnp.int32)
        index = (iota((TOK, 128), 0) + block * TOK).astype(F32)
        angle = (index - first) * frequency[...]
        cosine, sine = jnp.cos(angle), jnp.sin(angle)
        table[0, rows] = jnp.where(lane < 32, cosine, 1.0)
        table[1, rows] = jnp.where(lane < 16, -sine, 0.0)
        table[2, rows] = jnp.where((lane >= 16) & (lane < 32), sine, 0.0)
    begin_row[...] = row_total.astype(jnp.int32)


def attend(r, query, keys, values, begin, attended, marks, lse):
    width = (r + 1) * TOK
    rows = pl.ds(r * TOK, TOK)
    row = iota((TOK, width), 0) + r * TOK
    column = iota((TOK, width), 1)
    allowed = (column >= begin[rows]) & (column <= row)
    lane = iota((TOK, 128), 1)

    def pair(g, _):
        lanes = pl.ds(pl.multiple_of(g * 128, 128), 128)
        q, k, v = query[rows, lanes], keys[:width, lanes], values[:width, lanes]
        outs = []
        for half in range(2):
            mine = jnp.where((lane // 64) == half, q, jnp.zeros_like(q))
            scores = jnp.where(allowed, dot_cols(mine, k), -1e30)
            peak = jnp.max(scores, axis=-1, keepdims=True)
            weights = jnp.exp(scores - peak)
            total = jnp.sum(weights, axis=-1, keepdims=True)
            outs.append(dot(weights.astype(BF), v) * (1.0 / total))
            marks[...] = jnp.where(lane == 2 * g + half, peak + jnp.log(total), marks[...])
        attended[rows, lanes] = jnp.where(lane < 64, outs[0], outs[1]).astype(BF)
        return 0

    lax.fori_loop(0, 2, pair, 0)
    lse[:, rows] = marks[...].T[:8]


def forward_kernel(
    tokens, small, segments, frequency, proj_own, cotangent, qkv_own, up_own, down_own,
    mixed, middle, norms, lse, begin_row, table, cot_h, normed_h, joined_h, attended_h, active_h, slope_h, wq_h, wu_h, wd_h, wp_h,
    four, small_table, folded, wq, wu, wd, wf, wp,
    normed, joined, attended, active, slope, partial, pair, across, marks, last, begin,
    loads, sends, recvs,
):
    place = Place()
    sems = Sems(sends, recvs)
    t = place.t
    yh = t // 2
    copies = Loads(loads)
    both = proj_own[...].astype(F32)
    folded[...] = jnp.concatenate([both[..., :512], both[..., 512:]], axis=1).astype(BF)
    meet(ring_peers(place) + second_peers(place) + tensor_peers(place))

    links = [Link(sems, peer) for peer in tensor_peers(place)]
    four[t] = small[...]
    for link in links:
        link.start(small, four.at[t])
    jobs = {}
    for layer in range(2):
        for name, own, full, lead in (
            ("qkv", qkv_own, wq, 1), ("up", up_own, wu, 0), ("down", down_own, wd, 0), ("proj", folded, wf, 0)
        ):
            number = 4 * layer + len(jobs) % 4
            jobs[name, layer] = Gather(place, sems, own.at[layer], full.at[layer], lead, loads.at[number])
    copies.used = 9
    early = [jobs[name, 0] for name in ("qkv", "up", "down", "proj")]
    late = [jobs[name, 1] for name in ("qkv", "up", "down", "proj")]

    def go(layer, *stages):
        for stage in stages:
            job = jobs[{"q": "qkv", "u": "up", "d": "down", "p": "proj"}[stage[0]], layer]
            job.stage(int(stage[1]))

    go(0, "q0", "u0", "d0", "p0")
    for link, flip in zip(links, (1, 2, 3)):
        link.arrived(four.at[t ^ flip])
    row = iota((8, 128), 0)
    packed = jnp.zeros((8, 128), F32)
    for other in range(4):
        packed = jnp.where(row == other, four[other], packed)
    small_table[place.at["y"], place.at["x"], place.at["z"]] = packed
    shared = QuickGather(place, sems, small_table)
    shared.begin("y")
    go(0, "q1")
    shared.end("y")
    shared.begin("x")
    go(0, "u1")
    shared.end("x")
    shared.begin("z")
    go(0, "q2", "d1", "p1")
    shared.end("z")
    unpack_small(small_table, norms, 0, t, (0, 1))
    turn_cot = Spread(place, sems, cotangent, cot_h)
    open_copies = []
    spreads, collects = [], []

    for layer in range(2):
        state = tokens[...].astype(F32) if layer == 0 else middle[...]
        result = middle if layer == 0 else last
        norm = norms.at[layer]
        here, act, slp = normed.at[layer], active.at[layer], slope.at[layer]
        query, keys, values = [joined.at[layer, c] for c in range(3)]
        att = attended.at[layer]
        unit, _ = normalize(state)
        here[t] = (unit * norm[0:1] + norm[1:2]).astype(BF)
        spread = Spread(place, sems, here.at[t], here)
        spread.start()
        spreads.append(spread)
        if layer == 0:
            go(0, "u2", "q3")
            unpack_small(small_table, norms, 0, t, (2, 3))
            go(0, "d2", "p2", "u3")
            places(segments, begin, begin_row, frequency, table)
            go(0, "q4")
            unpack_small(small_table, norms, 1, t)
            go(0, "q5", "d3")
        else:
            go(1, "q5", "u4", "p3")

        def project(i, _, layer=layer, here=here):
            j = t ^ i
            x, rows = here[j], rows_of(j)
            for c in range(3):
                y = dot(x, wq[layer, c].reshape(1024, 256))
                for h in range(2):
                    z = y[:, h * 128 : (h + 1) * 128]
                    if c < 2:
                        z = turned(z, table, rows, 1)
                    if c == 0:
                        z = z * (HEAD_DIM ** -0.5)
                    joined[layer, c, rows, pl.ds(h * 128, 128)] = z.astype(BF)
            return 0

        def expand(i, _, layer=layer, here=here, act=act, slp=slp, norm=norm):
            j = t ^ i
            x, rows = here[j], rows_of(j)
            for m in range(4):
                cols = pl.ds(m * 256, 256)
                u = dot(x, wu[layer, :, :, :, :, cols].reshape(1024, 256)) + norm[3:4, cols]
                a, s = gelu_and_slope(u)
                act[rows, cols] = a.astype(BF)
                slp[rows, cols] = s.astype(BF)
            return 0

        def attention(far, layer=layer, att=att, query=query, keys=keys, values=values):
            for r in range(4):
                wanted = (yh != r // 2) if far else (yh == r // 2)
                pl.when(wanted)(
                    functools.partial(attend, r, query, keys, values, begin, att, marks, lse.at[layer])
                )

        def keep(*pairs, layer=layer):
            for a, b in pairs:
                open_copies.append(copies.start(a, b.at[layer]))

        marks[...] = jnp.zeros_like(marks)
        lax.fori_loop(0, 1, project, 0)
        spread.near_here()
        lax.fori_loop(1, 2, project, 0)
        go(*((0, "u4") if layer == 0 else (1, "d4", "u5")))
        if layer == 1:
            lax.fori_loop(0, 2, expand, 0)
        spread.far_here()
        if layer == 0:
            go(1, "q0", "u0", "d0", "p0")
            turn_cot.start()
        lax.fori_loop(2, 3, project, 0)
        if layer == 1:
            lax.fori_loop(2, 3, expand, 0)
        spread.both_here()
        lax.fori_loop(3, 4, project, 0)
        if layer == 1:
            lax.fori_loop(3, 4, expand, 0)
        keep((here, normed_h), (joined.at[layer], joined_h), (wq.at[layer], wq_h))
        if layer == 0:
            go(0, "p3", "d4")
            attention(True)
            go(0, "u5", "p4")
            attention(False)
            go(0, "d5")
            lax.fori_loop(0, 2, expand, 0)
            go(0, "p5")
            lax.fori_loop(2, 4, expand, 0)
            go(1, "q1", "u1", "d1", "p1")
            turn_cot.near_here()
        else:
            go(1, "p4")
            attention(True)
            go(1, "d5", "p5")
        keep((act, active_h), (slp, slope_h), (wu.at[layer], wu_h))
        full = wf[layer].reshape(32, 16, 512).astype(F32)
        wp[layer] = jnp.concatenate([full[:, :8], full[:, 8:]], axis=2).reshape(256, 1024).astype(BF)
        collect = Collect(place, sems, partial.at[layer], pair.at[layer], across.at[layer])
        collects.append(collect)

        def output(j, layer=layer, att=att, act=act):
            x, y = att[rows_of(j)], act[rows_of(j)]
            for m in range(2):
                cols = pl.ds(m * 512, 512)
                out = dot(x, wp[layer, :, cols]) + dot(y, wd[layer, :, :, :, :, cols].reshape(1024, 512))
                partial[layer, j, :, cols] = out.astype(BF)

        output(t ^ 3)
        collect.first()
        output(t ^ 2)
        collect.second()
        if layer == 0:
            go(1, "q2", "u2", "q3")
        if layer == 1:
            attention(False)
        keep((att, attended_h), (wd.at[layer], wd_h), (wp.at[layer], wp_h))
        output(t ^ 1)
        collect.third()
        output(t)
        if layer == 0:
            go(1, "d2", "p2", "u3")
        result[...] = state + norm[2:3] + collect.chip_sum()
        if layer == 0:
            turn_cot.far_here()
        result[...] += collect.far_sum()
        if layer == 0:
            go(1, "q4", "d3")
    mixed[...] = last[...].astype(BF)
    turn_cot.both_here()
    shared.sent()
    for link in links:
        link.sent()
    for part in spreads + collects + [turn_cot]:
        part.sent()
    for copy in open_copies:
        copy.wait()


def forward(tokens, small, segments, frequency, proj, cotangent, qkv, up, down):
    vm, anywhere = pl.BlockSpec(memory_space=pltpu.VMEM), pl.BlockSpec(memory_space=pl.ANY)
    number = 3 + QuickGather.links + 8 * Gather.links + 3 * Spread.links + 2 * Collect.links
    S, V = jax.ShapeDtypeStruct, pltpu.VMEM
    ring = (2, 4, 4)
    q, w, p = (2, 3) + ring + (32, 256), (2,) + ring + (32, 1024), (2,) + ring + (16, 512)
    group, square, slim = (2, 4, TOK, 1024), (2, 1024, 1024), (2, 1024, 256)
    joined = (2, 3, 1024, 256)
    return pl.pallas_call(
        forward_kernel,
        out_shape=[
            S((TOK, 1024), BF), S((TOK, 1024), F32), S((2, 8, 1024), F32), S((2, 8, 1024), F32),
            S((1, 1024), jnp.int32), S((3, 1024, 128), F32),
            S((4, TOK, 1024), BF), S(group, BF), S(joined, BF), S(slim, BF), S(square, BF), S(square, BF),
            S(q, BF), S(w, BF), S(w, BF), S((2, 256, 1024), BF),
        ],
        in_specs=[vm] * 5 + [anywhere] * 4,
        out_specs=[vm] * 6 + [anywhere] * 10,
        scratch_shapes=[
            V((4, 8, 128), F32), V(ring + (8, 128), F32), V((2, 16, 512), BF),
            V(q, BF), V(w, BF), V(w, BF), V(p, BF), V((2, 256, 1024), BF),
            V(group, BF), V(joined, BF), V(slim, BF), V(square, BF), V(square, BF),
            V(group, BF), V((2, 2, TOK, 1024), BF), V((2, TOK, 1024), BF), V((TOK, 128), F32), V((TOK, 1024), F32), V((1024, 1), jnp.int32),
            pltpu.SemaphoreType.DMA((28,)),
            pltpu.SemaphoreType.DMA((number,)), pltpu.SemaphoreType.DMA((number,)),
        ],
        compiler_params=pltpu.CompilerParams(
            collective_id=0, has_side_effects=True, vmem_limit_bytes=62 * 2**20
        ),
        name="forward_layers",
    )(tokens, small, segments, frequency, proj, cotangent, qkv, up, down)


def attend_back(g, query, keys, values, grad_out, begin, lse, delta, grad_query, grad_joined, table):
    lanes = pl.ds(g * 128, 128)
    for block in range(4):
        start, size = block * TOK, 1024 - block * TOK
        here, on = pl.ds(start, TOK), pl.ds(start, size)
        k, v = keys[here, lanes], values[here, lanes]
        q, d = query[on, lanes], grad_out[on, lanes]
        row = iota((TOK, size), 0) + start
        column = iota((TOK, size), 1) + start
        allowed = (row >= begin[:, on]) & (row <= column)
        lane = iota((TOK, 128), 1)
        by_value, by_key, by_query = [], [], None
        for half in range(2):
            head = pl.ds(2 * g + half, 1)
            mine = (lane // 64) == half
            kh, vh = [jnp.where(mine, part, jnp.zeros_like(part)) for part in (k, v)]
            scores = jnp.where(allowed, dot_cols(kh, q), -1e30)
            probs = jnp.exp(scores - lse[head, on])
            grad_scores = (probs * (dot_cols(vh, d) - delta[head, on])).astype(BF)
            by_value.append(dot(probs.astype(BF), d))
            by_key.append(dot(grad_scores, q))
            back = dot_rows(grad_scores, kh)
            by_query = back if by_query is None else by_query + back
        if block == 0:
            grad_query[on, lanes] = by_query
        else:
            grad_query[on, lanes] += by_query
        both = jnp.where(lane < 64, by_key[0], by_key[1])
        grad_joined[1, here, lanes] = turned(both, table, here, -1).astype(BF)
        grad_joined[2, here, lanes] = jnp.where(lane < 64, by_value[0], by_value[1]).astype(BF)


def grouped(b, *rest):
    return (b // 2, pl.ds(2 * (b % 2), 2)) + rest


def backward_kernel(
    tokens, middle, cotangent, norms, table, begin, lse,
    cot_h, normed_h, joined_h, attended_h, active_h, slope_h, wq_h, wu_h, wd_h, wp_h,
    token_grad, own_sums, total_q, total_p, total_u, total_d,
    wq, wu, wd, wp, normed, joined, attended, active, slope,
    whole, grad_up, grad_att, delta, grad_query, grad_joined, dqkv, dup, ddown, dproj,
    partial, pair, across, sums, small_table, tile, four, first, second, third,
    loads, clear, sends, recvs, *scratch,
):
    place = Place()
    sems = Sems(sends, recvs)
    t = place.t
    copies = Loads(loads)
    sources = {
        "whole": (cot_h, whole.at[1]), "wd": (wd_h, wd), "slope": (slope_h, slope), "wp": (wp_h, wp),
        "attended": (attended_h, attended), "active": (active_h, active), "normed": (normed_h, normed),
        "joined": (joined_h, joined), "wu": (wu_h, wu), "wq": (wq_h, wq),
    }
    fetched = {}

    def fetch(layer, *names):
        for name in names:
            src, dst = sources[name]
            if name == "whole":
                fetched[layer, name] = [copies.start(src.at[t ^ flip], dst.at[t ^ flip]) for flip in (1, 2, 3)]
            else:
                fetched[layer, name] = [copies.start(src.at[layer], dst)]

    def need(layer, *names):
        for name in names:
            for copy in fetched[layer, name]:
                copy.wait()

    fetch(1, *sources)
    meet(ring_peers(place) + second_peers(place) + tensor_peers(place))
    head = iota((8, 256), 0)
    member = jnp.where(iota((8, 256), 1) // 64 == head, 1.0, 0.0).astype(BF)
    closing = []
    holders = [scratch[11 * number : 11 * number + 11] for number in range(4)]

    def reduce_job(number, given, total, lead):
        return Reduce(place, sems, given, total, lead, holders[number])

    def wide_jobs(layer):
        return [reduce_job(0, ddown, total_d.at[layer], 0), reduce_job(1, dup, total_u.at[layer], 0)]

    def slim_jobs(layer):
        return [reduce_job(3, dqkv, total_q.at[layer], 1), reduce_job(2, dproj, total_p.at[layer], 0)]

    def run(jobs, stage):
        for job in jobs:
            job.stage(stage)

    ring = ring_peers(place)

    def hand_over(number):
        for peer in ring:
            pl.semaphore_signal(clear.at[number], inc=1, device_id=peer, device_id_type=MESH)

    def take_over(number):
        pl.semaphore_wait(clear.at[number], len(ring))

    for layer in (1, 0):
        grad = cotangent[...].astype(F32) if layer == 1 else token_grad[...]
        state = middle[...] if layer == 1 else tokens[...].astype(F32)
        rows_in = whole.at[layer]
        small = sums.at[layer]
        small[...] = jnp.zeros((8, 1024), F32)
        small[2:3] = jnp.sum(grad, axis=0, keepdims=True)
        if layer == 0:
            rows_in[t] = grad.astype(BF)
            spread = Spread(place, sems, rows_in.at[t], rows_in)
            spread.start()
            closing.append(spread)
            run(wide, 3)
        else:
            rows_in[t] = cotangent[...]
            need(1, "whole")
        need(layer, "wd", "slope", "wp", "attended")

        def enter(i, _, rows_in=rows_in, small=small):
            j = t ^ i
            g, rows = rows_in[j], rows_of(j)
            for m in range(4):
                cols = pl.ds(m * 256, 256)
                low = (dot_cols(g, wd[cols]) * slope[rows, cols].astype(F32)).astype(BF)
                grad_up[rows, cols] = low
                small[3:4, cols] += jnp.sum(low.astype(F32), axis=0, keepdims=True)
            d = dot_cols(g, wp[...]).astype(BF)
            grad_att[rows] = d
            both = d.astype(F32) * attended[rows].astype(F32)
            high = both.astype(BF)
            rest = (both - high.astype(F32)).astype(BF)
            delta[:, rows] = dot_cols(member, high) + dot_cols(member, rest)
            return 0

        if layer == 1:
            lax.fori_loop(0, 4, enter, 0)
        else:
            lax.fori_loop(0, 1, enter, 0)
            spread.near_here()
            lax.fori_loop(1, 2, enter, 0)
            spread.far_here()
            run(slim, 2)
            run(wide, 4)
            lax.fori_loop(2, 3, enter, 0)
            spread.both_here()
            lax.fori_loop(3, 4, enter, 0)
            run(slim, 3)
            run(wide, 5)
            hand_over(0)
        need(layer, "active", "normed")

        def wide_grads(b, _, rows_in=rows_in):
            cols = pl.ds(pl.multiple_of(b * 256, 256), 256)
            left = active[:, cols].T
            for m in range(2):
                right = pl.ds(m * 512, 512)
                out = dot(left[:, :TOK], rows_in[0, :, right])
                for j in range(1, 4):
                    out = out + dot(left[:, j * TOK : (j + 1) * TOK], rows_in[j, :, right])
                ddown[grouped(b, slice(None), slice(None), right)] = out.astype(BF).reshape(2, 4, 32, 512)
            left = normed[:, cols].T
            for m in range(2):
                right = pl.ds(m * 512, 512)
                out = dot(left, grad_up[:, right]).astype(BF)
                dup[grouped(b, slice(None), slice(None), right)] = out.reshape(2, 4, 32, 512)
            return 0

        lax.fori_loop(0, 4, wide_grads, 0)
        if layer == 0:
            run(slim, 4)
            take_over(0)
        wide = wide_jobs(layer)
        run(wide, 0)
        need(layer, "joined")
        for g in range(2):
            attend_back(
                g, joined.at[0], joined.at[1], joined.at[2], grad_att, begin, lse.at[layer], delta,
                grad_query, grad_joined, table,
            )
            if layer == 0 and g == 0:
                run(slim, 5)
                hand_over(1)
        need(layer, "wu", "wq")
        if layer == 1:
            fetch(0, "wd", "slope", "wp", "active", "joined")

        def turn_back(j, _):
            rows = rows_of(j)
            for h in range(2):
                lanes = pl.ds(h * 128, 128)
                z = grad_query[rows, lanes] * (HEAD_DIM ** -0.5)
                grad_joined[0, rows, lanes] = turned(z, table, rows, -1).astype(BF)
            return 0

        lax.fori_loop(0, 4, turn_back, 0)

        def leave(j):
            rows = rows_of(j)
            for m in range(4):
                cols = pl.ds(m * 256, 256)
                out = dot_cols(grad_up[rows], wu[cols])
                for c in range(3):
                    out = out + dot_cols(grad_joined[c, rows], wq[c, cols])
                partial[j, :, cols] = out.astype(BF)

        def slim_grads(b, _):
            left = normed[:, pl.ds(pl.multiple_of(b * 256, 256), 256)].T
            for c in range(3):
                dqkv[(c,) + grouped(b)] = dot(left, grad_joined[c]).astype(BF).reshape(2, 4, 32, 256)
            return 0

        def slim_all():
            lax.fori_loop(0, 4, slim_grads, 0)
            left = attended[...].T
            halves = []
            for m in range(2):
                right = pl.ds(m * 512, 512)
                out = dot(left[:, :TOK], rows_in[0, :, right])
                for j in range(1, 4):
                    out = out + dot(left[:, j * TOK : (j + 1) * TOK], rows_in[j, :, right])
                halves.append(out.reshape(32, 8, 512))
            dproj[...] = jnp.concatenate(halves, axis=1).astype(BF).reshape(2, 4, 4, 16, 512)
        if layer == 0:
            slim_all()
            slim = slim_jobs(layer)
            take_over(1)
            run(wide, 1)
            run(slim, 0)
        collect = Collect(place, sems, partial, pair.at[layer], across.at[layer])
        leave(t ^ 3)
        collect.first()
        leave(t ^ 2)
        collect.second()
        if layer == 1:
            run(wide, 1)
        leave(t ^ 1)
        collect.third()
        leave(t)

        if layer == 1:
            slim_all()
            fetch(0, "attended", "normed", "wu", "wq")
            slim = slim_jobs(layer)
            run(slim, 0)
        if layer == 0:
            early = [(1, 0), (1, 1), (1, 2), (1, 3), (0, 2), (0, 3)]
            pack_small(sums, small_table, early, t, True)

            run(wide, 2)
            run(slim, 1)
        own = collect.chip_sum() + collect.far_sum()
        run(wide, 2 if layer == 1 else 3)
        collect.sent()
        unit, inverse = normalize(state)
        small[0:1] = jnp.sum(own * unit, axis=0, keepdims=True)
        small[1:2] = jnp.sum(own, axis=0, keepdims=True)
        scaled = own * norms[layer, 0:1]
        after = grad + inverse * (
            scaled
            - jnp.mean(scaled, axis=-1, keepdims=True)
            - unit * jnp.mean(scaled * unit, axis=-1, keepdims=True)
        )
        token_grad[...] = after
        run(slim, 1 if layer == 1 else 2)

    pack_small(sums, small_table, [(0, 0), (0, 1)], t, False)
    quick = QuickReduce(place, sems, small_table, first, second, third, tile)
    quick.begin("z")
    run(wide, 4)
    quick.end("z")
    quick.begin("x")
    run(slim, 3)
    quick.end("x")
    quick.begin("y")
    run(wide, 5)
    quick.end("y")
    links = [Link(sems, peer) for peer in tensor_peers(place)]
    for number, link in enumerate(links):
        link.start(tile, four.at[number])
    run(slim, 4)
    whole_tile = tile[...]
    for number, link in enumerate(links):
        link.arrived(four.at[number])
        whole_tile = whole_tile + four[number]
    own_sums[...] = whole_tile
    run(slim, 5)
    quick.sent()
    for part in closing:
        part.sent()
    for link in links:
        link.sent()


def backward(tokens, middle, cotangent, norms, table, begin, lse, saved):
    vm, anywhere = pl.BlockSpec(memory_space=pltpu.VMEM), pl.BlockSpec(memory_space=pl.ANY)
    S, V = jax.ShapeDtypeStruct, pltpu.VMEM
    ring = (2, 4, 4)
    square, slim, three = (1024, 1024), (1024, 256), (3, 1024, 256)
    group = (4, TOK, 1024)
    big, q, p = ring + (32, 1024), (3,) + ring + (32, 256), ring + (16, 512)
    number = 3 + QuickReduce.links + Spread.links + 2 * Collect.links
    number += 2 * (2 * Reduce.links(1024) + Reduce.links(256) + Reduce.links(512))
    reduce_scratch = []
    for shape in (big, big, p, q):
        reduce_scratch += Reduce.scratch(shape, BF)
    return pl.pallas_call(
        backward_kernel,
        out_shape=[
            S((TOK, 1024), F32), S((8, 128), F32), S((2, 3, 32, 256), F32), S((2, 16, 512), F32),
            S((2, 32, 1024), F32), S((2, 32, 1024), F32),
        ],
        in_specs=[vm] * 7 + [anywhere] * 10,
        out_specs=[vm] * 6,
        scratch_shapes=[
            V(three, BF), V(square, BF), V(square, BF), V((256, 1024), BF),
            V(square, BF), V(three, BF), V(slim, BF), V(square, BF), V(square, BF),
            V((2,) + group, BF), V(square, BF), V(slim, BF), V((8, 1024), F32), V(slim, F32), V(three, BF),
            V(q, BF), V(big, BF), V(big, BF), V(p, BF),
            V(group, BF), V((2, 2, TOK, 1024), BF), V((2, TOK, 1024), BF), V((2, 8, 1024), F32),
            V(ring + (8, 128), F32), V((8, 128), F32), V((3, 8, 128), F32),
            V((4, 2, 4, 8, 128), F32), V((4, 2, 8, 128), F32), V((8, 128), F32),
            pltpu.SemaphoreType.DMA((21,)), pltpu.SemaphoreType.REGULAR((2,)),
            pltpu.SemaphoreType.DMA((number,)), pltpu.SemaphoreType.DMA((number,)),
        ]
        + reduce_scratch,
        compiler_params=pltpu.CompilerParams(
            collective_id=1, has_side_effects=True, vmem_limit_bytes=62 * 2**20
        ),
        name="backward_layers",
    )(tokens, middle, cotangent, norms, table, begin, lse, *saved)


def finish_kernel(
    sums, proj, mixed, token_grad, qkv, up, down,
    gain_o, shift_o, final_o, hidden_o, proj_o, mixed_o, token_grad_o, qkv_o, up_o, down_o, sems,
):
    pairs = ((token_grad, token_grad_o), (mixed, mixed_o), (up, up_o), (down, down_o), (qkv, qkv_o))
    copies = [pltpu.make_async_copy(a, b, sems.at[number]) for number, (a, b) in enumerate(pairs)]
    for copy in copies:
        copy.start()
    proj_o[:, :, :512] = proj[:, :8]
    proj_o[:, :, 512:] = proj[:, 8:]
    line = jnp.broadcast_to(sums[pl.ds(lax.axis_index("tensor"), 1)], (8, 128))
    for layer in range(2):
        for member, out in enumerate((gain_o, shift_o, final_o)):
            start = member * 16 + layer * 8
            out[layer : layer + 1] = pltpu.roll(line, (128 - start) % 128, 1)[:1, :8]
        hidden_o[layer : layer + 1] = pltpu.roll(line, 80 - 32 * layer, 1)[:1, :32]
    for copy in copies:
        copy.wait()


def finish(sums, proj, *big):
    vm, anywhere = pl.BlockSpec(memory_space=pltpu.VMEM), pl.BlockSpec(memory_space=pl.ANY)
    S = jax.ShapeDtypeStruct
    return pl.pallas_call(
        finish_kernel,
        out_shape=[S((2, 8), F32)] * 3 + [S((2, 32), F32), S((2, 8, 1024), F32)]
        + [S(part.shape, part.dtype) for part in big],
        in_specs=[vm] * 7,
        out_specs=[vm] * 5 + [anywhere] * 5,
        scratch_shapes=[pltpu.SemaphoreType.DMA((5,))],
        name="results",
    )(sums, proj, *big)


def local(
    tokens,
    segment_ids,
    norm_gain,
    norm_shift,
    qkv_weight,
    proj_weight,
    up_weight,
    hidden_bias,
    down_weight,
    final_bias,
    cotangent,
):
    parts = [part[layer : layer + 1] for part in (norm_gain, norm_shift, final_bias, hidden_bias) for layer in range(2)]
    row = jnp.concatenate(parts + [jnp.zeros((1, 16), BF)], axis=1).astype(F32)
    small = jnp.broadcast_to(row, (8, 128))
    half = ROT // 2
    angles = np.exp(np.arange(half) * (-2.0 * math.log(10000.0) / ROT)).astype(np.float32)
    frequency = np.tile(angles, 128 // half)[None]
    mixed, middle, norms, lse, begin, table, cot, *saved = forward(
        tokens, small, segment_ids[None], frequency, proj_weight, cotangent,
        qkv_weight, up_weight, down_weight,
    )
    saved[5] = saved[5].reshape(2, 3, 1024, 256)
    saved[6] = saved[6].reshape(2, 1024, 1024)
    saved[7] = saved[7].reshape(2, 1024, 1024)
    saved[0] = saved[0].reshape(2, 1024, 1024)
    token_grad, sums, qkv, proj, up, down = backward(
        tokens, middle, cotangent, norms, table, begin, lse, [cot] + saved
    )
    gain, shift, final, hidden, proj, mixed, token_grad, qkv, up, down = finish(
        sums, proj, mixed, token_grad, qkv, up, down
    )
    return (mixed, token_grad, gain, shift, qkv, proj, up, hidden, down, final)


def solution(mesh):
    placed = (
        P(("dp", "tensor"), None),
        P("dp"),
        P(None, ("dp", "tensor")),
        P(None, ("dp", "tensor")),
        P(None, None, "dp", "tensor"),
        P(None, ("tensor", "dp"), None),
        P(None, "dp", "tensor"),
        P(None, ("tensor", "dp")),
        P(None, ("tensor", "dp"), None),
        P(None, ("dp", "tensor")),
        P(("dp", "tensor"), None),
    )
    return jax.shard_map(
        local,
        mesh=mesh,
        in_specs=placed,
        out_specs=(
            P(("dp", "tensor"), None),
            P(("dp", "tensor"), None),
            P(None, ("dp", "tensor")),
            P(None, ("dp", "tensor")),
            P(None, None, "dp", "tensor"),
            P(None, ("tensor", "dp"), None),
            P(None, "dp", "tensor"),
            P(None, ("tensor", "dp")),
            P(None, ("tensor", "dp"), None),
            P(None, ("dp", "tensor")),
        ),
        check_vma=False,
    )
```

```python
import functools
import math

import jax
import jax.numpy as jnp
import numpy as np
from jax import lax
from jax.experimental import pallas as pl
from jax.experimental.pallas import tpu as pltpu
from jax.sharding import PartitionSpec as P

HEAD_DIM = 64
ROT = 32
MESH = pl.DeviceIdType.MESH
ALL = slice(None)


epsilon = 1e-05


class Place:
    def __init__(self):
        dp = lax.axis_index("dp")
        self.t = lax.axis_index("tensor")
        self.dp = dp
        self.at = {"y": dp // 16, "x": lax.rem(dp // 4, 4), "z": lax.rem(dp, 4)}

    def plus(self, axis, step):
        return lax.rem(self.at[axis] + (step % 4), 4)

    def peer(self, axis, step):
        if axis == "core":
            return (self.dp, self.t ^ 1)
        if axis == "far":
            return (self.dp, self.t ^ 2)
        if axis == "both":
            return (self.dp, self.t ^ 3)
        c = dict(self.at)
        c[axis] = 1 - c["y"] if axis == "y" else self.plus(axis, step)
        return ((c["y"] * 4 + c["x"]) * 4 + c["z"], self.t)


def meet(peers):
    barrier = pltpu.get_barrier_semaphore()
    for peer in peers:
        pl.semaphore_signal(barrier, inc=1, device_id=peer, device_id_type=MESH)
    pl.semaphore_wait(barrier, len(peers))


def ring_peers(place):
    return [place.peer(a, s) for a, s in (("x", 1), ("x", -1), ("z", 1), ("z", -1), ("y", 1))]


def second_peers(place):
    return [place.peer("x", 2), place.peer("z", 2)]


def tensor_peers(place):
    return [place.peer(a, 0) for a in ("core", "far", "both")]


class Sems:
    def __init__(self, send, recv):
        self.send, self.recv, self.used = send, recv, 0

    def take(self):
        self.used += 1
        return self.send.at[self.used - 1], self.recv.at[self.used - 1]


class Link:
    def __init__(self, sems, peer):
        self.send, self.recv = sems.take()
        self.peer = peer

    def copy(self, src, dst):
        return pltpu.make_async_remote_copy(
            src_ref=src, dst_ref=dst, send_sem=self.send, recv_sem=self.recv,
            device_id=self.peer, device_id_type=MESH,
        )

    def start(self, src, dst):
        self.out = self.copy(src, dst)
        self.out.start()

    def arrived(self, dst):
        self.copy(dst, dst).wait_recv()

    def sent(self):
        self.out.wait_send()


def paths_of(columns, both):
    half = columns // 2
    if both:
        return (("z", "x", pl.ds(0, half)), ("x", "z", pl.ds(half, half)))
    return (("z", "x", pl.ds(0, columns)),)


def region(ref, lead, where, cols):
    return ref.at[(ALL,) * lead + (where["y"], where["x"], where["z"], ALL, cols)]


class Gather:
    links = 17
    stages = 6

    def __init__(self, place, sems, own, full, lead, local_sem):
        self.place, self.own, self.full, self.lead, self.local_sem = place, own, full, lead, local_sem
        self.paths = paths_of(full.shape[-1], full.shape[-1] % 256 == 0)
        self.cross = Link(sems, place.peer("y", 1))
        self.rings = []
        for first, second, cols in self.paths:
            self.rings.append(
                [
                    [Link(sems, place.peer(axis, 1)), Link(sems, place.peer(axis, -1)),
                     Link(sems, place.peer(axis, 1)), Link(sems, place.peer(axis, -1))]
                    for axis in (first, second)
                ]
            )

    def _at(self, cols, **where):
        return region(self.full, self.lead, where, cols)

    def stage(self, number):
        place, everything = self.place, pl.ds(0, self.full.shape[-1])
        here = dict(place.at)
        if number == 0:
            mine = self._at(everything, **here)
            self.local = pltpu.make_async_copy(self.own, mine, self.local_sem)
            self.local.start()
            self.cross.start(self.own, mine)
            return
        if number == 1:
            self.local.wait()
            self.cross.arrived(self._at(everything, **{**here, "y": 1 - here["y"]}))
        for (first, second, cols), rings in zip(self.paths, self.rings):
            axis = first if number <= 2 else second
            other = here[second] if number <= 2 else ALL
            rest = second if number <= 2 else first
            ring = rings[0] if number <= 2 else rings[1]

            def at(y, step):
                index = here[axis] if step == 0 else place.plus(axis, step)
                return self._at(cols, **{"y": y, axis: index, rest: other})

            if number in (1, 3):
                if number == 3:
                    self._close(rings[0], first, second, cols, here[second])
                ring[0].start(at(ALL, 0), at(ALL, 0))
                ring[1].start(at(ALL, 0), at(ALL, 0))
            elif number in (2, 4):
                ring[0].arrived(at(ALL, -1))
                ring[2].start(at(0, -1), at(0, -1))
                ring[1].arrived(at(ALL, 1))
                ring[3].start(at(1, 1), at(1, 1))
            else:
                self._close(ring, axis, rest, cols, ALL)
        if number == 5:
            self.cross.sent()
            for rings in self.rings:
                for ring in rings:
                    for link in ring:
                        link.sent()

    def _close(self, ring, axis, rest, cols, other):
        opposite = self.place.plus(axis, 2)
        ring[2].arrived(self._at(cols, **{"y": 0, axis: opposite, rest: other}))
        ring[3].arrived(self._at(cols, **{"y": 1, axis: opposite, rest: other}))


class Reduce:
    stages = 6

    @staticmethod
    def links(columns):
        return 1 + 12 * len(paths_of(columns, columns % 256 == 0))

    @staticmethod
    def scratch(shape, dtype):
        *lead, _, _, _, rows, columns = shape
        lead = tuple(lead)
        shapes = []
        for _, _, cols in paths_of(columns, columns % 256 == 0):
            w = cols.size
            shapes += [pltpu.VMEM(lead + (2, 4, rows, w), dtype)]
            shapes += [pltpu.VMEM(lead + (2, 2, 4, rows, w), dtype)]
            shapes += [pltpu.VMEM(lead + (2, rows, w), dtype)]
            shapes += [pltpu.VMEM(lead + (2, 2, rows, w), dtype)]
        shapes += [pltpu.VMEM(lead + (2, rows, columns), jnp.float32)]
        shapes += [pltpu.VMEM(lead + (rows, columns), dtype)] * 2
        return shapes

    def __init__(self, place, sems, given, total, lead, scratch):
        self.place, self.given, self.total, self.lead = place, given, total, lead
        columns = given.shape[-1]
        self.dtype = given.dtype
        self.paths = paths_of(columns, columns % 256 == 0)
        self.cross = Link(sems, place.peer("y", 1))
        self.work = []
        for number, (first, second, cols) in enumerate(self.paths):
            ends = []
            for axis in (first, second):
                ends.append([Link(sems, place.peer(axis, s)) for s in (1, -1, 1, -1, 1, -1)])
            self.work.append((ends, scratch[4 * number : 4 * number + 4]))
        self.summed, self.leaving, self.coming = scratch[-3:]

    def _given(self, cols, **where):
        return region(self.given, self.lead, where, cols)

    def _pre(self, *index):
        return (ALL,) * self.lead + index

    def _add(self, into, *terms):
        total = terms[0][...].astype(into.dtype)
        for term in terms[1:]:
            total = total + term[...].astype(into.dtype)
        into[...] = total

    def _send(self, links, near, far, at):
        pre = self._pre
        links[0].start(at(0, 2), near.at[pre(0)])
        links[1].start(at(1, 2), near.at[pre(1)])
        links[2].start(at(1, 1), far.at[pre(0, 1)])
        links[3].start(at(0, -1), far.at[pre(1, 0)])

    def _pass(self, links, near, far, at):
        pre = self._pre
        for way, step in ((0, 1), (1, -1)):
            slot = near.at[pre(way)]
            links[way].arrived(slot)
            self._add(slot, slot, at(way, step))
            links[4 + way].start(slot, far.at[pre(way, way)])

    def _join(self, links, far):
        pre = self._pre
        links[2].arrived(far.at[pre(0, 1)])
        links[3].arrived(far.at[pre(1, 0)])
        links[4].arrived(far.at[pre(0, 0)])
        links[5].arrived(far.at[pre(1, 1)])

    def stage(self, number):
        place, pre = self.place, self._pre
        here = dict(place.at)
        for (first, second, cols), (ends, (near1, far1, near2, far2)) in zip(self.paths, self.work):

            def at1(y, step):
                index = here[first] if step == 0 else place.plus(first, step)
                return self._given(cols, **{"y": y, first: index, second: ALL})

            def at2(y, step):
                index = here[second] if step == 0 else place.plus(second, step)
                return far1.at[pre(0, y, index)]

            if number == 0:
                self._send(ends[0], near1, far1, at1)
            elif number == 1:
                self._pass(ends[0], near1, far1, at1)
            elif number == 2:
                self._join(ends[0], far1)
                for y in (0, 1):
                    slot = far1.at[pre(0, y)]
                    self._add(slot, slot, far1.at[pre(1, y)], at1(y, 0))
                self._send(ends[1], near2, far2, at2)
            elif number == 3:
                self._pass(ends[1], near2, far2, at2)
            elif number == 4:
                self._join(ends[1], far2)
                for y in (0, 1):
                    into = self.summed.at[pre(y, ALL, cols)]
                    self._add(into, at2(y, 0), far2.at[pre(0, y)], far2.at[pre(1, y)])
        if number == 4:
            self._add(self.leaving, self.summed.at[pre(1 - here["y"])])
            self.cross.start(self.leaving, self.coming)
        elif number == 5:
            self.cross.arrived(self.coming)
            self._add(self.total, self.summed.at[pre(here["y"])], self.coming)
            self.cross.sent()
            for ends, _ in self.work:
                for links in ends:
                    for link in links:
                        link.sent()


TOK = 256
CHUNKS = 4
BF = jnp.bfloat16
F32 = jnp.float32


def dot(left, right):
    return jnp.dot(left, right, preferred_element_type=F32)


def dot_cols(left, right):
    return lax.dot_general(left, right, (((1,), (1,)), ((), ())), preferred_element_type=F32)


def dot_rows(left, right):
    return lax.dot_general(left, right, (((0,), (0,)), ((), ())), preferred_element_type=F32)


def rows_of(block):
    return pl.ds(pl.multiple_of(block * TOK, TOK), TOK)


def iota(shape, dim):
    return lax.broadcasted_iota(jnp.int32, shape, dim)


def turned(z, table, rows, sign):
    ahead, behind = pltpu.roll(z, 112, 1), pltpu.roll(z, 16, 1)
    if sign > 0:
        return z * table[0, rows] + ahead * table[1, rows] + behind * table[2, rows]
    return z * table[0, rows] - ahead * table[1, rows] - behind * table[2, rows]


def gelu_and_slope(u):
    c, a = math.sqrt(2.0 / math.pi), 0.044715
    square = u * u
    t = jnp.tanh(c * u * (1.0 + a * square))
    half = 0.5 * (1.0 + t)
    return u * half, half + (0.5 * c) * u * (1.0 - t * t) * (1.0 + (3.0 * a) * square)


def normalize(x):
    center = x - jnp.mean(x, axis=-1, keepdims=True)
    inverse = lax.rsqrt(jnp.mean(center * center, axis=-1, keepdims=True) + epsilon)
    return center * inverse, inverse


class Loads:
    def __init__(self, sems):
        self.sems, self.used = sems, 0

    def start(self, src, dst):
        copy = pltpu.make_async_copy(src, dst, self.sems.at[self.used])
        self.used += 1
        copy.start()
        return copy


class QuickGather:
    links = 7

    def __init__(self, place, sems, full):
        self.place, self.full = place, full
        self.ends = {"y": [Link(sems, place.peer("y", 1))]}
        for axis in ("x", "z"):
            self.ends[axis] = [Link(sems, place.peer(axis, step)) for step in (1, 2, 3)]

    def _at(self, axis, step):
        here = self.place.at
        if axis == "y":
            return self.full.at[here["y"] if step == 0 else 1 - here["y"], here["x"], here["z"]]
        if axis == "x":
            return self.full.at[:, self.place.plus("x", step), here["z"]]
        return self.full.at[:, :, self.place.plus("z", step)]

    def begin(self, axis):
        for link in self.ends[axis]:
            link.start(self._at(axis, 0), self._at(axis, 0))

    def end(self, axis):
        for number, link in enumerate(self.ends[axis]):
            link.arrived(self._at(axis, -1 - number))

    def sent(self):
        for links in self.ends.values():
            for link in links:
                link.sent()


class QuickReduce:
    links = 7

    def __init__(self, place, sems, given, first, second, third, total):
        self.place, self.given, self.total = place, given, total
        self.first, self.second, self.third = first, second, third
        self.ends = {"y": [Link(sems, place.peer("y", 1))]}
        for axis in ("x", "z"):
            self.ends[axis] = [Link(sems, place.peer(axis, step)) for step in (1, 2, 3)]

    def begin(self, axis):
        place = self.place
        if axis == "y":
            self.ends["y"][0].start(self.second.at[3, 1 - place.at["y"]], self.third)
            return
        for number, link in enumerate(self.ends[axis]):
            if axis == "z":
                link.start(self.given.at[:, :, place.plus("z", number + 1)], self.first.at[number])
            else:
                link.start(self.first.at[3, :, place.plus("x", number + 1)], self.second.at[number])

    def end(self, axis):
        place = self.place
        if axis == "y":
            self.ends["y"][0].arrived(self.third)
            self.total[...] = self.second[3, place.at["y"]] + self.third[...]
            return
        into = self.first if axis == "z" else self.second
        total = self.given[:, :, place.at["z"]] if axis == "z" else self.first[3, :, place.at["x"]]
        for number, link in enumerate(self.ends[axis]):
            link.arrived(into.at[number])
            total = total + into[number]
        into[3] = total

    def sent(self):
        for links in self.ends.values():
            for link in links:
                link.sent()


class Spread:
    links = 2 * CHUNKS + 1

    def __init__(self, place, sems, own, whole):
        self.t, self.own, self.whole = place.t, own, whole
        core, far = place.peer("core", 0), place.peer("far", 0)
        self.across = [Link(sems, far) for _ in range(CHUNKS)]
        self.onward = [Link(sems, core) for _ in range(CHUNKS)]
        self.near = Link(sems, core)
        n = TOK // CHUNKS
        self.part = [pl.ds(k * n, n) for k in range(CHUNKS)]

    def start(self):
        for k, part in enumerate(self.part):
            self.across[k].start(self.own.at[part], self.whole.at[self.t, part])
        self.near.start(self.own, self.whole.at[self.t])

    def near_here(self):
        self.near.arrived(self.whole.at[self.t ^ 1])

    def far_here(self):
        for k, part in enumerate(self.part):
            got = self.whole.at[self.t ^ 2, part]
            self.across[k].arrived(got)
            self.onward[k].start(got, got)

    def both_here(self):
        for k, part in enumerate(self.part):
            self.onward[k].arrived(self.whole.at[self.t ^ 3, part])

    def sent(self):
        for link in self.across + self.onward + [self.near]:
            link.sent()


class Collect:
    links = 3

    def __init__(self, place, sems, partial, pair, across):
        self.t, self.partial, self.pair, self.across = place.t, partial, pair, across
        self.to_core, self.back = Link(sems, place.peer("core", 0)), Link(sems, place.peer("core", 0))
        self.to_far = Link(sems, place.peer("far", 0))

    def first(self):
        self.to_core.start(self.partial.at[self.t ^ 3], self.pair.at[0])

    def second(self):
        self.to_core.arrived(self.pair.at[0])
        self.pair[0] = self.pair[0] + self.partial[self.t ^ 2]
        self.to_far.start(self.pair.at[0], self.across)

    def third(self):
        self.back.start(self.partial.at[self.t ^ 1], self.pair.at[1])

    def chip_sum(self):
        self.back.arrived(self.pair.at[1])
        return self.partial[self.t].astype(F32) + self.pair[1].astype(F32)

    def far_sum(self):
        self.to_far.arrived(self.across)
        return self.across[...].astype(F32)

    def sent(self):
        for link in (self.to_core, self.to_far, self.back):
            link.sent()


def feature_owner(shape):
    row, column = iota(shape, 0), iota(shape, 1)
    return ((column >> 3) == (row >> 3) * 4 + (row & 7)) & ((row & 7) < 4)


def hidden_owner(shape, t):
    row, column = iota(shape, 0), iota(shape, 1)
    return ((column >> 5) == (row >> 3)) & ((row & 7) == t)


def lane_of(layer, member, column):
    if member < 3:
        return member * 16 + layer * 8 + (column & 7)
    return 48 + layer * 32 + (column & 31)


def unpack_small(small_table, norms, layer, t, members=range(4)):
    packed = small_table[...].reshape(256, 128).astype(BF)
    lane, column = iota((128, 1024), 0), iota((128, 1024), 1)
    shape = (256, 1024)
    for member in members:
        mine = feature_owner(shape) if member < 3 else hidden_owner(shape, t)
        pick = jnp.where(lane == lane_of(layer, member, column), 1.0, 0.0).astype(BF)
        row = jnp.sum(jnp.where(mine, dot(packed, pick), 0.0), axis=0, keepdims=True)
        norms[layer, member : member + 1] = row


def pack_small(sums, small_table, rows, t, fresh):
    lane, column = iota((1024, 128), 1), iota((1024, 128), 0)
    shape = (256, 1024)
    total = jnp.zeros((256, 128), F32)
    for layer, member in rows:
        mine = feature_owner(shape) if member < 3 else hidden_owner(shape, t)
        pick = jnp.where(lane == lane_of(layer, member, column), 1.0, 0.0).astype(BF)
        rest = jnp.where(mine, sums[layer, member : member + 1], 0.0)
        for _ in range(3):
            part = rest.astype(BF)
            total = total + dot(part, pick)
            rest = rest - part.astype(F32)
    total = total.reshape(2, 4, 4, 8, 128)
    small_table[...] = total if fresh else small_table[...] + total


def places(segments, beginning, begin_row, frequency, table):
    ids = segments[...].astype(F32)
    down = jnp.broadcast_to(ids, (128, 1024)).T
    row_total = jnp.zeros((1, 1024), F32)
    lane = iota((TOK, 128), 1) & 63
    for block in range(4):
        rows = pl.ds(block * TOK, TOK)
        column = down[block * TOK : (block + 1) * TOK, :1]
        row_total = row_total + jnp.sum(jnp.where(column < ids, 1.0, 0.0), axis=0, keepdims=True)
        first = jnp.sum(jnp.where(ids < column, 1.0, 0.0), axis=1, keepdims=True)
        beginning[rows] = first.astype(jnp.int32)
        index = (iota((TOK, 128), 0) + block * TOK).astype(F32)
        angle = (index - first) * frequency[...]
        cosine, sine = jnp.cos(angle), jnp.sin(angle)
        table[0, rows] = jnp.where(lane < 32, cosine, 1.0)
        table[1, rows] = jnp.where(lane < 16, -sine, 0.0)
        table[2, rows] = jnp.where((lane >= 16) & (lane < 32), sine, 0.0)
    begin_row[...] = row_total.astype(jnp.int32)


def attend(r, query, keys, values, begin, attended, marks, lse):
    width = (r + 1) * TOK
    rows = pl.ds(r * TOK, TOK)
    row = iota((TOK, width), 0) + r * TOK
    column = iota((TOK, width), 1)
    allowed = (column >= begin[rows]) & (column <= row)
    lane = iota((TOK, 128), 1)

    def pair(g, _):
        lanes = pl.ds(pl.multiple_of(g * 128, 128), 128)
        q, k, v = query[rows, lanes], keys[:width, lanes], values[:width, lanes]
        outs = []
        for half in range(2):
            mine = jnp.where((lane // 64) == half, q, jnp.zeros_like(q))
            scores = jnp.where(allowed, dot_cols(mine, k), -1e30)
            peak = jnp.max(scores, axis=-1, keepdims=True)
            weights = jnp.exp(scores - peak)
            total = jnp.sum(weights, axis=-1, keepdims=True)
            outs.append(dot(weights.astype(BF), v) * (1.0 / total))
            marks[...] = jnp.where(lane == 2 * g + half, peak + jnp.log(total), marks[...])
        attended[rows, lanes] = jnp.where(lane < 64, outs[0], outs[1]).astype(BF)
        return 0

    lax.fori_loop(0, 2, pair, 0)
    lse[:, rows] = marks[...].T[:8]


def forward_kernel(
    tokens, small, segments, frequency, proj_own, cotangent, qkv_own, up_own, down_own,
    mixed, norms, lse, begin_row, middle_h, table_h, cot_h, normed_h, joined_h, attended_h, active_h, slope_h, wq_h, wu_h, wd_h, wp_h,
    four, small_table, folded, wq, wu, wd, wf, wp,
    normed, joined, attended, active, slope, partial, pair, across, marks, last, begin, middle, table,
    loads, sends, recvs,
):
    place = Place()
    sems = Sems(sends, recvs)
    t = place.t
    yh = t // 2
    copies = Loads(loads)
    both = proj_own[...].astype(F32)
    folded[...] = jnp.concatenate([both[..., :512], both[..., 512:]], axis=1).astype(BF)
    meet(ring_peers(place) + second_peers(place) + tensor_peers(place))

    links = [Link(sems, peer) for peer in tensor_peers(place)]
    four[t] = small[...]
    for link in links:
        link.start(small, four.at[t])
    jobs = {}
    for layer in range(2):
        for name, own, full, lead in (
            ("qkv", qkv_own, wq, 1), ("up", up_own, wu, 0), ("down", down_own, wd, 0), ("proj", folded, wf, 0)
        ):
            number = 4 * layer + len(jobs) % 4
            jobs[name, layer] = Gather(place, sems, own.at[layer], full.at[layer], lead, loads.at[number])
    copies.used = 9
    early = [jobs[name, 0] for name in ("qkv", "up", "down", "proj")]
    late = [jobs[name, 1] for name in ("qkv", "up", "down", "proj")]

    def go(layer, *stages):
        for stage in stages:
            job = jobs[{"q": "qkv", "u": "up", "d": "down", "p": "proj"}[stage[0]], layer]
            job.stage(int(stage[1]))

    go(0, "q0", "u0", "d0", "p0")
    for link, flip in zip(links, (1, 2, 3)):
        link.arrived(four.at[t ^ flip])
    row = iota((8, 128), 0)
    packed = jnp.zeros((8, 128), F32)
    for other in range(4):
        packed = jnp.where(row == other, four[other], packed)
    small_table[place.at["y"], place.at["x"], place.at["z"]] = packed
    shared = QuickGather(place, sems, small_table)
    shared.begin("y")
    go(0, "q1")
    shared.end("y")
    shared.begin("x")
    go(0, "u1")
    shared.end("x")
    shared.begin("z")
    go(0, "q2", "d1", "p1")
    shared.end("z")
    unpack_small(small_table, norms, 0, t, (0, 1))
    turn_cot = Spread(place, sems, cotangent, cot_h)
    open_copies = []
    spreads, collects = [], []

    for layer in range(2):
        state = tokens[...].astype(F32) if layer == 0 else middle[...]
        result = middle if layer == 0 else last
        norm = norms.at[layer]
        here, act, slp = normed.at[layer], active.at[layer], slope.at[layer]
        query, keys, values = [joined.at[layer, c] for c in range(3)]
        att = attended.at[layer]
        unit, _ = normalize(state)
        here[t] = (unit * norm[0:1] + norm[1:2]).astype(BF)
        spread = Spread(place, sems, here.at[t], here)
        spread.start()
        spreads.append(spread)
        if layer == 0:
            go(0, "u2", "q3", "u3")
            go(1, "p0", "u0")
            unpack_small(small_table, norms, 0, t, (2, 3))
            places(segments, begin, begin_row, frequency, table)
            open_copies.append(copies.start(table, table_h))
            go(0, "d2", "q4")
            unpack_small(small_table, norms, 1, t)
            go(1, "q0")
            go(0, "d3", "q5")
        else:
            go(1, "u4", "q5", "d3", "u5")

        def project(i, _, layer=layer, here=here):
            j = t ^ i
            x, rows = here[j], rows_of(j)
            for c in range(3):
                y = dot(x, wq[layer, c].reshape(1024, 256))
                for h in range(2):
                    z = y[:, h * 128 : (h + 1) * 128]
                    if c < 2:
                        z = turned(z, table, rows, 1)
                    if c == 0:
                        z = z * (HEAD_DIM ** -0.5)
                    joined[layer, c, rows, pl.ds(h * 128, 128)] = z.astype(BF)
            return 0

        def expand(i, _, layer=layer, here=here, act=act, slp=slp, norm=norm):
            j = t ^ i
            x, rows = here[j], rows_of(j)
            for m in range(4):
                cols = pl.ds(m * 256, 256)
                u = dot(x, wu[layer, :, :, :, :, cols].reshape(1024, 256)) + norm[3:4, cols]
                a, s = gelu_and_slope(u)
                act[rows, cols] = a.astype(BF)
                slp[rows, cols] = s.astype(BF)
            return 0

        def attention(far, layer=layer, att=att, query=query, keys=keys, values=values):
            for r in range(4):
                wanted = (yh != r // 2) if far else (yh == r // 2)
                pl.when(wanted)(
                    functools.partial(attend, r, query, keys, values, begin, att, marks, lse.at[layer])
                )

        def keep(*pairs, layer=layer):
            for a, b in pairs:
                open_copies.append(copies.start(a, b.at[layer]))

        marks[...] = jnp.zeros_like(marks)
        lax.fori_loop(0, 1, project, 0)
        if layer == 0:
            go(0, "p2")
        spread.near_here()
        lax.fori_loop(1, 2, project, 0)
        if layer == 1:
            lax.fori_loop(0, 2, expand, 0)
            go(1, "p3", "d4")
        spread.far_here()
        if layer == 0:
            go(0, "u4")
            go(1, "q1")
            turn_cot.start()
        lax.fori_loop(2, 3, project, 0)
        if layer == 1:
            lax.fori_loop(2, 3, expand, 0)
        spread.both_here()
        lax.fori_loop(3, 4, project, 0)
        if layer == 1:
            lax.fori_loop(3, 4, expand, 0)
        keep((here, normed_h), (joined.at[layer], joined_h), (wq.at[layer], wq_h))
        if layer == 0:
            attention(True)
            go(0, "p3", "d4")
            go(1, "p1", "u1")
            attention(False)
            go(0, "u5")
            lax.fori_loop(0, 2, expand, 0)
            go(0, "p4")
            lax.fori_loop(2, 4, expand, 0)
            go(0, "d5")
            go(1, "q2")
            go(0, "p5")
            go(1, "u2", "d0")
            turn_cot.near_here()
        else:
            go(1, "d5", "p4")
            attention(True)
            go(1, "p5")
        keep((act, active_h), (slp, slope_h), (wu.at[layer], wu_h))
        full = wf[layer].reshape(32, 16, 512).astype(F32)
        wp[layer] = jnp.concatenate([full[:, :8], full[:, 8:]], axis=2).reshape(256, 1024).astype(BF)
        collect = Collect(place, sems, partial.at[layer], pair.at[layer], across.at[layer])
        collects.append(collect)

        def output(j, layer=layer, att=att, act=act):
            x, y = att[rows_of(j)], act[rows_of(j)]
            for m in range(2):
                cols = pl.ds(m * 512, 512)
                out = dot(x, wp[layer, :, cols]) + dot(y, wd[layer, :, :, :, :, cols].reshape(1024, 512))
                partial[layer, j, :, cols] = out.astype(BF)

        output(t ^ 3)
        collect.first()
        output(t ^ 2)
        collect.second()
        if layer == 0:
            go(1, "d1", "q3")
        if layer == 1:
            attention(False)
        keep((att, attended_h), (wd.at[layer], wd_h), (wp.at[layer], wp_h))
        output(t ^ 1)
        collect.third()
        output(t)
        if layer == 0:
            go(1, "p2", "u3")
        result[...] = state + norm[2:3] + collect.chip_sum()
        if layer == 0:
            turn_cot.far_here()
        result[...] += collect.far_sum()
        if layer == 0:
            open_copies.append(copies.start(middle, middle_h))
            go(1, "d2", "q4")
    mixed[...] = last[...].astype(BF)
    turn_cot.both_here()
    shared.sent()
    for link in links:
        link.sent()
    for part in spreads + collects + [turn_cot]:
        part.sent()
    for copy in open_copies:
        copy.wait()


def forward(tokens, small, segments, frequency, proj, cotangent, qkv, up, down):
    vm, anywhere = pl.BlockSpec(memory_space=pltpu.VMEM), pl.BlockSpec(memory_space=pl.ANY)
    number = 3 + QuickGather.links + 8 * Gather.links + 3 * Spread.links + 2 * Collect.links
    S, V = jax.ShapeDtypeStruct, pltpu.VMEM
    ring = (2, 4, 4)
    q, w, p = (2, 3) + ring + (32, 256), (2,) + ring + (32, 1024), (2,) + ring + (16, 512)
    group, square, slim = (2, 4, TOK, 1024), (2, 1024, 1024), (2, 1024, 256)
    joined = (2, 3, 1024, 256)
    return pl.pallas_call(
        forward_kernel,
        out_shape=[
            S((TOK, 1024), BF), S((2, 8, 1024), F32), S((2, 8, 1024), F32), S((1, 1024), jnp.int32),
            S((TOK, 1024), F32), S((3, 1024, 128), F32),
            S((4, TOK, 1024), BF), S(group, BF), S(joined, BF), S(slim, BF), S(square, BF), S(square, BF),
            S(q, BF), S(w, BF), S(w, BF), S((2, 256, 1024), BF),
        ],
        in_specs=[vm] * 5 + [anywhere] * 4,
        out_specs=[vm] * 4 + [anywhere] * 12,
        scratch_shapes=[
            V((4, 8, 128), F32), V(ring + (8, 128), F32), V((2, 16, 512), BF),
            V(q, BF), V(w, BF), V(w, BF), V(p, BF), V((2, 256, 1024), BF),
            V(group, BF), V(joined, BF), V(slim, BF), V(square, BF), V(square, BF),
            V(group, BF), V((2, 2, TOK, 1024), BF), V((2, TOK, 1024), BF), V((TOK, 128), F32), V((TOK, 1024), F32), V((1024, 1), jnp.int32), V((TOK, 1024), F32), V((3, 1024, 128), F32),
            pltpu.SemaphoreType.DMA((30,)),
            pltpu.SemaphoreType.DMA((number,)), pltpu.SemaphoreType.DMA((number,)),
        ],
        compiler_params=pltpu.CompilerParams(
            collective_id=0, has_side_effects=True, vmem_limit_bytes=62 * 2**20
        ),
        name="forward_layers",
    )(tokens, small, segments, frequency, proj, cotangent, qkv, up, down)


def attend_back(g, query, keys, values, grad_out, begin, lse, delta, grad_query, grad_joined, table):
    lanes = pl.ds(g * 128, 128)
    for block in range(4):
        start, size = block * TOK, 1024 - block * TOK
        here, on = pl.ds(start, TOK), pl.ds(start, size)
        k, v = keys[here, lanes], values[here, lanes]
        q, d = query[on, lanes], grad_out[on, lanes]
        row = iota((TOK, size), 0) + start
        column = iota((TOK, size), 1) + start
        allowed = (row >= begin[:, on]) & (row <= column)
        lane = iota((TOK, 128), 1)
        by_value, by_key, by_query = [], [], None
        for half in range(2):
            head = pl.ds(2 * g + half, 1)
            mine = (lane // 64) == half
            kh, vh = [jnp.where(mine, part, jnp.zeros_like(part)) for part in (k, v)]
            scores = jnp.where(allowed, dot_cols(kh, q), -1e30)
            probs = jnp.exp(scores - lse[head, on])
            grad_scores = (probs * (dot_cols(vh, d) - delta[head, on])).astype(BF)
            by_value.append(dot(probs.astype(BF), d))
            by_key.append(dot(grad_scores, q))
            back = dot_rows(grad_scores, kh)
            by_query = back if by_query is None else by_query + back
        if block == 0:
            grad_query[on, lanes] = by_query
        else:
            grad_query[on, lanes] += by_query
        both = jnp.where(lane < 64, by_key[0], by_key[1])
        grad_joined[1, here, lanes] = turned(both, table, here, -1).astype(BF)
        grad_joined[2, here, lanes] = jnp.where(lane < 64, by_value[0], by_value[1]).astype(BF)


def grouped(b, *rest):
    return (b // 2, pl.ds(2 * (b % 2), 2)) + rest


def backward_kernel(
    cotangent, norms, begin, lse, tokens_h, middle_h, table_h,
    cot_h, normed_h, joined_h, attended_h, active_h, slope_h, wq_h, wu_h, wd_h, wp_h,
    token_grad, own_sums, total_q, total_p, total_u, total_d,
    tokens, middle, table, wq, wu, wd, wp, normed, joined, attended, active, slope,
    whole, grad_up, grad_att, delta, grad_query, grad_joined, dqkv, dup, ddown, dproj,
    partial, pair, across, sums, small_table, tile, four, first, second, third,
    loads, clear, sends, recvs, *scratch,
):
    place = Place()
    sems = Sems(sends, recvs)
    t = place.t
    copies = Loads(loads)
    sources = {
        "whole": (cot_h, whole.at[1]), "wd": (wd_h, wd), "slope": (slope_h, slope), "wp": (wp_h, wp),
        "attended": (attended_h, attended), "active": (active_h, active), "normed": (normed_h, normed),
        "joined": (joined_h, joined), "wu": (wu_h, wu), "wq": (wq_h, wq),
    }
    fetched = {}

    def fetch(layer, *names):
        for name in names:
            src, dst = sources[name]
            if name == "whole":
                fetched[layer, name] = [copies.start(src.at[t ^ flip], dst.at[t ^ flip]) for flip in (1, 2, 3)]
            else:
                fetched[layer, name] = [copies.start(src.at[layer], dst)]

    def need(layer, *names):
        for name in names:
            for copy in fetched[layer, name]:
                copy.wait()

    fetch(1, *sources)
    for name, src, dst in (("table", table_h, table), ("middle", middle_h, middle), ("tokens", tokens_h, tokens)):
        fetched[1, name] = [copies.start(src, dst)]
    meet(ring_peers(place) + second_peers(place) + tensor_peers(place))
    head = iota((8, 256), 0)
    member = jnp.where(iota((8, 256), 1) // 64 == head, 1.0, 0.0).astype(BF)
    closing = []
    holders = [scratch[11 * number : 11 * number + 11] for number in range(4)]

    def reduce_job(number, given, total, lead):
        return Reduce(place, sems, given, total, lead, holders[number])

    reducing = {}

    def wide_jobs(layer):
        reducing[layer, "d"] = reduce_job(0, ddown, total_d.at[layer], 0)
        reducing[layer, "u"] = reduce_job(1, dup, total_u.at[layer], 0)

    def slim_jobs(layer):
        reducing[layer, "q"] = reduce_job(3, dqkv, total_q.at[layer], 1)
        reducing[layer, "p"] = reduce_job(2, dproj, total_p.at[layer], 0)

    def go(layer, *stages):
        for stage in stages:
            reducing[layer, stage[0]].stage(int(stage[1]))

    ring = ring_peers(place)

    def hand_over(number):
        for peer in ring:
            pl.semaphore_signal(clear.at[number], inc=1, device_id=peer, device_id_type=MESH)

    def take_over(number):
        pl.semaphore_wait(clear.at[number], len(ring))

    for layer in (1, 0):
        grad = cotangent[...].astype(F32) if layer == 1 else token_grad[...]
        rows_in = whole.at[layer]
        small = sums.at[layer]
        small[...] = jnp.zeros((8, 1024), F32)
        small[2:3] = jnp.sum(grad, axis=0, keepdims=True)
        if layer == 0:
            rows_in[t] = grad.astype(BF)
            spread = Spread(place, sems, rows_in.at[t], rows_in)
            spread.start()
            closing.append(spread)
            go(1, "p1", "q1", "p2")
        else:
            rows_in[t] = cotangent[...]
            need(1, "whole")
        need(layer, "wd", "slope", "wp", "attended")

        def enter(i, _, rows_in=rows_in, small=small):
            j = t ^ i
            g, rows = rows_in[j], rows_of(j)
            for m in range(4):
                cols = pl.ds(m * 256, 256)
                low = (dot_cols(g, wd[cols]) * slope[rows, cols].astype(F32)).astype(BF)
                grad_up[rows, cols] = low
                small[3:4, cols] += jnp.sum(low.astype(F32), axis=0, keepdims=True)
            d = dot_cols(g, wp[...]).astype(BF)
            grad_att[rows] = d
            both = d.astype(F32) * attended[rows].astype(F32)
            high = both.astype(BF)
            rest = (both - high.astype(F32)).astype(BF)
            delta[:, rows] = dot_cols(member, high) + dot_cols(member, rest)
            return 0

        if layer == 1:
            lax.fori_loop(0, 4, enter, 0)
        else:
            lax.fori_loop(0, 1, enter, 0)
            go(1, "q2")
            spread.near_here()
            lax.fori_loop(1, 2, enter, 0)
            go(1, "p3", "u5", "p4", "d4", "q3")
            spread.far_here()
            lax.fori_loop(2, 3, enter, 0)
            spread.both_here()
            lax.fori_loop(3, 4, enter, 0)
            go(1, "d5", "q4")
            hand_over(0)
            go(1, "p5")
        need(layer, "active", "normed")

        def wide_grads(b, _, rows_in=rows_in):
            cols = pl.ds(pl.multiple_of(b * 256, 256), 256)
            left = active[:, cols].T
            for m in range(2):
                right = pl.ds(m * 512, 512)
                out = dot(left[:, :TOK], rows_in[0, :, right])
                for j in range(1, 4):
                    out = out + dot(left[:, j * TOK : (j + 1) * TOK], rows_in[j, :, right])
                ddown[grouped(b, slice(None), slice(None), right)] = out.astype(BF).reshape(2, 4, 32, 512)
            left = normed[:, cols].T
            for m in range(2):
                right = pl.ds(m * 512, 512)
                out = dot(left, grad_up[:, right]).astype(BF)
                dup[grouped(b, slice(None), slice(None), right)] = out.reshape(2, 4, 32, 512)
            return 0

        lax.fori_loop(0, 4, wide_grads, 0)
        wide_jobs(layer)
        if layer == 0:
            take_over(0)
            go(0, "d0", "u0")
            go(1, "q5")
            hand_over(1)
        else:
            go(1, "u0")
        need(layer, "joined")
        if layer == 1:
            need(1, "table")
        for g in range(2):
            attend_back(
                g, joined.at[0], joined.at[1], joined.at[2], grad_att, begin, lse.at[layer], delta,
                grad_query, grad_joined, table,
            )
            if layer == 1 and g == 0:
                go(1, "d0")
        need(layer, "wu", "wq")
        if layer == 1:
            fetch(0, "wd", "slope", "wp", "active", "joined")

        def turn_back(j, _):
            rows = rows_of(j)
            for h in range(2):
                lanes = pl.ds(h * 128, 128)
                z = grad_query[rows, lanes] * (HEAD_DIM ** -0.5)
                grad_joined[0, rows, lanes] = turned(z, table, rows, -1).astype(BF)
            return 0

        lax.fori_loop(0, 4, turn_back, 0)

        def leave(j):
            rows = rows_of(j)
            for m in range(4):
                cols = pl.ds(m * 256, 256)
                out = dot_cols(grad_up[rows], wu[cols])
                for c in range(3):
                    out = out + dot_cols(grad_joined[c, rows], wq[c, cols])
                partial[j, :, cols] = out.astype(BF)

        def slim_grads(b, _):
            left = normed[:, pl.ds(pl.multiple_of(b * 256, 256), 256)].T
            for c in range(3):
                dqkv[(c,) + grouped(b)] = dot(left, grad_joined[c]).astype(BF).reshape(2, 4, 32, 256)
            return 0

        def slim_all():
            lax.fori_loop(0, 4, slim_grads, 0)
            left = attended[...].T
            halves = []
            for m in range(2):
                right = pl.ds(m * 512, 512)
                out = dot(left[:, :TOK], rows_in[0, :, right])
                for j in range(1, 4):
                    out = out + dot(left[:, j * TOK : (j + 1) * TOK], rows_in[j, :, right])
                halves.append(out.reshape(32, 8, 512))
            dproj[...] = jnp.concatenate(halves, axis=1).astype(BF).reshape(2, 4, 4, 16, 512)
        if layer == 0:
            slim_all()
            slim_jobs(layer)
            take_over(1)
            go(0, "q0")
        collect = Collect(place, sems, partial, pair.at[layer], across.at[layer])
        leave(t ^ 3)
        collect.first()
        leave(t ^ 2)
        collect.second()
        if layer == 1:
            go(1, "u1")
        leave(t ^ 1)
        collect.third()
        leave(t)

        if layer == 1:
            go(1, "d1", "u2", "d2", "u3")
            slim_all()
            fetch(0, "attended", "normed", "wu", "wq")
            slim_jobs(layer)
            go(1, "p0", "q0", "d3", "u4")
        if layer == 0:
            early = [(1, 0), (1, 1), (1, 2), (1, 3), (0, 2), (0, 3)]
            go(0, "p0", "d1")
            pack_small(sums, small_table, early, t, True)
            go(0, "p1", "u1", "d2", "q1", "p2")
        own = collect.chip_sum() + collect.far_sum()
        collect.sent()
        if layer == 1:
            need(1, "middle", "tokens")
        unit, inverse = normalize(middle[...] if layer == 1 else tokens[...].astype(F32))
        small[0:1] = jnp.sum(own * unit, axis=0, keepdims=True)
        small[1:2] = jnp.sum(own, axis=0, keepdims=True)
        scaled = own * norms[layer, 0:1]
        after = grad + inverse * (
            scaled
            - jnp.mean(scaled, axis=-1, keepdims=True)
            - unit * jnp.mean(scaled * unit, axis=-1, keepdims=True)
        )
        token_grad[...] = after
        if layer == 0:
            go(0, "u2", "d3")

    pack_small(sums, small_table, [(0, 0), (0, 1)], t, False)
    quick = QuickReduce(place, sems, small_table, first, second, third, tile)
    quick.begin("z")
    go(0, "q2")
    quick.end("z")
    quick.begin("x")
    go(0, "p3", "u3", "d4")
    quick.end("x")
    quick.begin("y")
    go(0, "q3", "p4", "u4")
    quick.end("y")
    links = [Link(sems, peer) for peer in tensor_peers(place)]
    for number, link in enumerate(links):
        link.start(tile, four.at[number])
    go(0, "p5", "q4")
    whole_tile = tile[...]
    for number, link in enumerate(links):
        link.arrived(four.at[number])
        whole_tile = whole_tile + four[number]
    own_sums[...] = whole_tile
    go(0, "u5", "d5", "q5")
    quick.sent()
    for part in closing:
        part.sent()
    for link in links:
        link.sent()


def backward(tokens, middle, cotangent, norms, table, begin, lse, saved):
    vm, anywhere = pl.BlockSpec(memory_space=pltpu.VMEM), pl.BlockSpec(memory_space=pl.ANY)
    S, V = jax.ShapeDtypeStruct, pltpu.VMEM
    ring = (2, 4, 4)
    square, slim, three = (1024, 1024), (1024, 256), (3, 1024, 256)
    group = (4, TOK, 1024)
    big, q, p = ring + (32, 1024), (3,) + ring + (32, 256), ring + (16, 512)
    number = 3 + QuickReduce.links + Spread.links + 2 * Collect.links
    number += 2 * (2 * Reduce.links(1024) + Reduce.links(256) + Reduce.links(512))
    reduce_scratch = []
    for shape in (big, big, p, q):
        reduce_scratch += Reduce.scratch(shape, BF)
    return pl.pallas_call(
        backward_kernel,
        out_shape=[
            S((TOK, 1024), F32), S((8, 128), F32), S((2, 3, 32, 256), F32), S((2, 16, 512), F32),
            S((2, 32, 1024), F32), S((2, 32, 1024), F32),
        ],
        in_specs=[vm] * 4 + [anywhere] * 13,
        out_specs=[vm] * 6,
        scratch_shapes=[
            V((TOK, 1024), BF), V((TOK, 1024), F32), V((3, 1024, 128), F32),
            V(three, BF), V(square, BF), V(square, BF), V((256, 1024), BF),
            V(square, BF), V(three, BF), V(slim, BF), V(square, BF), V(square, BF),
            V((2,) + group, BF), V(square, BF), V(slim, BF), V((8, 1024), F32), V(slim, F32), V(three, BF),
            V(q, BF), V(big, BF), V(big, BF), V(p, BF),
            V(group, BF), V((2, 2, TOK, 1024), BF), V((2, TOK, 1024), BF), V((2, 8, 1024), F32),
            V(ring + (8, 128), F32), V((8, 128), F32), V((3, 8, 128), F32),
            V((4, 2, 4, 8, 128), F32), V((4, 2, 8, 128), F32), V((8, 128), F32),
            pltpu.SemaphoreType.DMA((24,)), pltpu.SemaphoreType.REGULAR((2,)),
            pltpu.SemaphoreType.DMA((number,)), pltpu.SemaphoreType.DMA((number,)),
        ]
        + reduce_scratch,
        compiler_params=pltpu.CompilerParams(
            collective_id=1, has_side_effects=True, vmem_limit_bytes=62 * 2**20
        ),
        name="backward_layers",
    )(cotangent, norms, begin, lse, tokens, middle, table, *saved)


def finish_kernel(
    sums, proj, mixed, token_grad, qkv, up, down,
    gain_o, shift_o, final_o, hidden_o, proj_o, mixed_o, token_grad_o, qkv_o, up_o, down_o, sems,
):
    pairs = ((token_grad, token_grad_o), (mixed, mixed_o), (up, up_o), (down, down_o), (qkv, qkv_o))
    copies = [pltpu.make_async_copy(a, b, sems.at[number]) for number, (a, b) in enumerate(pairs)]
    for copy in copies:
        copy.start()
    proj_o[:, :, :512] = proj[:, :8]
    proj_o[:, :, 512:] = proj[:, 8:]
    line = jnp.broadcast_to(sums[pl.ds(lax.axis_index("tensor"), 1)], (8, 128))
    for layer in range(2):
        for member, out in enumerate((gain_o, shift_o, final_o)):
            start = member * 16 + layer * 8
            out[layer : layer + 1] = pltpu.roll(line, (128 - start) % 128, 1)[:1, :8]
        hidden_o[layer : layer + 1] = pltpu.roll(line, 80 - 32 * layer, 1)[:1, :32]
    for copy in copies:
        copy.wait()


def finish(sums, proj, *big):
    vm, anywhere = pl.BlockSpec(memory_space=pltpu.VMEM), pl.BlockSpec(memory_space=pl.ANY)
    S = jax.ShapeDtypeStruct
    return pl.pallas_call(
        finish_kernel,
        out_shape=[S((2, 8), F32)] * 3 + [S((2, 32), F32), S((2, 8, 1024), F32)]
        + [S(part.shape, part.dtype) for part in big],
        in_specs=[vm] * 7,
        out_specs=[vm] * 5 + [anywhere] * 5,
        scratch_shapes=[pltpu.SemaphoreType.DMA((5,))],
        name="results",
    )(sums, proj, *big)


def local(
    tokens,
    segment_ids,
    norm_gain,
    norm_shift,
    qkv_weight,
    proj_weight,
    up_weight,
    hidden_bias,
    down_weight,
    final_bias,
    cotangent,
):
    parts = [part[layer : layer + 1] for part in (norm_gain, norm_shift, final_bias, hidden_bias) for layer in range(2)]
    row = jnp.concatenate(parts + [jnp.zeros((1, 16), BF)], axis=1).astype(F32)
    small = jnp.broadcast_to(row, (8, 128))
    half = ROT // 2
    angles = np.exp(np.arange(half) * (-2.0 * math.log(10000.0) / ROT)).astype(np.float32)
    frequency = np.tile(angles, 128 // half)[None]
    mixed, norms, lse, begin, middle, table, cot, *saved = forward(
        tokens, small, segment_ids[None], frequency, proj_weight, cotangent,
        qkv_weight, up_weight, down_weight,
    )
    saved[5] = saved[5].reshape(2, 3, 1024, 256)
    saved[6] = saved[6].reshape(2, 1024, 1024)
    saved[7] = saved[7].reshape(2, 1024, 1024)
    saved[0] = saved[0].reshape(2, 1024, 1024)
    token_grad, sums, qkv, proj, up, down = backward(
        tokens, middle, cotangent, norms, table, begin, lse, [cot] + saved
    )
    gain, shift, final, hidden, proj, mixed, token_grad, qkv, up, down = finish(
        sums, proj, mixed, token_grad, qkv, up, down
    )
    return (mixed, token_grad, gain, shift, qkv, proj, up, hidden, down, final)


def solution(mesh):
    placed = (
        P(("dp", "tensor"), None),
        P("dp"),
        P(None, ("dp", "tensor")),
        P(None, ("dp", "tensor")),
        P(None, None, "dp", "tensor"),
        P(None, ("tensor", "dp"), None),
        P(None, "dp", "tensor"),
        P(None, ("tensor", "dp")),
        P(None, ("tensor", "dp"), None),
        P(None, ("dp", "tensor")),
        P(("dp", "tensor"), None),
    )
    return jax.shard_map(
        local,
        mesh=mesh,
        in_specs=placed,
        out_specs=(
            P(("dp", "tensor"), None),
            P(("dp", "tensor"), None),
            P(None, ("dp", "tensor")),
            P(None, ("dp", "tensor")),
            P(None, None, "dp", "tensor"),
            P(None, ("tensor", "dp"), None),
            P(None, "dp", "tensor"),
            P(None, ("tensor", "dp")),
            P(None, ("tensor", "dp"), None),
            P(None, ("dp", "tensor")),
        ),
        check_vma=False,
    )
```

```python
import functools
import math

import jax
import jax.numpy as jnp
import numpy as np
from jax import lax
from jax.experimental import pallas as pl
from jax.experimental.pallas import tpu as pltpu
from jax.sharding import PartitionSpec as P

HEAD_DIM = 64
ROT = 32
MESH = pl.DeviceIdType.MESH
ALL = slice(None)


epsilon = 1e-05


class Place:
    def __init__(self):
        dp = lax.axis_index("dp")
        self.t = lax.axis_index("tensor")
        self.dp = dp
        self.at = {"y": dp // 16, "x": lax.rem(dp // 4, 4), "z": lax.rem(dp, 4)}

    def plus(self, axis, step):
        return lax.rem(self.at[axis] + (step % 4), 4)

    def peer(self, axis, step):
        if axis == "core":
            return (self.dp, self.t ^ 1)
        if axis == "far":
            return (self.dp, self.t ^ 2)
        if axis == "both":
            return (self.dp, self.t ^ 3)
        c = dict(self.at)
        c[axis] = 1 - c["y"] if axis == "y" else self.plus(axis, step)
        return ((c["y"] * 4 + c["x"]) * 4 + c["z"], self.t)


def meet(peers):
    barrier = pltpu.get_barrier_semaphore()
    for peer in peers:
        pl.semaphore_signal(barrier, inc=1, device_id=peer, device_id_type=MESH)
    pl.semaphore_wait(barrier, len(peers))


def ring_peers(place):
    return [place.peer(a, s) for a, s in (("x", 1), ("x", -1), ("z", 1), ("z", -1), ("y", 1))]


def second_peers(place):
    return [place.peer("x", 2), place.peer("z", 2)]


def tensor_peers(place):
    return [place.peer(a, 0) for a in ("core", "far", "both")]


class Sems:
    def __init__(self, send, recv):
        self.send, self.recv, self.used = send, recv, 0

    def take(self):
        self.used += 1
        return self.send.at[self.used - 1], self.recv.at[self.used - 1]


class Link:
    def __init__(self, sems, peer):
        self.send, self.recv = sems.take()
        self.peer = peer

    def copy(self, src, dst):
        return pltpu.make_async_remote_copy(
            src_ref=src, dst_ref=dst, send_sem=self.send, recv_sem=self.recv,
            device_id=self.peer, device_id_type=MESH,
        )

    def start(self, src, dst):
        self.out = self.copy(src, dst)
        self.out.start()

    def arrived(self, dst):
        self.copy(dst, dst).wait_recv()

    def sent(self):
        self.out.wait_send()


def paths_of(columns, both):
    half = columns // 2
    if both:
        return (("z", "x", pl.ds(0, half)), ("x", "z", pl.ds(half, half)))
    return (("z", "x", pl.ds(0, columns)),)


def region(ref, lead, where, cols):
    return ref.at[(ALL,) * lead + (where["y"], where["x"], where["z"], ALL, cols)]


class Gather:
    links = 17
    stages = 6

    def __init__(self, place, sems, own, full, lead, local_sem):
        self.place, self.own, self.full, self.lead, self.local_sem = place, own, full, lead, local_sem
        self.paths = paths_of(full.shape[-1], full.shape[-1] % 256 == 0)
        self.cross = Link(sems, place.peer("y", 1))
        self.rings = []
        for first, second, cols in self.paths:
            self.rings.append(
                [
                    [Link(sems, place.peer(axis, 1)), Link(sems, place.peer(axis, -1)),
                     Link(sems, place.peer(axis, 1)), Link(sems, place.peer(axis, -1))]
                    for axis in (first, second)
                ]
            )

    def _at(self, cols, **where):
        return region(self.full, self.lead, where, cols)

    def stage(self, number):
        place, everything = self.place, pl.ds(0, self.full.shape[-1])
        here = dict(place.at)
        if number == 0:
            mine = self._at(everything, **here)
            self.local = pltpu.make_async_copy(self.own, mine, self.local_sem)
            self.local.start()
            self.cross.start(self.own, mine)
            return
        if number == 1:
            self.local.wait()
            self.cross.arrived(self._at(everything, **{**here, "y": 1 - here["y"]}))
        for (first, second, cols), rings in zip(self.paths, self.rings):
            axis = first if number <= 2 else second
            other = here[second] if number <= 2 else ALL
            rest = second if number <= 2 else first
            ring = rings[0] if number <= 2 else rings[1]

            def at(y, step):
                index = here[axis] if step == 0 else place.plus(axis, step)
                return self._at(cols, **{"y": y, axis: index, rest: other})

            if number in (1, 3):
                if number == 3:
                    self._close(rings[0], first, second, cols, here[second])
                ring[0].start(at(ALL, 0), at(ALL, 0))
                ring[1].start(at(ALL, 0), at(ALL, 0))
            elif number in (2, 4):
                ring[0].arrived(at(ALL, -1))
                ring[2].start(at(0, -1), at(0, -1))
                ring[1].arrived(at(ALL, 1))
                ring[3].start(at(1, 1), at(1, 1))
            else:
                self._close(ring, axis, rest, cols, ALL)
        if number == 5:
            self.cross.sent()
            for rings in self.rings:
                for ring in rings:
                    for link in ring:
                        link.sent()

    def _close(self, ring, axis, rest, cols, other):
        opposite = self.place.plus(axis, 2)
        ring[2].arrived(self._at(cols, **{"y": 0, axis: opposite, rest: other}))
        ring[3].arrived(self._at(cols, **{"y": 1, axis: opposite, rest: other}))


class Reduce:
    stages = 6

    @staticmethod
    def links(columns):
        return 1 + 12 * len(paths_of(columns, columns % 256 == 0))

    @staticmethod
    def scratch(shape, dtype):
        *lead, _, _, _, rows, columns = shape
        lead = tuple(lead)
        shapes = []
        for _, _, cols in paths_of(columns, columns % 256 == 0):
            w = cols.size
            shapes += [pltpu.VMEM(lead + (2, 4, rows, w), dtype)]
            shapes += [pltpu.VMEM(lead + (2, 2, 4, rows, w), dtype)]
            shapes += [pltpu.VMEM(lead + (2, rows, w), dtype)]
            shapes += [pltpu.VMEM(lead + (2, 2, rows, w), dtype)]
        shapes += [pltpu.VMEM(lead + (2, rows, columns), jnp.float32)]
        shapes += [pltpu.VMEM(lead + (rows, columns), dtype)] * 2
        return shapes

    def __init__(self, place, sems, given, total, lead, scratch):
        self.place, self.given, self.total, self.lead = place, given, total, lead
        columns = given.shape[-1]
        self.dtype = given.dtype
        self.paths = paths_of(columns, columns % 256 == 0)
        self.cross = Link(sems, place.peer("y", 1))
        self.work = []
        for number, (first, second, cols) in enumerate(self.paths):
            ends = []
            for axis in (first, second):
                ends.append([Link(sems, place.peer(axis, s)) for s in (1, -1, 1, -1, 1, -1)])
            self.work.append((ends, scratch[4 * number : 4 * number + 4]))
        self.summed, self.leaving, self.coming = scratch[-3:]

    def _given(self, cols, **where):
        return region(self.given, self.lead, where, cols)

    def _pre(self, *index):
        return (ALL,) * self.lead + index

    def _add(self, into, *terms):
        total = terms[0][...].astype(into.dtype)
        for term in terms[1:]:
            total = total + term[...].astype(into.dtype)
        into[...] = total

    def _send(self, links, near, far, at):
        pre = self._pre
        links[0].start(at(0, 2), near.at[pre(0)])
        links[1].start(at(1, 2), near.at[pre(1)])
        links[2].start(at(1, 1), far.at[pre(0, 1)])
        links[3].start(at(0, -1), far.at[pre(1, 0)])

    def _pass(self, links, near, far, at):
        pre = self._pre
        for way, step in ((0, 1), (1, -1)):
            slot = near.at[pre(way)]
            links[way].arrived(slot)
            self._add(slot, slot, at(way, step))
            links[4 + way].start(slot, far.at[pre(way, way)])

    def _join(self, links, far):
        pre = self._pre
        links[2].arrived(far.at[pre(0, 1)])
        links[3].arrived(far.at[pre(1, 0)])
        links[4].arrived(far.at[pre(0, 0)])
        links[5].arrived(far.at[pre(1, 1)])

    def stage(self, number):
        place, pre = self.place, self._pre
        here = dict(place.at)
        for (first, second, cols), (ends, (near1, far1, near2, far2)) in zip(self.paths, self.work):

            def at1(y, step):
                index = here[first] if step == 0 else place.plus(first, step)
                return self._given(cols, **{"y": y, first: index, second: ALL})

            def at2(y, step):
                index = here[second] if step == 0 else place.plus(second, step)
                return far1.at[pre(0, y, index)]

            if number == 0:
                self._send(ends[0], near1, far1, at1)
            elif number == 1:
                self._pass(ends[0], near1, far1, at1)
            elif number == 2:
                self._join(ends[0], far1)
                for y in (0, 1):
                    slot = far1.at[pre(0, y)]
                    self._add(slot, slot, far1.at[pre(1, y)], at1(y, 0))
                self._send(ends[1], near2, far2, at2)
            elif number == 3:
                self._pass(ends[1], near2, far2, at2)
            elif number == 4:
                self._join(ends[1], far2)
                for y in (0, 1):
                    into = self.summed.at[pre(y, ALL, cols)]
                    self._add(into, at2(y, 0), far2.at[pre(0, y)], far2.at[pre(1, y)])
        if number == 4:
            self._add(self.leaving, self.summed.at[pre(1 - here["y"])])
            self.cross.start(self.leaving, self.coming)
        elif number == 5:
            self.cross.arrived(self.coming)
            self._add(self.total, self.summed.at[pre(here["y"])], self.coming)
            self.cross.sent()
            for ends, _ in self.work:
                for links in ends:
                    for link in links:
                        link.sent()


TOK = 256
CHUNKS = 4
BF = jnp.bfloat16
F32 = jnp.float32


def dot(left, right):
    return jnp.dot(left, right, preferred_element_type=F32)


def dot_cols(left, right):
    return lax.dot_general(left, right, (((1,), (1,)), ((), ())), preferred_element_type=F32)


def dot_rows(left, right):
    return lax.dot_general(left, right, (((0,), (0,)), ((), ())), preferred_element_type=F32)


def rows_of(block):
    return pl.ds(pl.multiple_of(block * TOK, TOK), TOK)


def iota(shape, dim):
    return lax.broadcasted_iota(jnp.int32, shape, dim)


def turned(z, table, rows, sign):
    ahead, behind = pltpu.roll(z, 112, 1), pltpu.roll(z, 16, 1)
    if sign > 0:
        return z * table[0, rows] + ahead * table[1, rows] + behind * table[2, rows]
    return z * table[0, rows] - ahead * table[1, rows] - behind * table[2, rows]


def gelu_and_slope(u):
    c, a = math.sqrt(2.0 / math.pi), 0.044715
    square = u * u
    t = jnp.tanh(c * u * (1.0 + a * square))
    half = 0.5 * (1.0 + t)
    return u * half, half + (0.5 * c) * u * (1.0 - t * t) * (1.0 + (3.0 * a) * square)


def normalize(x):
    center = x - jnp.mean(x, axis=-1, keepdims=True)
    inverse = lax.rsqrt(jnp.mean(center * center, axis=-1, keepdims=True) + epsilon)
    return center * inverse, inverse


class Loads:
    def __init__(self, sems):
        self.sems, self.used = sems, 0

    def start(self, src, dst):
        copy = pltpu.make_async_copy(src, dst, self.sems.at[self.used])
        self.used += 1
        copy.start()
        return copy


class QuickGather:
    links = 7

    def __init__(self, place, sems, full):
        self.place, self.full = place, full
        self.ends = {"y": [Link(sems, place.peer("y", 1))]}
        for axis in ("x", "z"):
            self.ends[axis] = [Link(sems, place.peer(axis, step)) for step in (1, 2, 3)]

    def _at(self, axis, step):
        here = self.place.at
        if axis == "y":
            return self.full.at[here["y"] if step == 0 else 1 - here["y"], here["x"], here["z"]]
        if axis == "x":
            return self.full.at[:, self.place.plus("x", step), here["z"]]
        return self.full.at[:, :, self.place.plus("z", step)]

    def begin(self, axis):
        for link in self.ends[axis]:
            link.start(self._at(axis, 0), self._at(axis, 0))

    def end(self, axis):
        for number, link in enumerate(self.ends[axis]):
            link.arrived(self._at(axis, -1 - number))

    def sent(self):
        for links in self.ends.values():
            for link in links:
                link.sent()


class QuickReduce:
    links = 7

    def __init__(self, place, sems, given, first, second, third, total):
        self.place, self.given, self.total = place, given, total
        self.first, self.second, self.third = first, second, third
        self.ends = {"y": [Link(sems, place.peer("y", 1))]}
        for axis in ("x", "z"):
            self.ends[axis] = [Link(sems, place.peer(axis, step)) for step in (1, 2, 3)]

    def begin(self, axis):
        place = self.place
        if axis == "y":
            self.ends["y"][0].start(self.second.at[3, 1 - place.at["y"]], self.third)
            return
        for number, link in enumerate(self.ends[axis]):
            if axis == "z":
                link.start(self.given.at[:, :, place.plus("z", number + 1)], self.first.at[number])
            else:
                link.start(self.first.at[3, :, place.plus("x", number + 1)], self.second.at[number])

    def end(self, axis):
        place = self.place
        if axis == "y":
            self.ends["y"][0].arrived(self.third)
            self.total[...] = self.second[3, place.at["y"]] + self.third[...]
            return
        into = self.first if axis == "z" else self.second
        total = self.given[:, :, place.at["z"]] if axis == "z" else self.first[3, :, place.at["x"]]
        for number, link in enumerate(self.ends[axis]):
            link.arrived(into.at[number])
            total = total + into[number]
        into[3] = total

    def sent(self):
        for links in self.ends.values():
            for link in links:
                link.sent()


class Spread:
    links = 2 * CHUNKS + 1

    def __init__(self, place, sems, own, whole):
        self.t, self.own, self.whole = place.t, own, whole
        core, far = place.peer("core", 0), place.peer("far", 0)
        self.across = [Link(sems, far) for _ in range(CHUNKS)]
        self.onward = [Link(sems, core) for _ in range(CHUNKS)]
        self.near = Link(sems, core)
        n = TOK // CHUNKS
        self.part = [pl.ds(k * n, n) for k in range(CHUNKS)]

    def start(self):
        for k, part in enumerate(self.part):
            self.across[k].start(self.own.at[part], self.whole.at[self.t, part])
        self.near.start(self.own, self.whole.at[self.t])

    def near_here(self):
        self.near.arrived(self.whole.at[self.t ^ 1])

    def far_here(self):
        for k, part in enumerate(self.part):
            got = self.whole.at[self.t ^ 2, part]
            self.across[k].arrived(got)
            self.onward[k].start(got, got)

    def both_here(self):
        for k, part in enumerate(self.part):
            self.onward[k].arrived(self.whole.at[self.t ^ 3, part])

    def sent(self):
        for link in self.across + self.onward + [self.near]:
            link.sent()


class Collect:
    links = 3

    def __init__(self, place, sems, partial, pair, across):
        self.t, self.partial, self.pair, self.across = place.t, partial, pair, across
        self.to_core, self.back = Link(sems, place.peer("core", 0)), Link(sems, place.peer("core", 0))
        self.to_far = Link(sems, place.peer("far", 0))

    def first(self):
        self.to_core.start(self.partial.at[self.t ^ 3], self.pair.at[0])

    def second(self):
        self.to_core.arrived(self.pair.at[0])
        self.pair[0] = self.pair[0] + self.partial[self.t ^ 2]
        self.to_far.start(self.pair.at[0], self.across)

    def third(self):
        self.back.start(self.partial.at[self.t ^ 1], self.pair.at[1])

    def chip_sum(self):
        self.back.arrived(self.pair.at[1])
        return self.partial[self.t].astype(F32) + self.pair[1].astype(F32)

    def far_sum(self):
        self.to_far.arrived(self.across)
        return self.across[...].astype(F32)

    def sent(self):
        for link in (self.to_core, self.to_far, self.back):
            link.sent()


def feature_owner(shape):
    row, column = iota(shape, 0), iota(shape, 1)
    return ((column >> 3) == (row >> 3) * 4 + (row & 7)) & ((row & 7) < 4)


def hidden_owner(shape, t):
    row, column = iota(shape, 0), iota(shape, 1)
    return ((column >> 5) == (row >> 3)) & ((row & 7) == t)


def lane_of(layer, member, column):
    if member < 3:
        return member * 16 + layer * 8 + (column & 7)
    return 48 + layer * 32 + (column & 31)


def unpack_small(small_table, norms, layer, t, members=range(4)):
    packed = small_table[...].reshape(256, 128).astype(BF)
    lane, column = iota((128, 1024), 0), iota((128, 1024), 1)
    shape = (256, 1024)
    for member in members:
        mine = feature_owner(shape) if member < 3 else hidden_owner(shape, t)
        pick = jnp.where(lane == lane_of(layer, member, column), 1.0, 0.0).astype(BF)
        row = jnp.sum(jnp.where(mine, dot(packed, pick), 0.0), axis=0, keepdims=True)
        norms[layer, member : member + 1] = row


def pack_small(sums, small_table, rows, t, fresh):
    lane, column = iota((1024, 128), 1), iota((1024, 128), 0)
    shape = (256, 1024)
    total = jnp.zeros((256, 128), F32)
    for layer, member in rows:
        mine = feature_owner(shape) if member < 3 else hidden_owner(shape, t)
        pick = jnp.where(lane == lane_of(layer, member, column), 1.0, 0.0).astype(BF)
        rest = jnp.where(mine, sums[layer, member : member + 1], 0.0)
        for _ in range(3):
            part = rest.astype(BF)
            total = total + dot(part, pick)
            rest = rest - part.astype(F32)
    total = total.reshape(2, 4, 4, 8, 128)
    small_table[...] = total if fresh else small_table[...] + total


def places(segments, beginning, begin_row, frequency, table):
    ids = segments[...].astype(F32)
    down = jnp.broadcast_to(ids, (128, 1024)).T
    row_total = jnp.zeros((1, 1024), F32)
    lane = iota((TOK, 128), 1) & 63
    for block in range(4):
        rows = pl.ds(block * TOK, TOK)
        column = down[block * TOK : (block + 1) * TOK, :1]
        row_total = row_total + jnp.sum(jnp.where(column < ids, 1.0, 0.0), axis=0, keepdims=True)
        first = jnp.sum(jnp.where(ids < column, 1.0, 0.0), axis=1, keepdims=True)
        beginning[rows] = first.astype(jnp.int32)
        index = (iota((TOK, 128), 0) + block * TOK).astype(F32)
        angle = (index - first) * frequency[...]
        cosine, sine = jnp.cos(angle), jnp.sin(angle)
        table[0, rows] = jnp.where(lane < 32, cosine, 1.0)
        table[1, rows] = jnp.where(lane < 16, -sine, 0.0)
        table[2, rows] = jnp.where((lane >= 16) & (lane < 32), sine, 0.0)
    begin_row[...] = row_total.astype(jnp.int32)


def attend(r, query, keys, values, begin, attended, marks, lse):
    width = (r + 1) * TOK
    rows = pl.ds(r * TOK, TOK)
    row = iota((TOK, width), 0) + r * TOK
    column = iota((TOK, width), 1)
    allowed = (column >= begin[rows]) & (column <= row)
    lane = iota((TOK, 128), 1)

    def pair(g, _):
        lanes = pl.ds(pl.multiple_of(g * 128, 128), 128)
        q, k, v = query[rows, lanes], keys[:width, lanes], values[:width, lanes]
        outs = []
        for half in range(2):
            mine = jnp.where((lane // 64) == half, q, jnp.zeros_like(q))
            scores = jnp.where(allowed, dot_cols(mine, k), -1e30)
            peak = jnp.max(scores, axis=-1, keepdims=True)
            weights = jnp.exp(scores - peak)
            total = jnp.sum(weights, axis=-1, keepdims=True)
            outs.append(dot(weights.astype(BF), v) * (1.0 / total))
            marks[...] = jnp.where(lane == 2 * g + half, peak + jnp.log(total), marks[...])
        attended[rows, lanes] = jnp.where(lane < 64, outs[0], outs[1]).astype(BF)
        return 0

    lax.fori_loop(0, 2, pair, 0)
    lse[:, rows] = marks[...].T[:8]


def forward_kernel(
    tokens, gain_own, shift_own, final_own, hidden_own, segments, frequency, proj_own,
    cotangent, qkv_own, up_own, down_own,
    mixed, norms, lse, begin_row, middle_h, table_h, cot_h, normed_h, joined_h, attended_h, active_h, slope_h, wq_h, wu_h, wd_h, wp_h,
    four, small_table, folded, wq, wu, wd, wf, wp,
    normed, joined, attended, active, slope, partial, pair, across, marks, last, begin, middle, table, spare,
    loads, sends, recvs,
):
    place = Place()
    sems = Sems(sends, recvs)
    t = place.t
    yh = t // 2
    copies = Loads(loads)
    line = jnp.zeros((8, 128), F32)
    for member, part in enumerate((gain_own, shift_own, final_own, hidden_own)):
        width = part.shape[1]
        for layer in range(2):
            spare[...] = jnp.zeros((8, 128), F32)
            spare[0:1, 0:width] = part[...].astype(F32)[layer : layer + 1]
            start = member * 16 + layer * width
            line = line + pltpu.roll(jnp.broadcast_to(spare[0:1], (8, 128)), start, 1)
    four[t] = line
    both = proj_own[...].astype(F32)
    folded[...] = jnp.concatenate([both[..., :512], both[..., 512:]], axis=1).astype(BF)
    meet(ring_peers(place) + second_peers(place) + tensor_peers(place))

    links = [Link(sems, peer) for peer in tensor_peers(place)]
    small = four.at[t]
    for link in links:
        link.start(small, small)
    jobs = {}
    for layer in range(2):
        for name, own, full, lead in (
            ("qkv", qkv_own, wq, 1), ("up", up_own, wu, 0), ("down", down_own, wd, 0), ("proj", folded, wf, 0)
        ):
            number = 4 * layer + len(jobs) % 4
            jobs[name, layer] = Gather(place, sems, own.at[layer], full.at[layer], lead, loads.at[number])
    copies.used = 9
    early = [jobs[name, 0] for name in ("qkv", "up", "down", "proj")]
    late = [jobs[name, 1] for name in ("qkv", "up", "down", "proj")]

    def go(layer, *stages):
        for stage in stages:
            job = jobs[{"q": "qkv", "u": "up", "d": "down", "p": "proj"}[stage[0]], layer]
            job.stage(int(stage[1]))

    go(0, "q0", "u0", "d0", "p0")
    for link, flip in zip(links, (1, 2, 3)):
        link.arrived(four.at[t ^ flip])
    row = iota((8, 128), 0)
    packed = jnp.zeros((8, 128), F32)
    for other in range(4):
        packed = jnp.where(row == other, four[other], packed)
    small_table[place.at["y"], place.at["x"], place.at["z"]] = packed
    shared = QuickGather(place, sems, small_table)
    shared.begin("y")
    go(0, "q1")
    shared.end("y")
    shared.begin("x")
    go(0, "u1")
    shared.end("x")
    shared.begin("z")
    go(0, "q2", "d1", "p1")
    shared.end("z")
    unpack_small(small_table, norms, 0, t, (0, 1))
    turn_cot = Spread(place, sems, cotangent, cot_h)
    open_copies = []
    spreads, collects = [], []

    for layer in range(2):
        state = tokens[...].astype(F32) if layer == 0 else middle[...]
        result = middle if layer == 0 else last
        norm = norms.at[layer]
        here, act, slp = normed.at[layer], active.at[layer], slope.at[layer]
        query, keys, values = [joined.at[layer, c] for c in range(3)]
        att = attended.at[layer]
        unit, _ = normalize(state)
        here[t] = (unit * norm[0:1] + norm[1:2]).astype(BF)
        spread = Spread(place, sems, here.at[t], here)
        spread.start()
        spreads.append(spread)
        if layer == 0:
            go(0, "u2", "q3", "u3")
            go(1, "p0", "u0")
            unpack_small(small_table, norms, 0, t, (2, 3))
            places(segments, begin, begin_row, frequency, table)
            open_copies.append(copies.start(table, table_h))
            go(0, "d2", "q4")
            unpack_small(small_table, norms, 1, t)
            go(1, "q0")
            go(0, "d3", "q5")
        else:
            go(1, "u4", "q5", "d3", "u5")

        def project(i, _, layer=layer, here=here):
            j = t ^ i
            x, rows = here[j], rows_of(j)
            for c in range(3):
                y = dot(x, wq[layer, c].reshape(1024, 256))
                for h in range(2):
                    z = y[:, h * 128 : (h + 1) * 128]
                    if c < 2:
                        z = turned(z, table, rows, 1)
                    if c == 0:
                        z = z * (HEAD_DIM ** -0.5)
                    joined[layer, c, rows, pl.ds(h * 128, 128)] = z.astype(BF)
            return 0

        def expand(i, _, layer=layer, here=here, act=act, slp=slp, norm=norm):
            j = t ^ i
            x, rows = here[j], rows_of(j)
            for m in range(4):
                cols = pl.ds(m * 256, 256)
                u = dot(x, wu[layer, :, :, :, :, cols].reshape(1024, 256)) + norm[3:4, cols]
                a, s = gelu_and_slope(u)
                act[rows, cols] = a.astype(BF)
                slp[rows, cols] = s.astype(BF)
            return 0

        def attention(far, layer=layer, att=att, query=query, keys=keys, values=values):
            for r in range(4):
                wanted = (yh != r // 2) if far else (yh == r // 2)
                pl.when(wanted)(
                    functools.partial(attend, r, query, keys, values, begin, att, marks, lse.at[layer])
                )

        def keep(*pairs, layer=layer):
            for a, b in pairs:
                open_copies.append(copies.start(a, b.at[layer]))

        marks[...] = jnp.zeros_like(marks)
        lax.fori_loop(0, 1, project, 0)
        if layer == 0:
            go(0, "p2")
        spread.near_here()
        lax.fori_loop(1, 2, project, 0)
        if layer == 1:
            lax.fori_loop(0, 2, expand, 0)
            go(1, "p3", "d4")
        spread.far_here()
        if layer == 0:
            go(0, "u4")
            go(1, "q1")
            turn_cot.start()
        lax.fori_loop(2, 3, project, 0)
        if layer == 1:
            lax.fori_loop(2, 3, expand, 0)
        spread.both_here()
        lax.fori_loop(3, 4, project, 0)
        if layer == 1:
            lax.fori_loop(3, 4, expand, 0)
        keep((here, normed_h), (joined.at[layer], joined_h), (wq.at[layer], wq_h))
        if layer == 0:
            attention(True)
            go(0, "p3", "d4")
            go(1, "p1", "u1")
            attention(False)
            go(0, "u5")
            lax.fori_loop(0, 2, expand, 0)
            go(0, "p4")
            lax.fori_loop(2, 4, expand, 0)
            go(0, "d5")
            go(1, "q2")
            go(0, "p5")
            go(1, "u2", "d0")
            turn_cot.near_here()
        else:
            go(1, "d5", "p4")
            attention(True)
            go(1, "p5")
        keep((act, active_h), (slp, slope_h), (wu.at[layer], wu_h))
        full = wf[layer].reshape(32, 16, 512).astype(F32)
        wp[layer] = jnp.concatenate([full[:, :8], full[:, 8:]], axis=2).reshape(256, 1024).astype(BF)
        collect = Collect(place, sems, partial.at[layer], pair.at[layer], across.at[layer])
        collects.append(collect)

        def output(j, layer=layer, att=att, act=act):
            x, y = att[rows_of(j)], act[rows_of(j)]
            for m in range(2):
                cols = pl.ds(m * 512, 512)
                out = dot(x, wp[layer, :, cols]) + dot(y, wd[layer, :, :, :, :, cols].reshape(1024, 512))
                partial[layer, j, :, cols] = out.astype(BF)

        output(t ^ 3)
        collect.first()
        output(t ^ 2)
        collect.second()
        if layer == 0:
            go(1, "d1", "q3")
        if layer == 1:
            attention(False)
        keep((att, attended_h), (wd.at[layer], wd_h), (wp.at[layer], wp_h))
        output(t ^ 1)
        collect.third()
        output(t)
        if layer == 0:
            go(1, "p2", "u3")
        result[...] = state + norm[2:3] + collect.chip_sum()
        if layer == 0:
            turn_cot.far_here()
        result[...] += collect.far_sum()
        if layer == 0:
            open_copies.append(copies.start(middle, middle_h))
            go(1, "d2", "q4")
    mixed[...] = last[...].astype(BF)
    turn_cot.both_here()
    shared.sent()
    for link in links:
        link.sent()
    for part in spreads + collects + [turn_cot]:
        part.sent()
    for copy in open_copies:
        copy.wait()


def forward(tokens, gain, shift, final, hidden, segments, frequency, proj, cotangent, qkv, up, down):
    vm, anywhere = pl.BlockSpec(memory_space=pltpu.VMEM), pl.BlockSpec(memory_space=pl.ANY)
    number = 3 + QuickGather.links + 8 * Gather.links + 3 * Spread.links + 2 * Collect.links
    S, V = jax.ShapeDtypeStruct, pltpu.VMEM
    ring = (2, 4, 4)
    q, w, p = (2, 3) + ring + (32, 256), (2,) + ring + (32, 1024), (2,) + ring + (16, 512)
    group, square, slim = (2, 4, TOK, 1024), (2, 1024, 1024), (2, 1024, 256)
    joined = (2, 3, 1024, 256)
    return pl.pallas_call(
        forward_kernel,
        out_shape=[
            S((TOK, 1024), BF), S((2, 8, 1024), F32), S((2, 8, 1024), F32), S((1, 1024), jnp.int32),
            S((TOK, 1024), F32), S((3, 1024, 128), F32),
            S((4, TOK, 1024), BF), S(group, BF), S(joined, BF), S(slim, BF), S(square, BF), S(square, BF),
            S(q, BF), S(w, BF), S(w, BF), S((2, 256, 1024), BF),
        ],
        in_specs=[vm] * 8 + [anywhere] * 4,
        out_specs=[vm] * 4 + [anywhere] * 12,
        scratch_shapes=[
            V((4, 8, 128), F32), V(ring + (8, 128), F32), V((2, 16, 512), BF),
            V(q, BF), V(w, BF), V(w, BF), V(p, BF), V((2, 256, 1024), BF),
            V(group, BF), V(joined, BF), V(slim, BF), V(square, BF), V(square, BF),
            V(group, BF), V((2, 2, TOK, 1024), BF), V((2, TOK, 1024), BF), V((TOK, 128), F32), V((TOK, 1024), F32), V((1024, 1), jnp.int32), V((TOK, 1024), F32), V((3, 1024, 128), F32),
            V((8, 128), F32),
            pltpu.SemaphoreType.DMA((30,)),
            pltpu.SemaphoreType.DMA((number,)), pltpu.SemaphoreType.DMA((number,)),
        ],
        compiler_params=pltpu.CompilerParams(
            collective_id=0, has_side_effects=True, vmem_limit_bytes=62 * 2**20
        ),
        name="forward_layers",
    )(tokens, gain, shift, final, hidden, segments, frequency, proj, cotangent, qkv, up, down)


def attend_back(g, query, keys, values, grad_out, begin, lse, delta, grad_query, grad_joined, table):
    lanes = pl.ds(g * 128, 128)
    for block in range(4):
        start, size = block * TOK, 1024 - block * TOK
        here, on = pl.ds(start, TOK), pl.ds(start, size)
        k, v = keys[here, lanes], values[here, lanes]
        q, d = query[on, lanes], grad_out[on, lanes]
        row = iota((TOK, size), 0) + start
        column = iota((TOK, size), 1) + start
        allowed = (row >= begin[:, on]) & (row <= column)
        lane = iota((TOK, 128), 1)
        by_value, by_key, by_query = [], [], None
        for half in range(2):
            head = pl.ds(2 * g + half, 1)
            mine = (lane // 64) == half
            kh, vh = [jnp.where(mine, part, jnp.zeros_like(part)) for part in (k, v)]
            scores = jnp.where(allowed, dot_cols(kh, q), -1e30)
            probs = jnp.exp(scores - lse[head, on])
            grad_scores = (probs * (dot_cols(vh, d) - delta[head, on])).astype(BF)
            by_value.append(dot(probs.astype(BF), d))
            by_key.append(dot(grad_scores, q))
            back = dot_rows(grad_scores, kh)
            by_query = back if by_query is None else by_query + back
        if block == 0:
            grad_query[on, lanes] = by_query
        else:
            grad_query[on, lanes] += by_query
        both = jnp.where(lane < 64, by_key[0], by_key[1])
        grad_joined[1, here, lanes] = turned(both, table, here, -1).astype(BF)
        grad_joined[2, here, lanes] = jnp.where(lane < 64, by_value[0], by_value[1]).astype(BF)


def grouped(b, *rest):
    return (b // 2, pl.ds(2 * (b % 2), 2)) + rest


def backward_kernel(
    cotangent, norms, begin, lse, tokens_h, middle_h, table_h,
    cot_h, normed_h, joined_h, attended_h, active_h, slope_h, wq_h, wu_h, wd_h, wp_h,
    token_grad, own_sums, total_q, total_p, total_u, total_d,
    tokens, middle, table, wq, wu, wd, wp, normed, joined, attended, active, slope,
    whole, grad_up, grad_att, delta, grad_query, grad_joined, dqkv, dup, ddown, dproj,
    partial, pair, across, sums, small_table, tile, four, first, second, third,
    loads, clear, sends, recvs, *scratch,
):
    place = Place()
    sems = Sems(sends, recvs)
    t = place.t
    copies = Loads(loads)
    sources = {
        "whole": (cot_h, whole.at[1]), "wd": (wd_h, wd), "slope": (slope_h, slope), "wp": (wp_h, wp),
        "attended": (attended_h, attended), "active": (active_h, active), "normed": (normed_h, normed),
        "joined": (joined_h, joined), "wu": (wu_h, wu), "wq": (wq_h, wq),
    }
    fetched = {}

    def fetch(layer, *names):
        for name in names:
            src, dst = sources[name]
            if name == "whole":
                fetched[layer, name] = [copies.start(src.at[t ^ flip], dst.at[t ^ flip]) for flip in (1, 2, 3)]
            else:
                fetched[layer, name] = [copies.start(src.at[layer], dst)]

    def need(layer, *names):
        for name in names:
            for copy in fetched[layer, name]:
                copy.wait()

    fetch(1, *sources)
    for name, src, dst in (("table", table_h, table), ("middle", middle_h, middle), ("tokens", tokens_h, tokens)):
        fetched[1, name] = [copies.start(src, dst)]
    meet(ring_peers(place) + second_peers(place) + tensor_peers(place))
    head = iota((8, 256), 0)
    member = jnp.where(iota((8, 256), 1) // 64 == head, 1.0, 0.0).astype(BF)
    closing = []
    holders = [scratch[11 * number : 11 * number + 11] for number in range(4)]

    def reduce_job(number, given, total, lead):
        return Reduce(place, sems, given, total, lead, holders[number])

    reducing = {}

    def wide_jobs(layer):
        reducing[layer, "d"] = reduce_job(0, ddown, total_d.at[layer], 0)
        reducing[layer, "u"] = reduce_job(1, dup, total_u.at[layer], 0)

    def slim_jobs(layer):
        reducing[layer, "q"] = reduce_job(3, dqkv, total_q.at[layer], 1)
        reducing[layer, "p"] = reduce_job(2, dproj, total_p.at[layer], 0)

    def go(layer, *stages):
        for stage in stages:
            reducing[layer, stage[0]].stage(int(stage[1]))

    ring = ring_peers(place)

    def hand_over(number):
        for peer in ring:
            pl.semaphore_signal(clear.at[number], inc=1, device_id=peer, device_id_type=MESH)

    def take_over(number):
        pl.semaphore_wait(clear.at[number], len(ring))

    for layer in (1, 0):
        grad = cotangent[...].astype(F32) if layer == 1 else token_grad[...]
        rows_in = whole.at[layer]
        small = sums.at[layer]
        small[...] = jnp.zeros((8, 1024), F32)
        small[2:3] = jnp.sum(grad, axis=0, keepdims=True)
        if layer == 0:
            rows_in[t] = grad.astype(BF)
            spread = Spread(place, sems, rows_in.at[t], rows_in)
            spread.start()
            closing.append(spread)
            go(1, "p1", "q1", "p2")
        else:
            rows_in[t] = cotangent[...]
            need(1, "whole")
        need(layer, "wd", "slope", "wp", "attended")

        def enter(i, _, rows_in=rows_in, small=small):
            j = t ^ i
            g, rows = rows_in[j], rows_of(j)
            for m in range(4):
                cols = pl.ds(m * 256, 256)
                low = (dot_cols(g, wd[cols]) * slope[rows, cols].astype(F32)).astype(BF)
                grad_up[rows, cols] = low
                small[3:4, cols] += jnp.sum(low.astype(F32), axis=0, keepdims=True)
            d = dot_cols(g, wp[...]).astype(BF)
            grad_att[rows] = d
            both = d.astype(F32) * attended[rows].astype(F32)
            high = both.astype(BF)
            rest = (both - high.astype(F32)).astype(BF)
            delta[:, rows] = dot_cols(member, high) + dot_cols(member, rest)
            return 0

        if layer == 1:
            lax.fori_loop(0, 4, enter, 0)
        else:
            lax.fori_loop(0, 1, enter, 0)
            go(1, "q2")
            spread.near_here()
            lax.fori_loop(1, 2, enter, 0)
            go(1, "p3", "u5", "p4", "d4", "q3")
            spread.far_here()
            lax.fori_loop(2, 3, enter, 0)
            spread.both_here()
            lax.fori_loop(3, 4, enter, 0)
            go(1, "d5", "q4")
            hand_over(0)
            go(1, "p5")
        need(layer, "active", "normed")

        def wide_grads(b, _, rows_in=rows_in):
            cols = pl.ds(pl.multiple_of(b * 256, 256), 256)
            left = active[:, cols].T
            for m in range(2):
                right = pl.ds(m * 512, 512)
                out = dot(left[:, :TOK], rows_in[0, :, right])
                for j in range(1, 4):
                    out = out + dot(left[:, j * TOK : (j + 1) * TOK], rows_in[j, :, right])
                ddown[grouped(b, slice(None), slice(None), right)] = out.astype(BF).reshape(2, 4, 32, 512)
            left = normed[:, cols].T
            for m in range(2):
                right = pl.ds(m * 512, 512)
                out = dot(left, grad_up[:, right]).astype(BF)
                dup[grouped(b, slice(None), slice(None), right)] = out.reshape(2, 4, 32, 512)
            return 0

        lax.fori_loop(0, 4, wide_grads, 0)
        wide_jobs(layer)
        if layer == 0:
            take_over(0)
            go(0, "d0", "u0")
            go(1, "q5")
            hand_over(1)
        else:
            go(1, "u0")
        need(layer, "joined")
        if layer == 1:
            need(1, "table")
        for g in range(2):
            attend_back(
                g, joined.at[0], joined.at[1], joined.at[2], grad_att, begin, lse.at[layer], delta,
                grad_query, grad_joined, table,
            )
            if layer == 1 and g == 0:
                go(1, "d0")
        need(layer, "wu", "wq")
        if layer == 1:
            fetch(0, "wd", "slope", "wp", "active", "joined")

        def turn_back(j, _):
            rows = rows_of(j)
            for h in range(2):
                lanes = pl.ds(h * 128, 128)
                z = grad_query[rows, lanes] * (HEAD_DIM ** -0.5)
                grad_joined[0, rows, lanes] = turned(z, table, rows, -1).astype(BF)
            return 0

        lax.fori_loop(0, 4, turn_back, 0)

        def leave(j):
            rows = rows_of(j)
            for m in range(4):
                cols = pl.ds(m * 256, 256)
                out = dot_cols(grad_up[rows], wu[cols])
                for c in range(3):
                    out = out + dot_cols(grad_joined[c, rows], wq[c, cols])
                partial[j, :, cols] = out.astype(BF)

        def slim_grads(b, _):
            left = normed[:, pl.ds(pl.multiple_of(b * 256, 256), 256)].T
            for c in range(3):
                dqkv[(c,) + grouped(b)] = dot(left, grad_joined[c]).astype(BF).reshape(2, 4, 32, 256)
            return 0

        def slim_all():
            lax.fori_loop(0, 4, slim_grads, 0)
            left = attended[...].T
            halves = []
            for m in range(2):
                right = pl.ds(m * 512, 512)
                out = dot(left[:, :TOK], rows_in[0, :, right])
                for j in range(1, 4):
                    out = out + dot(left[:, j * TOK : (j + 1) * TOK], rows_in[j, :, right])
                halves.append(out.reshape(32, 8, 512))
            dproj[...] = jnp.concatenate(halves, axis=1).astype(BF).reshape(2, 4, 4, 16, 512)
        collect = Collect(place, sems, partial, pair.at[layer], across.at[layer])
        leave(t ^ 3)
        collect.first()
        leave(t ^ 2)
        collect.second()
        if layer == 1:
            go(1, "u1")
        else:
            slim_all()
            slim_jobs(layer)
            take_over(1)
            go(0, "q0")
        leave(t ^ 1)
        collect.third()
        leave(t)

        if layer == 1:
            go(1, "d1", "u2", "d2", "u3")
            slim_all()
            fetch(0, "attended", "normed", "wu", "wq")
            slim_jobs(layer)
            go(1, "p0", "q0", "d3", "u4")
        if layer == 0:
            early = [(1, 0), (1, 1), (1, 2), (1, 3), (0, 2), (0, 3)]
            go(0, "p0", "d1")
            pack_small(sums, small_table, early, t, True)
            go(0, "p1", "u1", "d2", "q1", "p2")
        own = collect.chip_sum() + collect.far_sum()
        collect.sent()
        if layer == 1:
            need(1, "middle", "tokens")
        unit, inverse = normalize(middle[...] if layer == 1 else tokens[...].astype(F32))
        small[0:1] = jnp.sum(own * unit, axis=0, keepdims=True)
        small[1:2] = jnp.sum(own, axis=0, keepdims=True)
        scaled = own * norms[layer, 0:1]
        after = grad + inverse * (
            scaled
            - jnp.mean(scaled, axis=-1, keepdims=True)
            - unit * jnp.mean(scaled * unit, axis=-1, keepdims=True)
        )
        token_grad[...] = after
        if layer == 0:
            go(0, "u2", "d3")

    pack_small(sums, small_table, [(0, 0), (0, 1)], t, False)
    quick = QuickReduce(place, sems, small_table, first, second, third, tile)
    quick.begin("z")
    go(0, "q2")
    quick.end("z")
    quick.begin("x")
    go(0, "p3", "u3", "d4")
    quick.end("x")
    quick.begin("y")
    go(0, "q3", "p4", "u4")
    quick.end("y")
    links = [Link(sems, peer) for peer in tensor_peers(place)]
    for number, link in enumerate(links):
        link.start(tile, four.at[number])
    go(0, "p5", "q4")
    whole_tile = tile[...]
    for number, link in enumerate(links):
        link.arrived(four.at[number])
        whole_tile = whole_tile + four[number]
    own_sums[...] = whole_tile
    go(0, "u5", "d5", "q5")
    quick.sent()
    for part in closing:
        part.sent()
    for link in links:
        link.sent()


def backward(tokens, middle, cotangent, norms, table, begin, lse, saved):
    vm, anywhere = pl.BlockSpec(memory_space=pltpu.VMEM), pl.BlockSpec(memory_space=pl.ANY)
    S, V = jax.ShapeDtypeStruct, pltpu.VMEM
    ring = (2, 4, 4)
    square, slim, three = (1024, 1024), (1024, 256), (3, 1024, 256)
    group = (4, TOK, 1024)
    big, q, p = ring + (32, 1024), (3,) + ring + (32, 256), ring + (16, 512)
    number = 3 + QuickReduce.links + Spread.links + 2 * Collect.links
    number += 2 * (2 * Reduce.links(1024) + Reduce.links(256) + Reduce.links(512))
    reduce_scratch = []
    for shape in (big, big, p, q):
        reduce_scratch += Reduce.scratch(shape, BF)
    return pl.pallas_call(
        backward_kernel,
        out_shape=[
            S((TOK, 1024), F32), S((8, 128), F32), S((2, 3, 32, 256), F32), S((2, 16, 512), F32),
            S((2, 32, 1024), F32), S((2, 32, 1024), F32),
        ],
        in_specs=[vm] * 4 + [anywhere] * 13,
        out_specs=[vm] * 6,
        scratch_shapes=[
            V((TOK, 1024), BF), V((TOK, 1024), F32), V((3, 1024, 128), F32),
            V(three, BF), V(square, BF), V(square, BF), V((256, 1024), BF),
            V(square, BF), V(three, BF), V(slim, BF), V(square, BF), V(square, BF),
            V((2,) + group, BF), V(square, BF), V(slim, BF), V((8, 1024), F32), V(slim, F32), V(three, BF),
            V(q, BF), V(big, BF), V(big, BF), V(p, BF),
            V(group, BF), V((2, 2, TOK, 1024), BF), V((2, TOK, 1024), BF), V((2, 8, 1024), F32),
            V(ring + (8, 128), F32), V((8, 128), F32), V((3, 8, 128), F32),
            V((4, 2, 4, 8, 128), F32), V((4, 2, 8, 128), F32), V((8, 128), F32),
            pltpu.SemaphoreType.DMA((24,)), pltpu.SemaphoreType.REGULAR((2,)),
            pltpu.SemaphoreType.DMA((number,)), pltpu.SemaphoreType.DMA((number,)),
        ]
        + reduce_scratch,
        compiler_params=pltpu.CompilerParams(
            collective_id=1, has_side_effects=True, vmem_limit_bytes=62 * 2**20
        ),
        name="backward_layers",
    )(cotangent, norms, begin, lse, tokens, middle, table, *saved)


def finish_kernel(
    sums, proj, mixed, token_grad, qkv, up, down,
    gain_o, shift_o, final_o, hidden_o, proj_o, mixed_o, token_grad_o, qkv_o, up_o, down_o, sems,
):
    pairs = ((token_grad, token_grad_o), (mixed, mixed_o), (up, up_o), (down, down_o), (qkv, qkv_o))
    copies = [pltpu.make_async_copy(a, b, sems.at[number]) for number, (a, b) in enumerate(pairs)]
    for copy in copies:
        copy.start()
    proj_o[:, :, :512] = proj[:, :8]
    proj_o[:, :, 512:] = proj[:, 8:]
    line = jnp.broadcast_to(sums[pl.ds(lax.axis_index("tensor"), 1)], (8, 128))
    for layer in range(2):
        for member, out in enumerate((gain_o, shift_o, final_o)):
            start = member * 16 + layer * 8
            out[layer : layer + 1] = pltpu.roll(line, (128 - start) % 128, 1)[:1, :8]
        hidden_o[layer : layer + 1] = pltpu.roll(line, 80 - 32 * layer, 1)[:1, :32]
    for copy in copies:
        copy.wait()


def finish(sums, proj, *big):
    vm, anywhere = pl.BlockSpec(memory_space=pltpu.VMEM), pl.BlockSpec(memory_space=pl.ANY)
    S = jax.ShapeDtypeStruct
    return pl.pallas_call(
        finish_kernel,
        out_shape=[S((2, 8), F32)] * 3 + [S((2, 32), F32), S((2, 8, 1024), F32)]
        + [S(part.shape, part.dtype) for part in big],
        in_specs=[vm] * 7,
        out_specs=[vm] * 5 + [anywhere] * 5,
        scratch_shapes=[pltpu.SemaphoreType.DMA((5,))],
        name="results",
    )(sums, proj, *big)


def local(
    tokens,
    segment_ids,
    norm_gain,
    norm_shift,
    qkv_weight,
    proj_weight,
    up_weight,
    hidden_bias,
    down_weight,
    final_bias,
    cotangent,
):
    half = ROT // 2
    angles = np.exp(np.arange(half) * (-2.0 * math.log(10000.0) / ROT)).astype(np.float32)
    frequency = np.tile(angles, 128 // half)[None]
    mixed, norms, lse, begin, middle, table, cot, *saved = forward(
        tokens, norm_gain, norm_shift, final_bias, hidden_bias, segment_ids[None], frequency, proj_weight, cotangent,
        qkv_weight, up_weight, down_weight,
    )
    saved[5] = saved[5].reshape(2, 3, 1024, 256)
    saved[6] = saved[6].reshape(2, 1024, 1024)
    saved[7] = saved[7].reshape(2, 1024, 1024)
    saved[0] = saved[0].reshape(2, 1024, 1024)
    token_grad, sums, qkv, proj, up, down = backward(
        tokens, middle, cotangent, norms, table, begin, lse, [cot] + saved
    )
    gain, shift, final, hidden, proj, mixed, token_grad, qkv, up, down = finish(
        sums, proj, mixed, token_grad, qkv, up, down
    )
    return (mixed, token_grad, gain, shift, qkv, proj, up, hidden, down, final)


def solution(mesh):
    placed = (
        P(("dp", "tensor"), None),
        P("dp"),
        P(None, ("dp", "tensor")),
        P(None, ("dp", "tensor")),
        P(None, None, "dp", "tensor"),
        P(None, ("tensor", "dp"), None),
        P(None, "dp", "tensor"),
        P(None, ("tensor", "dp")),
        P(None, ("tensor", "dp"), None),
        P(None, ("dp", "tensor")),
        P(("dp", "tensor"), None),
    )
    return jax.shard_map(
        local,
        mesh=mesh,
        in_specs=placed,
        out_specs=(
            P(("dp", "tensor"), None),
            P(("dp", "tensor"), None),
            P(None, ("dp", "tensor")),
            P(None, ("dp", "tensor")),
            P(None, None, "dp", "tensor"),
            P(None, ("tensor", "dp"), None),
            P(None, "dp", "tensor"),
            P(None, ("tensor", "dp")),
            P(None, ("tensor", "dp"), None),
            P(None, ("dp", "tensor")),
        ),
        check_vma=False,
    )
```
